32 devices in a mesh: ctx: 8 (over z, x), head: 4 (over y, core).
Axes of the slice: x: 2, y: 2, z: 4, core: 2. Of those that a mesh axis runs over, the one named last changes fastest.
Arguments:
- layer_in: bfloat16 [2048, 2048], P(('ctx', 'head')), may hold values from -6 to 6
- in_proj: bfloat16 [2048, 8, 768], P(None, 'head'), may hold values from -0.125 to 0.125
- conv_weight: float32 [4, 8, 512], P(None, 'head'), may hold values from -2 to 2
- gate_logits: float32 [2, 16, 2048], P(None, 'head', 'ctx'), may hold values from -16 to 4
- norm_gain: float32 [128], replicated, may hold values from 0.1 to 1.9
- out_proj: bfloat16 [2048, 2048], P('head'), may hold values from -0.125 to 0.125
Outputs:
- layer_out: bfloat16 [2048, 2048], P(('ctx', 'head'))
The draws below stay inside these ranges and needn't reach their ends.
All inputs are finite; a program needn't handle non-finite values.
Results may differ from the reference program's by a relative error of at most 0.0065.
Values may be sent and summed in bfloat16 or wider, within the bound.
No kernel may reach another device: no remote copies, remote signals or barrier semaphores. Data moves between devices by JAX's collectives and lax.ppermute only.
A program may use at most 128 MiB of HBM per device.

```python
import math
import jax
import jax.numpy as jnp
from jax import lax

D = 2048
HK = 8
VALUE_HEADS = 16
DK = 128
DV = 128
KERNEL = 4
SPAN = 64
TOK_DEV = 256
WINDOW_TOKENS = 2048


def draw_gate_logits(key, part):
    split_random_keys = jax.random.split(key, 8)
    blocks = WINDOW_TOKENS // TOK_DEV
    slow_share = 0.5
    slow_mask = (jax.random.uniform(split_random_keys[0], (VALUE_HEADS, 1)) < slow_share).astype(jnp.float32)
    fast_rate = jnp.exp(jax.random.uniform(split_random_keys[1], (VALUE_HEADS, 1), minval=math.log(1.0 / 60.0), maxval=math.log(1.0 / 20.0)))
    slow_rate = 0.15 / WINDOW_TOKENS
    base_rate = slow_mask * slow_rate + (1.0 - slow_mask) * fast_rate
    block_factor = jnp.exp(jax.random.uniform(split_random_keys[2], (VALUE_HEADS, blocks, 1), minval=math.log(0.5), maxval=math.log(2.0)))
    block_factor = jnp.broadcast_to(block_factor, (VALUE_HEADS, blocks, TOK_DEV)).reshape(VALUE_HEADS, WINDOW_TOKENS)
    token_factor = jnp.exp(jax.random.uniform(split_random_keys[3], (VALUE_HEADS, WINDOW_TOKENS), minval=math.log(0.5), maxval=math.log(2.0)))
    current_rate = base_rate * block_factor * token_factor
    surge_positions = jax.random.randint(split_random_keys[4], (VALUE_HEADS, 3, 1), 0, WINDOW_TOKENS)
    surge_flag = jnp.any(jnp.arange(WINDOW_TOKENS)[None, None, :] == surge_positions, axis=1).astype(jnp.float32)
    surge_penalty = jax.random.uniform(split_random_keys[5], (VALUE_HEADS, WINDOW_TOKENS), minval=0.2, maxval=0.35)
    current_rate = current_rate - surge_flag * jnp.log(1.0 - surge_penalty)
    decay_logit = jnp.log(jnp.expm1(current_rate))
    beta_fast = jnp.clip(jax.random.normal(split_random_keys[6], (VALUE_HEADS, WINDOW_TOKENS)), -4.0, 4.0)
    beta_value = 0.3 * DK / WINDOW_TOKENS * jnp.exp(jax.random.uniform(split_random_keys[7], (VALUE_HEADS, WINDOW_TOKENS), minval=math.log(0.5), maxval=math.log(2.0)))
    beta_slow = jnp.log(beta_value) - jnp.log1p(-beta_value)
    beta_logit = slow_mask * beta_slow + (1.0 - slow_mask) * beta_fast
    return jnp.stack([decay_logit, beta_logit]).astype(jnp.float32)


def block_levels(key, dims, shards, smallest, largest):
    level, own = 1.0, jax.random.fold_in(key, 6)
    for position, blocks in shards:
        heights = jnp.exp(jax.random.uniform(jax.random.fold_in(own, position), (blocks,), jnp.float32, smallest / len(shards), largest / len(shards)))
        level = level * jnp.repeat(heights, dims[position] // blocks).reshape([-1 if axis == position else 1 for axis in range(len(dims))])
    return level


def gaussian(stream_key, extent, scale, limit, cuts=(), kind=jnp.bfloat16):
    drawn = scale * jax.random.normal(stream_key, extent, jnp.float32)
    if cuts:
        drawn = drawn * block_levels(stream_key, extent, cuts, -0.22, 0.18)
    return jnp.clip(drawn, -limit, limit).astype(kind)


def setup_inputs(seed: int = 0) -> dict:
    keys = jax.random.split(jax.random.key(seed), 7)
    return {
        "layer_in": gaussian(keys[0], (WINDOW_TOKENS, D), 1.0, 6.0, ((0, 32),)),
        "in_proj": gaussian(keys[1], (D, HK, 2 * DK + 2 * (VALUE_HEADS // HK) * DV), D ** -0.5, 0.125, ((1, 4),)),
        "conv_weight": gaussian(keys[2], (KERNEL, HK, 2 * DK + (VALUE_HEADS // HK) * DV), 0.5, 2.0, ((1, 4),), jnp.float32),
        "gate_logits": draw_gate_logits(jax.random.fold_in(keys[6], 71), 0),
        "norm_gain": jnp.clip(1.0 + 0.18 * jax.random.normal(keys[4], (DV,), jnp.float32), 0.1, 1.9),
        "out_proj": gaussian(keys[5], (VALUE_HEADS * DV, D), (VALUE_HEADS * DV) ** -0.5, 0.125, ((0, 4),)),
    }


EPSILON = 1e-06
HIGHEST_PREC = lax.Precision.HIGHEST

def product(pattern, first, second):
    return jnp.einsum(pattern, first, second, precision=HIGHEST_PREC)

def causal_conv(padded, weight, length):
    taps_count = weight.shape[0]
    running = padded[0:length] * weight[0]
    for offset in range(1, taps_count):
        running = running + padded[offset:offset + length] * weight[offset]
    return running

def l2_normed(values):
    return values * lax.rsqrt(lax.optimization_barrier(jnp.sum(values * values, axis=-1, keepdims=True)) + EPSILON)

def unit_inverse(lower_mat):
    size_now = lower_mat.shape[-1]
    levels = max((size_now - 1).bit_length(), 1)
    identity = jnp.eye(size_now, dtype=lower_mat.dtype)
    power = -lower_mat
    result = identity + power
    for level_index in range(1, levels):
        power = product('...ij,...jk->...ik', power, power)
        result = product('...ij,...jk->...ik', result, identity + power)
    return result

def span_terms(queries, key_rows, values, log_decay, beta_gate):
    cum_decay = jnp.cumsum(log_decay, axis=-1)
    row_ids = jnp.arange(log_decay.shape[-1])
    strict_below = row_ids[:, None] > row_ids[None, :]
    on_or_below = row_ids[:, None] >= row_ids[None, :]
    log_gap = cum_decay[..., :, None] - cum_decay[..., None, :]
    decay_mat = jnp.where(on_or_below, jnp.exp(jnp.where(on_or_below, log_gap, 0.0)), 0.0)
    key_gram = product('...id,...jd->...ij', key_rows, key_rows)
    lower_mat = jnp.where(strict_below, beta_gate[..., :, None] * key_gram * decay_mat, 0.0)
    solver = unit_inverse(lower_mat)
    scaled_k = key_rows * (beta_gate * jnp.exp(cum_decay))[..., None]
    scaled_v = values * beta_gate[..., None]
    w_rows = product('...ij,...jd->...id', solver, scaled_k)
    u_rows = product('...ij,...jd->...id', solver, scaled_v)
    qk_mat = product('...id,...jd->...ij', queries, key_rows) * decay_mat
    q_dec = queries * jnp.exp(cum_decay)[..., None]
    k_dec = key_rows * jnp.exp(cum_decay[..., -1:] - cum_decay)[..., None]
    span_decay = jnp.exp(cum_decay[..., -1])
    return (w_rows, u_rows, qk_mat, q_dec, k_dec, span_decay)

def reference(layer_in, in_proj, conv_weight, gate_logits, norm_gain, out_proj):
    group_ratio = VALUE_HEADS // HK
    conv_width = 2 * DK + group_ratio * DV
    group_width = conv_width + group_ratio * DV
    projected = jnp.dot(layer_in, in_proj.reshape(D, HK * group_width), preferred_element_type=jnp.float32).astype(jnp.bfloat16)
    projected = projected.reshape(WINDOW_TOKENS, HK, group_width)
    conv_in = projected[:, :, :conv_width].astype(jnp.float32)
    padded = jnp.concatenate([jnp.zeros((KERNEL - 1, HK, conv_width), jnp.float32), conv_in], axis=0)
    conv_out = jax.nn.silu(causal_conv(padded, conv_weight, WINDOW_TOKENS))
    queries = l2_normed(conv_out[:, :, :DK]) * DK ** (-0.5)
    key_rows = l2_normed(conv_out[:, :, DK:2 * DK])
    values = conv_out[:, :, 2 * DK:].reshape(WINDOW_TOKENS, VALUE_HEADS, DV)
    gate_z = projected[:, :, conv_width:].reshape(WINDOW_TOKENS, VALUE_HEADS, DV).astype(jnp.float32)
    queries = jnp.repeat(queries, group_ratio, axis=1)
    key_rows = jnp.repeat(key_rows, group_ratio, axis=1)
    spans = WINDOW_TOKENS // SPAN

    def by_span(array_in):
        return array_in.reshape(spans, SPAN, VALUE_HEADS, -1).transpose(0, 2, 1, 3)
    log_decay = (-jax.nn.softplus(gate_logits[0])).reshape(VALUE_HEADS, spans, SPAN).transpose(1, 0, 2)
    beta_gate = jax.nn.sigmoid(gate_logits[1]).reshape(VALUE_HEADS, spans, SPAN).transpose(1, 0, 2)

    def advance(carried, pieces):
        w_rows, u_rows, qk_mat, q_dec, k_dec, span_decay = span_terms(*pieces)
        fresh_values = u_rows - product('hcd,hde->hce', w_rows, carried)
        result = product('hcd,hde->hce', q_dec, carried) + product('hij,hje->hie', qk_mat, fresh_values)
        carried = span_decay[:, None, None] * carried + product('hcd,hce->hde', k_dec, fresh_values)
        return (carried, result)
    start_state = jnp.zeros((VALUE_HEADS, DK, DV), jnp.float32)
    final_state, outputs = lax.scan(advance, start_state, (by_span(queries), by_span(key_rows), by_span(values), log_decay, beta_gate))
    attended = outputs.transpose(0, 2, 1, 3).reshape(WINDOW_TOKENS, VALUE_HEADS, DV)
    mean_square = lax.optimization_barrier(jnp.mean(attended * attended, axis=-1, keepdims=True))
    normed = (attended * lax.rsqrt(mean_square + EPSILON) * norm_gain * jax.nn.silu(gate_z)).astype(jnp.bfloat16)
    normed = normed.reshape(WINDOW_TOKENS, VALUE_HEADS * DV)
    return jnp.dot(normed, out_proj, preferred_element_type=jnp.float32).astype(jnp.bfloat16)
```

```python
import functools

import jax
import jax.numpy as jnp
from jax import lax
from jax.experimental import pallas as pl
from jax.experimental.pallas import tpu as pltpu
from jax.sharding import PartitionSpec as P

DK = 128
DV = 128
KERNEL = 4
HALO = 16
HALF = 128
EPSILON = 1e-06
F32 = jnp.float32
BF16 = jnp.bfloat16
VMEM_BYTES = 40 * 1024 * 1024


def dot(a, b):
    return jnp.dot(a, b, preferred_element_type=F32)


def dot_t(a, b):
    return lax.dot_general(a, b, (((1,), (1,)), ((), ())), preferred_element_type=F32)


def silu(x):
    return x / (1.0 + jnp.exp(-x))


def l2_normed(x):
    return x * lax.rsqrt(jnp.sum(x * x, axis=-1, keepdims=True) + EPSILON)


def conv_silu(padded, slot, weight, lanes, rows):
    acc = padded[slot, HALO - KERNEL + 1 : HALO - KERNEL + 1 + rows, :] * weight[0:1, lanes]
    for i in range(1, KERNEL):
        lo = HALO - KERNEL + 1 + i
        acc = acc + padded[slot, lo : lo + rows, :] * weight[i : i + 1, lanes]
    return silu(acc)


def block_decay(ccol, crow, a, b):
    gap = ccol[a * HALF : (a + 1) * HALF] - crow[:, b * HALF : (b + 1) * HALF]
    return jnp.exp(jnp.minimum(gap, 0.0))


def keys_kernel(*refs, n_head, key_heads, ratio):
    pieces = refs[:n_head]
    halo, w, cw, cols, rows, s_out, y_out, k_out, x_out, padded = refs[n_head:]
    me = lax.axis_index("head")
    part = pieces[0].shape[0]
    toks = part * n_head
    blocks = toks // HALF
    heads = key_heads * ratio
    x_out[0:HALO, :] = halo[...]
    for s in range(n_head):
        at = pl.multiple_of(HALO + (me ^ s) * part, 16)
        x_out[pl.ds(at, part), :] = pieces[s][...]
    width = DK + ratio * DV
    for g in range(key_heads):
        proj = dot(x_out[...], w[:, g * width : (g + 1) * width])
        proj = proj.astype(BF16).astype(F32)
        for t in range(1 + ratio):
            padded[g * (1 + ratio) + t] = proj[:, t * 128 : (t + 1) * 128]
    ri = lax.broadcasted_iota(jnp.int32, (HALF, HALF), 0)
    ci = lax.broadcasted_iota(jnp.int32, (HALF, HALF), 1)
    below = ri > ci
    level = jnp.where(below, ri ^ ci, 0)
    eye = jnp.where(ri == ci, 1.0, 0.0).astype(F32)
    kts, rhs, lowers, offs = [], [], [], []
    for g in range(key_heads):
        base = g * (1 + ratio)
        k = l2_normed(conv_silu(padded, base, cw, slice(base * 128, base * 128 + 128), toks))
        kb = k.astype(BF16)
        k_out[g] = kb
        kf = kb.astype(F32)
        kts.append(kf.T)
        ks = [kb[b * HALF : (b + 1) * HALF] for b in range(blocks)]
        grams = {(a, b): dot_t(ks[a], ks[b]) for a in range(blocks) for b in range(a + 1)}
        for r in range(ratio):
            j = g * ratio + r
            lanes = slice((base + 1 + r) * 128, (base + 2 + r) * 128)
            v = conv_silu(padded, base + 1 + r, cw, lanes, toks)
            ccol = cols[:, j : j + 1]
            bcol = cols[:, heads + j : heads + j + 1]
            crow = rows[j : j + 1, :]
            rk = (kf * (bcol * jnp.exp(ccol))).astype(BF16)
            rv = (v * bcol).astype(BF16)
            rhs.append(jnp.concatenate([rk, rv], axis=1))
            low, off = [], {}
            for a in range(blocks):
                ba = bcol[a * HALF : (a + 1) * HALF]
                for b in range(a + 1):
                    m = ba * grams[(a, b)] * block_decay(ccol, crow, a, b)
                    if a == b:
                        low.append(jnp.where(below, m, 0.0))
                    else:
                        off[(a, b)] = m.astype(BF16)
            lowers += low
            offs.append(off)
    inv = [eye - jnp.where(level == 1, m, 0.0) for m in lowers]
    size = 2
    while size < HALF:
        here = (level >= size) & (level < 2 * size)
        inv_b = [m.astype(BF16) for m in inv]
        cx = [dot(jnp.where(here, m, 0.0).astype(BF16), x).astype(BF16) for m, x in zip(lowers, inv_b)]
        inv = [x - dot(xb, c) for x, xb, c in zip(inv, inv_b, cx)]
        size *= 2
    inv_b = [m.astype(BF16) for m in inv]
    for j in range(heads):
        ys = []
        for a in range(blocks):
            r = rhs[j][a * HALF : (a + 1) * HALF]
            if a:
                acc = r.astype(F32)
                for b in range(a):
                    acc = acc - dot(offs[j][(a, b)], ys[b])
                r = acc.astype(BF16)
            ys.append(dot(inv_b[j * blocks + a], r).astype(BF16))
        y = jnp.concatenate(ys, axis=0)
        y_out[j] = y
        crow = rows[j : j + 1, :]
        last = crow[:, toks - 1 : toks]
        kd = (kts[j // ratio] * jnp.exp(last - crow)).astype(BF16)
        s = dot(kd, y)
        s_out[j, :, 0:DK] = (eye * jnp.exp(last) - s[:, 0:DK]).astype(BF16)
        s_out[j, :, DK:] = s[:, DK:].astype(BF16)


def queries_kernel(x, w, cw, cols, rows, keys, ys, gain, q_out, o_out, g_out, padded, *, key_heads, ratio):
    toks = x.shape[0] - HALO
    blocks = toks // HALF
    width = DK + ratio * DV
    ri = lax.broadcasted_iota(jnp.int32, (HALF, HALF), 0)
    ci = lax.broadcasted_iota(jnp.int32, (HALF, HALF), 1)
    upto = ri >= ci
    for g in range(key_heads):
        proj = dot(x[...], w[:, g * width : (g + 1) * width]).astype(BF16).astype(F32)
        padded[g] = proj[:, 0:DK]
        for r in range(ratio):
            z = proj[HALO:, DK + r * DV : DK + (r + 1) * DV]
            g_out[g * ratio + r] = gain[...] * silu(z)
    for g in range(key_heads):
        q = l2_normed(conv_silu(padded, g, cw, slice(g * 128, g * 128 + 128), toks)) * DK ** (-0.5)
        qb = q.astype(BF16)
        kb = keys[g]
        grams = {
            (a, b): dot_t(qb[a * HALF : (a + 1) * HALF], kb[b * HALF : (b + 1) * HALF])
            for a in range(blocks)
            for b in range(a + 1)
        }
        for r in range(ratio):
            j = g * ratio + r
            ccol = cols[:, j : j + 1]
            crow = rows[j : j + 1, :]
            for a in range(blocks):
                at = slice(a * HALF, (a + 1) * HALF)
                acc = None
                for b in range(a + 1):
                    m = grams[(a, b)] * block_decay(ccol, crow, a, b)
                    if a == b:
                        m = jnp.where(upto, m, 0.0)
                    term = dot(m.astype(BF16), ys[j, b * HALF : (b + 1) * HALF, :])
                    acc = term if acc is None else acc + term
                q_out[j, at, :] = (q[at] * jnp.exp(ccol[at]) - acc[:, 0:DK]).astype(BF16)
                o_out[j, at, :] = acc[:, DK:]


def pair_kernel(own, got, b_out, t_out):
    odd = lax.axis_index("ctx") % 2 == 1
    for j in range(own.shape[0]):
        mine, other = own[j], got[j]
        later = jnp.where(odd, mine, other)
        earlier = jnp.where(odd, other, mine)
        prod = dot(later[:, 0:DK], earlier)
        t_out[j] = prod[:, 0:DK].astype(BF16)
        b_out[j] = (prod[:, DK:] + later[:, DK:].astype(F32)).astype(BF16)


def pair_absorb_kernel(q, o, got, q_out, o_out):
    odd = lax.axis_index("ctx") % 2 == 1
    for j in range(q.shape[0]):
        prod = dot(q[j], got[j])
        q_out[j] = jnp.where(odd, prod[:, 0:DK], q[j].astype(F32)).astype(BF16)
        o_out[j] = o[j] + jnp.where(odd, prod[:, DK:], 0.0)


def absorb_kernel(q, o, jb, jt, q_out, o_out):
    for j in range(q.shape[0]):
        o_out[j] = o[j] + dot(q[j], jb[j])
        q_out[j] = dot(q[j], jt[j]).astype(BF16)


def join_b_kernel(t, b, jb, b_out):
    for j in range(t.shape[0]):
        b_out[j] = (dot(t[j], jb[j]) + b[j].astype(F32)).astype(BF16)


def join_t_kernel(t, jt, t_out):
    for j in range(t.shape[0]):
        t_out[j] = dot(t[j], jt[j]).astype(BF16)


def normed_kernel(q, o, jb, gate, keep, send, scratch, *, n_head):
    me = lax.axis_index("head")
    for j in range(q.shape[0]):
        att = o[j] + dot(q[j], jb[j])
        scale = lax.rsqrt(jnp.mean(att * att, axis=-1, keepdims=True) + EPSILON)
        scratch[:, j * DV : (j + 1) * DV] = (att * scale * gate[j]).astype(BF16)
    part = scratch.shape[0] // n_head
    for i in range(n_head // 2):
        at = pl.multiple_of((me ^ (2 * i)) * part, 16)
        keep[i * part : (i + 1) * part, :] = scratch[pl.ds(at, part), :]
        at = pl.multiple_of((me ^ (2 * i + 1)) * part, 16)
        send[i * part : (i + 1) * part, :] = scratch[pl.ds(at, part), :]


def out_kernel(own, got, w_own, w_got, out, *, first, part):
    rows = slice(first * part, (first + 1) * part)
    a, b = own[rows, :], got[rows, :]
    out[...] = (dot(a, w_own[...]) + dot(b, w_got[...])).astype(out.dtype)


def call(body, out_shape, args, scratch=(), flops=0, **static):
    nbytes = sum(a.size * a.dtype.itemsize for a in args)
    vmem = pl.BlockSpec(memory_space=pltpu.VMEM)
    return pl.pallas_call(
        functools.partial(body, **static),
        out_shape=out_shape,
        in_specs=[vmem] * len(args),
        out_specs=jax.tree.map(lambda _: vmem, out_shape),
        scratch_shapes=list(scratch),
        compiler_params=pltpu.CompilerParams(vmem_limit_bytes=VMEM_BYTES),
        cost_estimate=pl.CostEstimate(flops=flops, bytes_accessed=nbytes, transcendentals=0),
    )(*args)


def shaped(shape, dtype):
    return jax.ShapeDtypeStruct(shape, dtype)


def xor_sent(value, axis, step):
    count = lax.axis_size(axis)
    return lax.ppermute(value, axis, [(i, i ^ step) for i in range(count)])


def passed_along(value, axis, steps):
    count = lax.axis_size(axis)
    return lax.ppermute(value, axis, [(i, i + steps) for i in range(count - steps)])


def local(layer_in, in_proj, conv_weight, gate_logits, norm_gain, out_proj):
    n_head, n_ctx = lax.axis_size("head"), lax.axis_size("ctx")
    width, key_heads, group = in_proj.shape
    heads = gate_logits.shape[1]
    ratio = heads // key_heads
    part = layer_in.shape[0]
    toks = part * n_head
    ctx_head = ("ctx", "head")

    pieces = [layer_in] + [None] * (n_head - 1)
    step = n_head // 2
    while step:
        for s in range(0, n_head, 2 * step):
            pieces[s + step] = xor_sent(pieces[s], "head", step)
        step //= 2
    tail = layer_in[part - HALO :]
    halo = None
    for h in range(n_head):
        perm = [((c - 1) * n_head + n_head - 1, c * n_head + h) for c in range(1, n_ctx)]
        got = lax.ppermute(tail, ctx_head, perm)
        halo = got if halo is None else halo + got

    def columns(w, spans):
        return jnp.concatenate([w[:, g, a:b] for g in range(key_heads) for a, b in spans], axis=1)

    kv_span = [(DK, 2 * DK + ratio * DV)]
    qz_span = [(0, DK), (2 * DK + ratio * DV, 2 * DK + 2 * ratio * DV)]
    w_kv = columns(in_proj, kv_span)
    w_qz = columns(in_proj, qz_span)
    c_kv = columns(conv_weight, kv_span)
    c_q = columns(conv_weight, [(0, DK)])
    cum = jnp.cumsum(-jax.nn.softplus(gate_logits[0]), axis=-1)
    beta = jax.nn.sigmoid(gate_logits[1])
    rows = cum
    cols = jnp.concatenate([cum, beta], axis=0).T
    w_other = xor_sent(out_proj, "head", 1)

    state = shaped((heads, DK, DV), BF16)
    s_own, ys, keys, x_full = call(
        keys_kernel,
        (
            shaped((heads, DK, DK + DV), BF16),
            shaped((heads, toks, DK + DV), BF16),
            shaped((key_heads, toks, DK), BF16),
            shaped((HALO + toks, width), BF16),
        ),
        [*pieces, halo, w_kv, c_kv, cols, rows],
        [pltpu.VMEM((key_heads * (1 + ratio), HALO + toks, 128), F32)],
        flops=2 * toks * width * group,
        n_head=n_head,
        key_heads=key_heads,
        ratio=ratio,
    )
    got = xor_sent(s_own, "ctx", 1)
    q_shape = shaped((heads, toks, DK), BF16)
    o_shape = shaped((heads, toks, DV), F32)
    q, o, gate = call(
        queries_kernel,
        (q_shape, o_shape, o_shape),
        [x_full, w_qz, c_q, cols, rows, keys, ys, norm_gain[None, :]],
        [pltpu.VMEM((key_heads, HALO + toks, 128), F32)],
        flops=2 * toks * width * group,
        key_heads=key_heads,
        ratio=ratio,
    )
    b, t = call(pair_kernel, (state, state), [s_own, got], flops=heads * 2**23)
    step = 2
    jb = passed_along(b, "ctx", step)
    jt = passed_along(t, "ctx", step)
    q, o = call(pair_absorb_kernel, (q_shape, o_shape), [q, o, got], flops=heads * 2**24)
    while 2 * step < n_ctx:
        b = call(join_b_kernel, state, [t, b, jb], flops=heads * 2**22)
        step *= 2
        more = 2 * step < n_ctx
        if more:
            t = call(join_t_kernel, state, [t, jt], flops=heads * 2**22)
        nb = passed_along(b, "ctx", step)
        nt = passed_along(t, "ctx", step) if more else None
        q, o = call(absorb_kernel, (q_shape, o_shape), [q, o, jb, jt], flops=heads * 2**24)
        jb, jt = nb, nt
    half = shaped((toks // 2, heads * DV), BF16)
    keep, send = call(
        normed_kernel,
        (half, half),
        [q, o, jb, gate],
        [pltpu.VMEM((toks, heads * DV), BF16)],
        flops=heads * 2**23,
        n_head=n_head,
    )
    other = xor_sent(send, "head", 1)
    out_args = [keep, other, out_proj, w_other]
    out = None
    partial = {}
    for i in reversed(range(n_head // 2)):
        dtype = F32 if i == 0 else BF16
        partial[i] = call(
            out_kernel, shaped((part, width), dtype), out_args, flops=part * width * 2**12, first=i, part=part
        )
        if i:
            partial[i] = xor_sent(partial[i], "head", 2 * i)
    for i in range(n_head // 2):
        out = partial[i].astype(F32) if out is None else out + partial[i].astype(F32)
    return out.astype(BF16)


def solution(mesh):
    in_specs = (
        P(("ctx", "head"), None),
        P(None, "head", None),
        P(None, "head", None),
        P(None, "head", "ctx"),
        P(),
        P("head", None),
    )
    out_specs = P(("ctx", "head"), None)
    return jax.shard_map(local, mesh=mesh, in_specs=in_specs, out_specs=out_specs, check_vma=False)
```

```python
import functools

import jax
import jax.numpy as jnp
from jax import lax
from jax.experimental import pallas as pl
from jax.experimental.pallas import tpu as pltpu
from jax.sharding import PartitionSpec as P

DK = 128
DV = 128
KERNEL = 4
HALO = 16
HALF = 128
EPSILON = 1e-06
F32 = jnp.float32
BF16 = jnp.bfloat16
VMEM_BYTES = 40 * 1024 * 1024


def dot(a, b):
    return jnp.dot(a, b, preferred_element_type=F32)


def dot_t(a, b):
    return lax.dot_general(a, b, (((1,), (1,)), ((), ())), preferred_element_type=F32)


def silu(x):
    return x / (1.0 + jnp.exp(-x))


def l2_normed(x):
    return x * lax.rsqrt(jnp.sum(x * x, axis=-1, keepdims=True) + EPSILON)


def conv_silu(padded, slot, weight, g, lanes, rows):
    acc = padded[slot, HALO - KERNEL + 1 : HALO - KERNEL + 1 + rows, :] * weight[0, g : g + 1, lanes]
    for i in range(1, KERNEL):
        lo = HALO - KERNEL + 1 + i
        acc = acc + padded[slot, lo : lo + rows, :] * weight[i, g : g + 1, lanes]
    return silu(acc)


def block_decay(ccol, crow, a, b):
    gap = ccol[a * HALF : (a + 1) * HALF] - crow[:, b * HALF : (b + 1) * HALF]
    return jnp.exp(jnp.minimum(gap, 0.0))


def gates_kernel(logits, rows, cols, decays):
    toks = logits.shape[2]
    blocks = toks // HALF
    x = logits[0]
    log_decay = -(jnp.maximum(x, 0.0) + jnp.log1p(jnp.exp(-jnp.abs(x))))
    beta = 1.0 / (1.0 + jnp.exp(-logits[1]))
    heads = x.shape[0]
    ri = lax.broadcasted_iota(jnp.int32, (toks, toks), 0)
    ci = lax.broadcasted_iota(jnp.int32, (toks, toks), 1)
    exact = lax.Precision.HIGHEST
    rows[...] = jnp.dot(log_decay, (ri <= ci).astype(F32), precision=exact, preferred_element_type=F32)
    last_dims = (((1,), (1,)), ((), ()))
    ccols = lax.dot_general((ri >= ci).astype(F32), log_decay, last_dims, precision=exact, preferred_element_type=F32)
    bcols = lax.dot_general((ri == ci).astype(F32), beta, last_dims, precision=exact, preferred_element_type=F32)
    cols[:, 0:heads] = ccols
    cols[:, heads : 2 * heads] = bcols
    below = ri[:HALF, :HALF] > ci[:HALF, :HALF]
    for j in range(heads):
        i = 0
        for a in range(blocks):
            for b in range(a + 1):
                m = block_decay(ccols[:, j : j + 1], rows[j : j + 1, :], a, b)
                m = m * bcols[a * HALF : (a + 1) * HALF, j : j + 1]
                decays[j, i] = jnp.where(below, m, 0.0) if a == b else m
                i += 1


def keys_kernel(*refs, n_head, key_heads, ratio):
    pieces = refs[:n_head]
    halo, halo_core, w, cw, cols, rows, decays, s_out, y_out, k_out, x_out, padded = refs[n_head:]
    me = lax.axis_index("head")
    part = pieces[0].shape[0]
    toks = part * n_head
    blocks = toks // HALF
    heads = key_heads * ratio
    x_out[0:HALO, :] = jnp.where(me % 2 == 1, halo[part - HALO :, :], halo_core[part - HALO :, :])
    for s in range(n_head):
        at = pl.multiple_of(HALO + (me ^ s) * part, 16)
        x_out[pl.ds(at, part), :] = pieces[s][...]
    group = 2 * DK + 2 * ratio * DV
    for g in range(key_heads):
        proj = dot(x_out[...], w[:, g * group + DK : g * group + 2 * DK + ratio * DV])
        proj = proj.astype(BF16).astype(F32)
        for t in range(1 + ratio):
            padded[g * (1 + ratio) + t] = proj[:, t * 128 : (t + 1) * 128]
    ri = lax.broadcasted_iota(jnp.int32, (HALF, HALF), 0)
    ci = lax.broadcasted_iota(jnp.int32, (HALF, HALF), 1)
    below = ri > ci
    level = jnp.where(below, ri ^ ci, 0)
    eye = jnp.where(ri == ci, 1.0, 0.0).astype(F32)
    kts, rhs, lowers, offs = [], [], [], []
    for g in range(key_heads):
        base = g * (1 + ratio)
        k = l2_normed(conv_silu(padded, base, cw, g, slice(DK, 2 * DK), toks))
        kb = k.astype(BF16)
        k_out[g] = kb
        kf = kb.astype(F32)
        kts.append(kf.T)
        ks = [kb[b * HALF : (b + 1) * HALF] for b in range(blocks)]
        grams = {(a, b): dot_t(ks[a], ks[b]) for a in range(blocks) for b in range(a + 1)}
        for r in range(ratio):
            j = g * ratio + r
            lanes = slice(2 * DK + r * DV, 2 * DK + (r + 1) * DV)
            v = conv_silu(padded, base + 1 + r, cw, g, lanes, toks)
            ccol = cols[:, j : j + 1]
            bcol = cols[:, heads + j : heads + j + 1]
            rk = (kf * (bcol * jnp.exp(ccol))).astype(BF16)
            rv = (v * bcol).astype(BF16)
            rhs.append(jnp.concatenate([rk, rv], axis=1))
            low, off, i = [], {}, 0
            for a in range(blocks):
                for b in range(a + 1):
                    m = grams[(a, b)] * decays[j, i]
                    i += 1
                    if a == b:
                        low.append(m)
                    else:
                        off[(a, b)] = m.astype(BF16)
            lowers += low
            offs.append(off)
    inv = [eye - jnp.where(level == 1, m, 0.0) for m in lowers]
    size = 2
    while size < HALF:
        here = (level >= size) & (level < 2 * size)
        inv_b = [m.astype(BF16) for m in inv]
        cx = [dot(jnp.where(here, m, 0.0).astype(BF16), x).astype(BF16) for m, x in zip(lowers, inv_b)]
        inv = [x - dot(xb, c) for x, xb, c in zip(inv, inv_b, cx)]
        size *= 2
    inv_b = [m.astype(BF16) for m in inv]
    for j in range(heads):
        ys = []
        for a in range(blocks):
            r = rhs[j][a * HALF : (a + 1) * HALF]
            if a:
                acc = r.astype(F32)
                for b in range(a):
                    acc = acc - dot(offs[j][(a, b)], ys[b])
                r = acc.astype(BF16)
            ys.append(dot(inv_b[j * blocks + a], r).astype(BF16))
        y = jnp.concatenate(ys, axis=0)
        y_out[j] = y
        crow = rows[j : j + 1, :]
        last = crow[:, toks - 1 : toks]
        kd = (kts[j // ratio] * jnp.exp(last - crow)).astype(BF16)
        s = dot(kd, y)
        s_out[j, :, 0:DK] = (eye * jnp.exp(last) - s[:, 0:DK]).astype(BF16)
        s_out[j, :, DK:] = s[:, DK:].astype(BF16)


def queries_kernel(x, w, cw, cols, rows, keys, ys, gain, q_out, o_out, g_out, padded, *, key_heads, ratio):
    toks = x.shape[0] - HALO
    blocks = toks // HALF
    group = 2 * DK + 2 * ratio * DV
    ri = lax.broadcasted_iota(jnp.int32, (HALF, HALF), 0)
    ci = lax.broadcasted_iota(jnp.int32, (HALF, HALF), 1)
    upto = ri >= ci
    for g in range(key_heads):
        padded[g] = dot(x[...], w[:, g * group : g * group + DK]).astype(BF16).astype(F32)
        proj = dot(x[HALO:, :], w[:, g * group + 2 * DK + ratio * DV : (g + 1) * group]).astype(BF16).astype(F32)
        for r in range(ratio):
            z = proj[:, r * DV : (r + 1) * DV]
            g_out[g * ratio + r] = gain[...] * silu(z)
    for g in range(key_heads):
        q = l2_normed(conv_silu(padded, g, cw, g, slice(0, DK), toks)) * DK ** (-0.5)
        qb = q.astype(BF16)
        kb = keys[g]
        grams = {
            (a, b): dot_t(qb[a * HALF : (a + 1) * HALF], kb[b * HALF : (b + 1) * HALF])
            for a in range(blocks)
            for b in range(a + 1)
        }
        for r in range(ratio):
            j = g * ratio + r
            ccol = cols[:, j : j + 1]
            crow = rows[j : j + 1, :]
            for a in range(blocks):
                at = slice(a * HALF, (a + 1) * HALF)
                acc = None
                for b in range(a + 1):
                    m = grams[(a, b)] * block_decay(ccol, crow, a, b)
                    if a == b:
                        m = jnp.where(upto, m, 0.0)
                    term = dot(m.astype(BF16), ys[j, b * HALF : (b + 1) * HALF, :])
                    acc = term if acc is None else acc + term
                q_out[j, at, :] = (q[at] * jnp.exp(ccol[at]) - acc[:, 0:DK]).astype(BF16)
                o_out[j, at, :] = acc[:, DK:]


def pair_kernel(own, got, b_out, t_out):
    odd = lax.axis_index("ctx") % 2 == 1
    for j in range(own.shape[0]):
        mine, other = own[j], got[j]
        later = jnp.where(odd, mine, other)
        earlier = jnp.where(odd, other, mine)
        prod = dot(later[:, 0:DK], earlier)
        t_out[j] = prod[:, 0:DK].astype(BF16)
        b_out[j] = (prod[:, DK:] + later[:, DK:].astype(F32)).astype(BF16)


def pair_absorb_kernel(q, o, got, q_out, o_out):
    odd = lax.axis_index("ctx") % 2 == 1
    for j in range(q.shape[0]):
        prod = dot(q[j], got[j])
        q_out[j] = jnp.where(odd, prod[:, 0:DK], q[j].astype(F32)).astype(BF16)
        o_out[j] = o[j] + jnp.where(odd, prod[:, DK:], 0.0)


def absorb_kernel(q, o, jb, jt, q_out, o_out):
    for j in range(q.shape[0]):
        o_out[j] = o[j] + dot(q[j], jb[j])
        q_out[j] = dot(q[j], jt[j]).astype(BF16)


def join_b_kernel(t, b, jb, b_out):
    for j in range(t.shape[0]):
        b_out[j] = (dot(t[j], jb[j]) + b[j].astype(F32)).astype(BF16)


def join_t_kernel(t, jt, t_out):
    for j in range(t.shape[0]):
        t_out[j] = dot(t[j], jt[j]).astype(BF16)


def normed_kernel(q, o, jb, gate, keep, send, scratch, *, n_head, last_step):
    me = lax.axis_index("head")
    upper = lax.axis_index("ctx") // last_step % 2 == 1
    for j in range(q.shape[0]):
        att = o[j] + jnp.where(upper, dot(q[j], jb[j]), 0.0)
        scale = lax.rsqrt(jnp.mean(att * att, axis=-1, keepdims=True) + EPSILON)
        scratch[:, j * DV : (j + 1) * DV] = (att * scale * gate[j]).astype(BF16)
    part = scratch.shape[0] // n_head
    for i in range(n_head // 2):
        at = pl.multiple_of((me ^ (2 * i)) * part, 16)
        keep[i * part : (i + 1) * part, :] = scratch[pl.ds(at, part), :]
        at = pl.multiple_of((me ^ (2 * i + 1)) * part, 16)
        send[i * part : (i + 1) * part, :] = scratch[pl.ds(at, part), :]


def out_kernel(own, got, w_own, w_got, out, *, first, part):
    rows = slice(first * part, (first + 1) * part)
    a, b = own[rows, :], got[rows, :]
    out[...] = (dot(a, w_own[...]) + dot(b, w_got[...])).astype(out.dtype)


def call(body, out_shape, args, scratch=(), flops=0, **static):
    nbytes = sum(a.size * a.dtype.itemsize for a in args)
    vmem = pl.BlockSpec(memory_space=pltpu.VMEM)
    return pl.pallas_call(
        functools.partial(body, **static),
        out_shape=out_shape,
        in_specs=[vmem] * len(args),
        out_specs=jax.tree.map(lambda _: vmem, out_shape),
        scratch_shapes=list(scratch),
        compiler_params=pltpu.CompilerParams(vmem_limit_bytes=VMEM_BYTES),
        cost_estimate=pl.CostEstimate(flops=flops, bytes_accessed=nbytes, transcendentals=0),
    )(*args)


def shaped(shape, dtype):
    return jax.ShapeDtypeStruct(shape, dtype)


def xor_sent(value, axis, step):
    count = lax.axis_size(axis)
    return lax.ppermute(value, axis, [(i, i ^ step) for i in range(count)])


def passed_along(value, axis, steps):
    count = lax.axis_size(axis)
    return lax.ppermute(value, axis, [(i, i + steps) for i in range(count - steps)])


def local(layer_in, in_proj, conv_weight, gate_logits, norm_gain, out_proj):
    n_head, n_ctx = lax.axis_size("head"), lax.axis_size("ctx")
    width, key_heads, group = in_proj.shape
    heads = gate_logits.shape[1]
    ratio = heads // key_heads
    part = layer_in.shape[0]
    toks = part * n_head
    ctx_head = ("ctx", "head")

    pieces = [layer_in] + [None] * (n_head - 1)
    step = n_head // 2
    while step:
        for s in range(0, n_head, 2 * step):
            pieces[s + step] = xor_sent(pieces[s], "head", step)
        step //= 2
    halo = None
    for h in range(1, n_head, 2):
        perm = [((c - 1) * n_head + n_head - 1, c * n_head + h) for c in range(1, n_ctx)]
        got = lax.ppermute(layer_in, ctx_head, perm)
        halo = got if halo is None else halo + got
    halo_core = xor_sent(halo, "head", 1)
    w_in = in_proj.reshape(width, key_heads * group)
    blocks = toks // HALF
    rows, cols, decays = call(
        gates_kernel,
        (
            shaped((heads, toks), F32),
            shaped((toks, 2 * heads), F32),
            shaped((heads, blocks * (blocks + 1) // 2, HALF, HALF), F32),
        ),
        [gate_logits],
    )
    w_other = xor_sent(out_proj, "head", 1)

    state = shaped((heads, DK, DV), BF16)
    s_own, ys, keys, x_full = call(
        keys_kernel,
        (
            shaped((heads, DK, DK + DV), BF16),
            shaped((heads, toks, DK + DV), BF16),
            shaped((key_heads, toks, DK), BF16),
            shaped((HALO + toks, width), BF16),
        ),
        [*pieces, halo, halo_core, w_in, conv_weight, cols, rows, decays],
        [pltpu.VMEM((key_heads * (1 + ratio), HALO + toks, 128), F32)],
        flops=2 * toks * width * group,
        n_head=n_head,
        key_heads=key_heads,
        ratio=ratio,
    )
    got = xor_sent(s_own, "ctx", 1)
    q_shape = shaped((heads, toks, DK), BF16)
    o_shape = shaped((heads, toks, DV), F32)
    q, o, gate = call(
        queries_kernel,
        (q_shape, o_shape, o_shape),
        [x_full, w_in, conv_weight, cols, rows, keys, ys, norm_gain[None, :]],
        [pltpu.VMEM((key_heads, HALO + toks, 128), F32)],
        flops=2 * toks * width * group,
        key_heads=key_heads,
        ratio=ratio,
    )
    b, t = call(pair_kernel, (state, state), [s_own, got], flops=heads * 2**23)
    step = 2
    jb = passed_along(b, "ctx", step)
    jt = passed_along(t, "ctx", step)
    q, o = call(pair_absorb_kernel, (q_shape, o_shape), [q, o, got], flops=heads * 2**24)
    while 2 * step < n_ctx:
        b = call(join_b_kernel, state, [t, b, jb], flops=heads * 2**22)
        step *= 2
        more = 2 * step < n_ctx
        if more:
            t = call(join_t_kernel, state, [t, jt], flops=heads * 2**22)
        nb = passed_along(b, "ctx", step) if more else xor_sent(b, "ctx", step)
        nt = passed_along(t, "ctx", step) if more else None
        q, o = call(absorb_kernel, (q_shape, o_shape), [q, o, jb, jt], flops=heads * 2**24)
        jb, jt = nb, nt
    half = shaped((toks // 2, heads * DV), BF16)
    keep, send = call(
        normed_kernel,
        (half, half),
        [q, o, jb, gate],
        [pltpu.VMEM((toks, heads * DV), BF16)],
        flops=heads * 2**23,
        n_head=n_head,
        last_step=step,
    )
    other = xor_sent(send, "head", 1)
    out_args = [keep, other, out_proj, w_other]
    out = None
    partial = {}
    for i in reversed(range(n_head // 2)):
        dtype = F32 if i == 0 else BF16
        partial[i] = call(
            out_kernel, shaped((part, width), dtype), out_args, flops=part * width * 2**12, first=i, part=part
        )
        if i:
            partial[i] = xor_sent(partial[i], "head", 2 * i)
    for i in range(n_head // 2):
        out = partial[i].astype(F32) if out is None else out + partial[i].astype(F32)
    return out.astype(BF16)


def solution(mesh):
    in_specs = (
        P(("ctx", "head"), None),
        P(None, "head", None),
        P(None, "head", None),
        P(None, "head", "ctx"),
        P(),
        P("head", None),
    )
    out_specs = P(("ctx", "head"), None)
    return jax.shard_map(local, mesh=mesh, in_specs=in_specs, out_specs=out_specs, check_vma=False)
```

```python
import functools

import jax
import jax.numpy as jnp
from jax import lax
from jax.experimental import pallas as pl
from jax.experimental.pallas import tpu as pltpu
from jax.sharding import PartitionSpec as P

DK = 128
DV = 128
KERNEL = 4
HALO = 16
HALF = 128
EPSILON = 1e-06
F32 = jnp.float32
BF16 = jnp.bfloat16
VMEM_BYTES = 40 * 1024 * 1024


def dot(a, b):
    return jnp.dot(a, b, preferred_element_type=F32)


def dot_t(a, b):
    return lax.dot_general(a, b, (((1,), (1,)), ((), ())), preferred_element_type=F32)


def silu(x):
    return x / (1.0 + jnp.exp(-x))


def l2_normed(x):
    return x * lax.rsqrt(jnp.sum(x * x, axis=-1, keepdims=True) + EPSILON)


def conv_silu(padded, slot, weight, g, lanes, rows):
    acc = padded[slot, HALO - KERNEL + 1 : HALO - KERNEL + 1 + rows, :] * weight[0, g : g + 1, lanes]
    for i in range(1, KERNEL):
        lo = HALO - KERNEL + 1 + i
        acc = acc + padded[slot, lo : lo + rows, :] * weight[i, g : g + 1, lanes]
    return silu(acc)


def block_decay(ccol, crow, a, b):
    gap = ccol[a * HALF : (a + 1) * HALF] - crow[:, b * HALF : (b + 1) * HALF]
    return jnp.exp(jnp.minimum(gap, 0.0))


def gates_kernel(logits, x_any, rows, cols, decays, tail, sem):
    copy = pltpu.make_async_copy(x_any.at[pl.ds(x_any.shape[0] - HALO, HALO), :], tail, sem)
    copy.start()
    toks = logits.shape[2]
    blocks = toks // HALF
    x = logits[0]
    log_decay = -(jnp.maximum(x, 0.0) + jnp.log1p(jnp.exp(-jnp.abs(x))))
    beta = 1.0 / (1.0 + jnp.exp(-logits[1]))
    heads = x.shape[0]
    ri = lax.broadcasted_iota(jnp.int32, (toks, toks), 0)
    ci = lax.broadcasted_iota(jnp.int32, (toks, toks), 1)
    exact = lax.Precision.HIGHEST
    rows[...] = jnp.dot(log_decay, (ri <= ci).astype(F32), precision=exact, preferred_element_type=F32)
    last_dims = (((1,), (1,)), ((), ()))
    ccols = lax.dot_general((ri >= ci).astype(F32), log_decay, last_dims, precision=exact, preferred_element_type=F32)
    bcols = lax.dot_general((ri == ci).astype(F32), beta, last_dims, precision=exact, preferred_element_type=F32)
    cols[:, 0:heads] = ccols
    cols[:, heads : 2 * heads] = bcols
    below = ri[:HALF, :HALF] > ci[:HALF, :HALF]
    for j in range(heads):
        i = 0
        for a in range(blocks):
            for b in range(a + 1):
                m = block_decay(ccols[:, j : j + 1], rows[j : j + 1, :], a, b)
                m = m * bcols[a * HALF : (a + 1) * HALF, j : j + 1]
                decays[j, i] = jnp.where(below, m, 0.0) if a == b else m
                i += 1
    copy.wait()


def keys_kernel(*refs, n_head, key_heads, ratio):
    pieces = refs[:n_head]
    halo, halo_core, w, cw, cols, rows, decays, s_out, y_out, k_out, x_out, padded = refs[n_head:]
    me = lax.axis_index("head")
    part = pieces[0].shape[0]
    toks = part * n_head
    blocks = toks // HALF
    heads = key_heads * ratio
    direct = (me % 2 == 1) != (me >= n_head - 2)
    x_out[0:HALO, :] = jnp.where(direct, halo[...], halo_core[...])
    for s in range(n_head):
        at = pl.multiple_of(HALO + (me ^ s) * part, 16)
        x_out[pl.ds(at, part), :] = pieces[s][...]
    width = DK + ratio * DV
    for g in range(key_heads):
        proj = dot(x_out[...], w[:, g * width : (g + 1) * width])
        proj = proj.astype(BF16).astype(F32)
        for t in range(1 + ratio):
            padded[g * (1 + ratio) + t] = proj[:, t * 128 : (t + 1) * 128]
    ri = lax.broadcasted_iota(jnp.int32, (HALF, HALF), 0)
    ci = lax.broadcasted_iota(jnp.int32, (HALF, HALF), 1)
    below = ri > ci
    level = jnp.where(below, ri ^ ci, 0)
    eye = jnp.where(ri == ci, 1.0, 0.0).astype(F32)
    kts, rhs, lowers, offs = [], [], [], []
    for g in range(key_heads):
        base = g * (1 + ratio)
        k = l2_normed(conv_silu(padded, base, cw, g, slice(DK, 2 * DK), toks))
        kb = k.astype(BF16)
        k_out[g] = kb
        kf = kb.astype(F32)
        kts.append(kf.T)
        ks = [kb[b * HALF : (b + 1) * HALF] for b in range(blocks)]
        grams = {(a, b): dot_t(ks[a], ks[b]) for a in range(blocks) for b in range(a + 1)}
        for r in range(ratio):
            j = g * ratio + r
            lanes = slice(2 * DK + r * DV, 2 * DK + (r + 1) * DV)
            v = conv_silu(padded, base + 1 + r, cw, g, lanes, toks)
            ccol = cols[:, j : j + 1]
            bcol = cols[:, heads + j : heads + j + 1]
            rk = (kf * (bcol * jnp.exp(ccol))).astype(BF16)
            rv = (v * bcol).astype(BF16)
            rhs.append(jnp.concatenate([rk, rv], axis=1))
            low, off, i = [], {}, 0
            for a in range(blocks):
                for b in range(a + 1):
                    m = grams[(a, b)] * decays[j, i]
                    i += 1
                    if a == b:
                        low.append(m)
                    else:
                        off[(a, b)] = m.astype(BF16)
            lowers += low
            offs.append(off)
    inv = [eye - jnp.where(level == 1, m, 0.0) for m in lowers]
    size = 2
    while size < HALF:
        here = (level >= size) & (level < 2 * size)
        inv_b = [m.astype(BF16) for m in inv]
        cx = [dot(jnp.where(here, m, 0.0).astype(BF16), x).astype(BF16) for m, x in zip(lowers, inv_b)]
        inv = [x - dot(xb, c) for x, xb, c in zip(inv, inv_b, cx)]
        size *= 2
    inv_b = [m.astype(BF16) for m in inv]
    for j in range(heads):
        ys = []
        for a in range(blocks):
            r = rhs[j][a * HALF : (a + 1) * HALF]
            if a:
                acc = r.astype(F32)
                for b in range(a):
                    acc = acc - dot(offs[j][(a, b)], ys[b])
                r = acc.astype(BF16)
            ys.append(dot(inv_b[j * blocks + a], r).astype(BF16))
        y = jnp.concatenate(ys, axis=0)
        y_out[j] = y
        crow = rows[j : j + 1, :]
        last = crow[:, toks - 1 : toks]
        kd = (kts[j // ratio] * jnp.exp(last - crow)).astype(BF16)
        s = dot(kd, y)
        s_out[j, :, 0:DK] = (eye * jnp.exp(last) - s[:, 0:DK]).astype(BF16)
        s_out[j, :, DK:] = s[:, DK:].astype(BF16)


def queries_kernel(x, wq, wz, cw, cols, rows, keys, ys, gain, q_out, o_out, g_out, padded, *, key_heads, ratio):
    toks = x.shape[0] - HALO
    blocks = toks // HALF
    ri = lax.broadcasted_iota(jnp.int32, (HALF, HALF), 0)
    ci = lax.broadcasted_iota(jnp.int32, (HALF, HALF), 1)
    upto = ri >= ci
    for g in range(key_heads):
        padded[g] = dot(x[...], wq[:, g * DK : (g + 1) * DK]).astype(BF16).astype(F32)
        proj = dot(x[HALO:, :], wz[:, g * ratio * DV : (g + 1) * ratio * DV]).astype(BF16).astype(F32)
        for r in range(ratio):
            z = proj[:, r * DV : (r + 1) * DV]
            g_out[g * ratio + r] = gain[...] * silu(z)
    for g in range(key_heads):
        q = l2_normed(conv_silu(padded, g, cw, g, slice(0, DK), toks)) * DK ** (-0.5)
        qb = q.astype(BF16)
        kb = keys[g]
        grams = {
            (a, b): dot_t(qb[a * HALF : (a + 1) * HALF], kb[b * HALF : (b + 1) * HALF])
            for a in range(blocks)
            for b in range(a + 1)
        }
        for r in range(ratio):
            j = g * ratio + r
            ccol = cols[:, j : j + 1]
            crow = rows[j : j + 1, :]
            for a in range(blocks):
                at = slice(a * HALF, (a + 1) * HALF)
                acc = None
                for b in range(a + 1):
                    m = grams[(a, b)] * block_decay(ccol, crow, a, b)
                    if a == b:
                        m = jnp.where(upto, m, 0.0)
                    term = dot(m.astype(BF16), ys[j, b * HALF : (b + 1) * HALF, :])
                    acc = term if acc is None else acc + term
                q_out[j, at, :] = (q[at] * jnp.exp(ccol[at]) - acc[:, 0:DK]).astype(BF16)
                o_out[j, at, :] = acc[:, DK:]


def pair_kernel(own, got, b_out, t_out):
    odd = lax.axis_index("ctx") % 2 == 1
    for j in range(own.shape[0]):
        mine, other = own[j], got[j]
        later = jnp.where(odd, mine, other)
        earlier = jnp.where(odd, other, mine)
        prod = dot(later[:, 0:DK], earlier)
        t_out[j] = prod[:, 0:DK].astype(BF16)
        b_out[j] = (prod[:, DK:] + later[:, DK:].astype(F32)).astype(BF16)


def pair_absorb_kernel(q, o, got, q_out, o_out):
    odd = lax.axis_index("ctx") % 2 == 1
    for j in range(q.shape[0]):
        prod = dot(q[j], got[j])
        q_out[j] = jnp.where(odd, prod[:, 0:DK], q[j].astype(F32)).astype(BF16)
        o_out[j] = o[j] + jnp.where(odd, prod[:, DK:], 0.0)


def absorb_kernel(q, o, jb, jt, q_out, o_out):
    for j in range(q.shape[0]):
        o_out[j] = o[j] + dot(q[j], jb[j])
        q_out[j] = dot(q[j], jt[j]).astype(BF16)


def join_b_kernel(t, b, jb, b_out):
    for j in range(t.shape[0]):
        b_out[j] = (dot(t[j], jb[j]) + b[j].astype(F32)).astype(BF16)


def join_t_kernel(t, jt, t_out):
    for j in range(t.shape[0]):
        t_out[j] = dot(t[j], jt[j]).astype(BF16)


def normed_kernel(q, o, jb, gate, keep, send, scratch, *, n_head, last_step):
    me = lax.axis_index("head")
    upper = lax.axis_index("ctx") // last_step % 2 == 1
    for j in range(q.shape[0]):
        att = o[j] + jnp.where(upper, dot(q[j], jb[j]), 0.0)
        scale = lax.rsqrt(jnp.mean(att * att, axis=-1, keepdims=True) + EPSILON)
        scratch[:, j * DV : (j + 1) * DV] = (att * scale * gate[j]).astype(BF16)
    part = scratch.shape[0] // n_head
    for i in range(n_head // 2):
        at = pl.multiple_of((me ^ (2 * i)) * part, 16)
        keep[i * part : (i + 1) * part, :] = scratch[pl.ds(at, part), :]
        at = pl.multiple_of((me ^ (2 * i + 1)) * part, 16)
        send[i * part : (i + 1) * part, :] = scratch[pl.ds(at, part), :]


def out_kernel(own, got, w_own, w_got, out, *, first, part):
    rows = slice(first * part, (first + 1) * part)
    a, b = own[rows, :], got[rows, :]
    out[...] = (dot(a, w_own[...]) + dot(b, w_got[...])).astype(out.dtype)


def call(body, out_shape, args, scratch=(), flops=0, any_space=(), **static):
    nbytes = sum(a.size * a.dtype.itemsize for a in args)
    vmem = pl.BlockSpec(memory_space=pltpu.VMEM)
    return pl.pallas_call(
        functools.partial(body, **static),
        out_shape=out_shape,
        in_specs=[pl.BlockSpec(memory_space=pl.ANY) if i in any_space else vmem for i in range(len(args))],
        out_specs=jax.tree.map(lambda _: vmem, out_shape),
        scratch_shapes=list(scratch),
        compiler_params=pltpu.CompilerParams(vmem_limit_bytes=VMEM_BYTES),
        cost_estimate=pl.CostEstimate(flops=flops, bytes_accessed=nbytes, transcendentals=0),
    )(*args)


def shaped(shape, dtype):
    return jax.ShapeDtypeStruct(shape, dtype)


def xor_sent(value, axis, step):
    count = lax.axis_size(axis)
    return lax.ppermute(value, axis, [(i, i ^ step) for i in range(count)])


def passed_along(value, axis, steps):
    count = lax.axis_size(axis)
    return lax.ppermute(value, axis, [(i, i + steps) for i in range(count - steps)])


def local(layer_in, in_proj, conv_weight, gate_logits, norm_gain, out_proj):
    n_head, n_ctx = lax.axis_size("head"), lax.axis_size("ctx")
    width, key_heads, group = in_proj.shape
    heads = gate_logits.shape[1]
    ratio = heads // key_heads
    part = layer_in.shape[0]
    toks = part * n_head
    ctx_head = ("ctx", "head")

    pieces = [layer_in] + [None] * (n_head - 1)
    step = n_head // 2
    while step:
        for s in range(0, n_head, 2 * step):
            pieces[s + step] = xor_sent(pieces[s], "head", step)
        step //= 2
    blocks = toks // HALF
    rows, cols, decays, tail = call(
        gates_kernel,
        (
            shaped((heads, toks), F32),
            shaped((toks, 2 * heads), F32),
            shaped((heads, blocks * (blocks + 1) // 2, HALF, HALF), F32),
            shaped((HALO, width), BF16),
        ),
        [gate_logits, layer_in],
        [pltpu.SemaphoreType.DMA],
        any_space=(1,),
    )
    me = lax.axis_index("head")
    halo = jnp.zeros_like(tail)
    for h in range(1, n_head, 2):
        target = h if h < n_head - 1 else h - 1
        perm = []
        for c in range(1, n_ctx):
            source, sink = (c - 1) * n_head + n_head - 1, c * n_head + target
            perm += [(source, sink), (sink, source)]
        halo = jnp.where(me == target, lax.ppermute(tail, ctx_head, perm), halo)
    halo_core = xor_sent(halo, "head", 1)
    v_end = 2 * DK + ratio * DV
    w_kv = in_proj[:, :, DK:v_end].reshape(width, key_heads * (v_end - DK))
    w_q = in_proj[:, :, 0:DK].reshape(width, key_heads * DK)
    w_z = in_proj[:, :, v_end:].reshape(width, heads * DV)

    state = shaped((heads, DK, DV), BF16)
    s_own, ys, keys, x_full = call(
        keys_kernel,
        (
            shaped((heads, DK, DK + DV), BF16),
            shaped((heads, toks, DK + DV), BF16),
            shaped((key_heads, toks, DK), BF16),
            shaped((HALO + toks, width), BF16),
        ),
        [*pieces, halo, halo_core, w_kv, conv_weight, cols, rows, decays],
        [pltpu.VMEM((key_heads * (1 + ratio), HALO + toks, 128), F32)],
        flops=2 * toks * width * group,
        n_head=n_head,
        key_heads=key_heads,
        ratio=ratio,
    )
    got = xor_sent(s_own, "ctx", 1)
    w_other = xor_sent(lax.optimization_barrier((out_proj, s_own))[0], "head", 1)
    q_shape = shaped((heads, toks, DK), BF16)
    o_shape = shaped((heads, toks, DV), F32)
    q, o, gate = call(
        queries_kernel,
        (q_shape, o_shape, o_shape),
        [x_full, w_q, w_z, conv_weight, cols, rows, keys, ys, norm_gain[None, :]],
        [pltpu.VMEM((key_heads, HALO + toks, 128), F32)],
        flops=2 * toks * width * group,
        key_heads=key_heads,
        ratio=ratio,
    )
    b, t = call(pair_kernel, (state, state), [s_own, got], flops=heads * 2**23)
    step = 2
    jb = passed_along(b, "ctx", step)
    jt = passed_along(t, "ctx", step)
    q, o = call(pair_absorb_kernel, (q_shape, o_shape), [q, o, got], flops=heads * 2**24)
    while 2 * step < n_ctx:
        b = call(join_b_kernel, state, [t, b, jb], flops=heads * 2**22)
        step *= 2
        more = 2 * step < n_ctx
        if more:
            t = call(join_t_kernel, state, [t, jt], flops=heads * 2**22)
        nb = passed_along(b, "ctx", step) if more else xor_sent(b, "ctx", step)
        nt = passed_along(t, "ctx", step) if more else None
        q, o = call(absorb_kernel, (q_shape, o_shape), [q, o, jb, jt], flops=heads * 2**24)
        jb, jt = nb, nt
    half = shaped((toks // 2, heads * DV), BF16)
    keep, send = call(
        normed_kernel,
        (half, half),
        [q, o, jb, gate],
        [pltpu.VMEM((toks, heads * DV), BF16)],
        flops=heads * 2**23,
        n_head=n_head,
        last_step=step,
    )
    other = xor_sent(send, "head", 1)
    out_args = [keep, other, out_proj, w_other]
    out = None
    partial = {}
    for i in reversed(range(n_head // 2)):
        dtype = F32 if i == 0 else BF16
        partial[i] = call(
            out_kernel, shaped((part, width), dtype), out_args, flops=part * width * 2**12, first=i, part=part
        )
        if i:
            partial[i] = xor_sent(partial[i], "head", 2 * i)
    for i in range(n_head // 2):
        out = partial[i].astype(F32) if out is None else out + partial[i].astype(F32)
    return out.astype(BF16)


def solution(mesh):
    in_specs = (
        P(("ctx", "head"), None),
        P(None, "head", None),
        P(None, "head", None),
        P(None, "head", "ctx"),
        P(),
        P("head", None),
    )
    out_specs = P(("ctx", "head"), None)
    return jax.shard_map(local, mesh=mesh, in_specs=in_specs, out_specs=out_specs, check_vma=False)
```

```python
import functools

import jax
import jax.numpy as jnp
from jax import lax
from jax.experimental import pallas as pl
from jax.experimental.pallas import tpu as pltpu
from jax.sharding import PartitionSpec as P

DK = 128
DV = 128
KERNEL = 4
HALO = 16
HALF = 128
EPSILON = 1e-06
F32 = jnp.float32
BF16 = jnp.bfloat16
VMEM_BYTES = 40 * 1024 * 1024


def dot(a, b):
    return jnp.dot(a, b, preferred_element_type=F32)


def dot_t(a, b):
    return lax.dot_general(a, b, (((1,), (1,)), ((), ())), preferred_element_type=F32)


def silu(x):
    return x / (1.0 + jnp.exp(-x))


def l2_normed(x):
    return x * lax.rsqrt(jnp.sum(x * x, axis=-1, keepdims=True) + EPSILON)


def conv_silu(padded, slot, weight, g, lanes, rows):
    acc = padded[slot, HALO - KERNEL + 1 : HALO - KERNEL + 1 + rows, :] * weight[0, g : g + 1, lanes]
    for i in range(1, KERNEL):
        lo = HALO - KERNEL + 1 + i
        acc = acc + padded[slot, lo : lo + rows, :] * weight[i, g : g + 1, lanes]
    return silu(acc)


def block_decay(ccol, crow, a, b):
    gap = ccol[a * HALF : (a + 1) * HALF] - crow[:, b * HALF : (b + 1) * HALF]
    return jnp.exp(jnp.minimum(gap, 0.0))


def gates_kernel(logits, x_any, rows, cols, decays, tail, x_own, sems):
    tail_copy = pltpu.make_async_copy(x_any.at[pl.ds(x_any.shape[0] - HALO, HALO), :], tail, sems.at[0])
    own_copy = pltpu.make_async_copy(x_any, x_own, sems.at[1])
    tail_copy.start()
    own_copy.start()
    toks = logits.shape[2]
    blocks = toks // HALF
    x = logits[0]
    log_decay = -(jnp.maximum(x, 0.0) + jnp.log1p(jnp.exp(-jnp.abs(x))))
    beta = 1.0 / (1.0 + jnp.exp(-logits[1]))
    heads = x.shape[0]
    ri = lax.broadcasted_iota(jnp.int32, (toks, toks), 0)
    ci = lax.broadcasted_iota(jnp.int32, (toks, toks), 1)
    exact = lax.Precision.HIGHEST
    rows[...] = jnp.dot(log_decay, (ri <= ci).astype(F32), precision=exact, preferred_element_type=F32)
    last_dims = (((1,), (1,)), ((), ()))
    ccols = lax.dot_general((ri >= ci).astype(F32), log_decay, last_dims, precision=exact, preferred_element_type=F32)
    bcols = lax.dot_general((ri == ci).astype(F32), beta, last_dims, precision=exact, preferred_element_type=F32)
    cols[:, 0:heads] = ccols
    cols[:, heads : 2 * heads] = bcols
    below = ri[:HALF, :HALF] > ci[:HALF, :HALF]
    for j in range(heads):
        i = 0
        for a in range(blocks):
            for b in range(a + 1):
                m = block_decay(ccols[:, j : j + 1], rows[j : j + 1, :], a, b)
                m = m * bcols[a * HALF : (a + 1) * HALF, j : j + 1]
                decays[j, i] = jnp.where(below, m, 0.0) if a == b else m
                i += 1
    tail_copy.wait()
    own_copy.wait()


def keys_kernel(*refs, n_head, key_heads, ratio):
    pieces = refs[:n_head]
    halo, halo_core, w, cw, cols, rows, decays, s_keep, s_send, y_out, k_out, x_out, padded, s_all = refs[n_head:]
    me = lax.axis_index("head")
    part = pieces[0].shape[0]
    toks = part * n_head
    blocks = toks // HALF
    heads = key_heads * ratio
    direct = (me % 2 == 1) != (me >= n_head - 2)
    x_out[0:HALO, :] = jnp.where(direct, halo[...], halo_core[...])
    for s in range(n_head):
        at = pl.multiple_of(HALO + (me ^ s) * part, 16)
        x_out[pl.ds(at, part), :] = pieces[s][...]
    width = DK + ratio * DV
    for g in range(key_heads):
        proj = dot(x_out[...], w[:, g * width : (g + 1) * width])
        proj = proj.astype(BF16).astype(F32)
        for t in range(1 + ratio):
            padded[g * (1 + ratio) + t] = proj[:, t * 128 : (t + 1) * 128]
    ri = lax.broadcasted_iota(jnp.int32, (HALF, HALF), 0)
    ci = lax.broadcasted_iota(jnp.int32, (HALF, HALF), 1)
    below = ri > ci
    level = jnp.where(below, ri ^ ci, 0)
    eye = jnp.where(ri == ci, 1.0, 0.0).astype(F32)
    kts, rhs, lowers, offs = [], [], [], []
    for g in range(key_heads):
        base = g * (1 + ratio)
        k = l2_normed(conv_silu(padded, base, cw, g, slice(DK, 2 * DK), toks))
        kb = k.astype(BF16)
        k_out[g] = kb
        kf = kb.astype(F32)
        kts.append(kf.T)
        ks = [kb[b * HALF : (b + 1) * HALF] for b in range(blocks)]
        grams = {(a, b): dot_t(ks[a], ks[b]) for a in range(blocks) for b in range(a + 1)}
        for r in range(ratio):
            j = g * ratio + r
            lanes = slice(2 * DK + r * DV, 2 * DK + (r + 1) * DV)
            v = conv_silu(padded, base + 1 + r, cw, g, lanes, toks)
            ccol = cols[:, j : j + 1]
            bcol = cols[:, heads + j : heads + j + 1]
            rk = (kf * (bcol * jnp.exp(ccol))).astype(BF16)
            rv = (v * bcol).astype(BF16)
            rhs.append(jnp.concatenate([rk, rv], axis=1))
            low, off, i = [], {}, 0
            for a in range(blocks):
                for b in range(a + 1):
                    m = grams[(a, b)] * decays[j, i]
                    i += 1
                    if a == b:
                        low.append(m)
                    else:
                        off[(a, b)] = m.astype(BF16)
            lowers += low
            offs.append(off)
    inv = [eye - jnp.where(level == 1, m, 0.0) for m in lowers]
    size = 2
    while size < HALF:
        here = (level >= size) & (level < 2 * size)
        inv_b = [m.astype(BF16) for m in inv]
        cx = [dot(jnp.where(here, m, 0.0).astype(BF16), x).astype(BF16) for m, x in zip(lowers, inv_b)]
        inv = [x - dot(xb, c) for x, xb, c in zip(inv, inv_b, cx)]
        size *= 2
    inv_b = [m.astype(BF16) for m in inv]
    for j in range(heads):
        ys = []
        for a in range(blocks):
            r = rhs[j][a * HALF : (a + 1) * HALF]
            if a:
                acc = r.astype(F32)
                for b in range(a):
                    acc = acc - dot(offs[j][(a, b)], ys[b])
                r = acc.astype(BF16)
            ys.append(dot(inv_b[j * blocks + a], r).astype(BF16))
        y = jnp.concatenate(ys, axis=0)
        y_out[j] = y
        crow = rows[j : j + 1, :]
        last = crow[:, toks - 1 : toks]
        kd = (kts[j // ratio] * jnp.exp(last - crow)).astype(BF16)
        s = dot(kd, y)
        s_all[j, :, 0:DK] = (eye * jnp.exp(last) - s[:, 0:DK]).astype(BF16)
        s_all[j, :, DK:] = s[:, DK:].astype(BF16)
    odd = lax.axis_index("ctx") % 2
    half = heads // 2
    s_keep[...] = s_all[pl.ds(odd * half, half)]
    s_send[...] = s_all[pl.ds((1 - odd) * half, half)]


def queries_kernel(x, wq, wz, cw, cols, rows, keys, ys, gain, q_out, o_out, g_out, padded, *, key_heads, ratio):
    toks = x.shape[0] - HALO
    blocks = toks // HALF
    ri = lax.broadcasted_iota(jnp.int32, (HALF, HALF), 0)
    ci = lax.broadcasted_iota(jnp.int32, (HALF, HALF), 1)
    upto = ri >= ci
    for g in range(key_heads):
        padded[g] = dot(x[...], wq[:, g * DK : (g + 1) * DK]).astype(BF16).astype(F32)
        proj = dot(x[HALO:, :], wz[:, g * ratio * DV : (g + 1) * ratio * DV]).astype(BF16).astype(F32)
        for r in range(ratio):
            z = proj[:, r * DV : (r + 1) * DV]
            g_out[g * ratio + r] = gain[...] * silu(z)
    for g in range(key_heads):
        q = l2_normed(conv_silu(padded, g, cw, g, slice(0, DK), toks)) * DK ** (-0.5)
        qb = q.astype(BF16)
        kb = keys[g]
        grams = {
            (a, b): dot_t(qb[a * HALF : (a + 1) * HALF], kb[b * HALF : (b + 1) * HALF])
            for a in range(blocks)
            for b in range(a + 1)
        }
        for r in range(ratio):
            j = g * ratio + r
            ccol = cols[:, j : j + 1]
            crow = rows[j : j + 1, :]
            for a in range(blocks):
                at = slice(a * HALF, (a + 1) * HALF)
                acc = None
                for b in range(a + 1):
                    m = grams[(a, b)] * block_decay(ccol, crow, a, b)
                    if a == b:
                        m = jnp.where(upto, m, 0.0)
                    term = dot(m.astype(BF16), ys[j, b * HALF : (b + 1) * HALF, :])
                    acc = term if acc is None else acc + term
                q_out[j, at, :] = (q[at] * jnp.exp(ccol[at]) - acc[:, 0:DK]).astype(BF16)
                o_out[j, at, :] = acc[:, DK:]


def placed(step):
    return lax.axis_index("ctx") // step % 2 == 1


def join_kernel(own, got, out, *, step):
    upper = placed(step)
    for j in range(own.shape[0]):
        mine, other = own[j], got[j]
        later = jnp.where(upper, mine, other)
        earlier = jnp.where(upper, other, mine)
        if out.shape[-1] == DV:
            out[j] = (dot(later[:, 0:DK], earlier[:, DK:]) + later[:, DK:].astype(F32)).astype(BF16)
        else:
            prod = dot(later[:, 0:DK], earlier)
            out[j, :, 0:DK] = prod[:, 0:DK].astype(BF16)
            out[j, :, DK:] = (prod[:, DK:] + later[:, DK:].astype(F32)).astype(BF16)


def prefix_kernel(before, got, out, *, step):
    upper = placed(step)
    for j in range(before.shape[0]):
        prod = dot(before[j, :, 0:DK], got[j])
        prod_t, prod_b = prod[:, 0:DK], prod[:, DK:] + before[j, :, DK:].astype(F32)
        out[j, :, 0:DK] = jnp.where(upper, prod_t.astype(BF16), before[j, :, 0:DK])
        out[j, :, DK:] = jnp.where(upper, prod_b.astype(BF16), before[j, :, DK:])


def states_kernel(own, pair, before, got, keep, send, *, before_step, step):
    odd = placed(1)
    began = placed(before_step)
    upper = placed(step)
    for j in range(own.shape[0]):
        t, b = before[j, :, 0:DK], before[j, :, DK:].astype(F32)
        if before_step == 2:
            last = got[j].astype(F32)
            entered = jnp.where(began, dot(t, got[j]), last)
            b = jnp.where(began, b, 0.0)
        else:
            entered = dot(t, got[j])
        entered = jnp.where(upper, entered, 0.0) + b
        first = jnp.where(odd, pair[j], own[j])
        passed = dot(first[:, 0:DK], entered.astype(BF16)) + first[:, DK:].astype(F32)
        keep[j] = jnp.where(odd, passed, entered).astype(BF16)
        send[j] = jnp.where(odd, entered, passed).astype(BF16)


def normed_kernel(q, o, own, got, gate, keep, send, scratch, *, n_head):
    me = lax.axis_index("head")
    odd = placed(1)
    half = own.shape[0]
    for j in range(q.shape[0]):
        mine, other = own[j % half], got[j % half]
        state = jnp.where(odd, mine, other) if j >= half else jnp.where(odd, other, mine)
        att = o[j] + dot(q[j], state)
        scale = lax.rsqrt(jnp.mean(att * att, axis=-1, keepdims=True) + EPSILON)
        scratch[:, j * DV : (j + 1) * DV] = (att * scale * gate[j]).astype(BF16)
    part = scratch.shape[0] // n_head
    for i in range(n_head // 2):
        at = pl.multiple_of((me ^ (2 * i)) * part, 16)
        keep[i * part : (i + 1) * part, :] = scratch[pl.ds(at, part), :]
        at = pl.multiple_of((me ^ (2 * i + 1)) * part, 16)
        send[i * part : (i + 1) * part, :] = scratch[pl.ds(at, part), :]


def out_kernel(own, got, w_own, w_got, out, *, first, part):
    rows = slice(first * part, (first + 1) * part)
    a, b = own[rows, :], got[rows, :]
    out[...] = (dot(a, w_own[...]) + dot(b, w_got[...])).astype(out.dtype)


def call(body, out_shape, args, scratch=(), flops=0, any_space=(), **static):
    nbytes = sum(a.size * a.dtype.itemsize for a in args)
    vmem = pl.BlockSpec(memory_space=pltpu.VMEM)
    return pl.pallas_call(
        functools.partial(body, **static),
        out_shape=out_shape,
        in_specs=[pl.BlockSpec(memory_space=pl.ANY) if i in any_space else vmem for i in range(len(args))],
        out_specs=jax.tree.map(lambda _: vmem, out_shape),
        scratch_shapes=list(scratch),
        compiler_params=pltpu.CompilerParams(vmem_limit_bytes=VMEM_BYTES),
        cost_estimate=pl.CostEstimate(flops=flops, bytes_accessed=nbytes, transcendentals=0),
    )(*args)


def shaped(shape, dtype):
    return jax.ShapeDtypeStruct(shape, dtype)


def xor_sent(value, axis, step):
    count = lax.axis_size(axis)
    return lax.ppermute(value, axis, [(i, i ^ step) for i in range(count)])


def passed_along(value, axis, steps):
    count = lax.axis_size(axis)
    return lax.ppermute(value, axis, [(i, i + steps) for i in range(count - steps)])


def local(layer_in, in_proj, conv_weight, gate_logits, norm_gain, out_proj):
    n_head, n_ctx = lax.axis_size("head"), lax.axis_size("ctx")
    width, key_heads, group = in_proj.shape
    heads = gate_logits.shape[1]
    ratio = heads // key_heads
    part = layer_in.shape[0]
    toks = part * n_head
    ctx_head = ("ctx", "head")

    pieces = [layer_in] + [None] * (n_head - 1)
    step = n_head // 2
    while step:
        for s in range(0, n_head, 2 * step):
            pieces[s + step] = xor_sent(pieces[s], "head", step)
        step //= 2
    blocks = toks // HALF
    rows, cols, decays, tail, x_own = call(
        gates_kernel,
        (
            shaped((heads, toks), F32),
            shaped((toks, 2 * heads), F32),
            shaped((heads, blocks * (blocks + 1) // 2, HALF, HALF), F32),
            shaped((HALO, width), BF16),
            shaped((part, width), BF16),
        ),
        [gate_logits, layer_in],
        [pltpu.SemaphoreType.DMA((2,))],
        any_space=(1,),
    )
    me = lax.axis_index("head")
    halo = jnp.zeros_like(tail)
    for h in range(1, n_head, 2):
        target = h if h < n_head - 1 else h - 1
        perm = []
        for c in range(1, n_ctx):
            source, sink = (c - 1) * n_head + n_head - 1, c * n_head + target
            perm += [(source, sink), (sink, source)]
        halo = jnp.where(me == target, lax.ppermute(tail, ctx_head, perm), halo)
    halo_core = xor_sent(halo, "head", 1)
    v_end = 2 * DK + ratio * DV
    w_kv = in_proj[:, :, DK:v_end].reshape(width, key_heads * (v_end - DK))
    w_q = in_proj[:, :, 0:DK].reshape(width, key_heads * DK)
    w_z = in_proj[:, :, v_end:].reshape(width, heads * DV)

    half = heads // 2
    pair_shape = shaped((half, DK, DK + DV), BF16)
    state_shape = shaped((half, DK, DV), BF16)
    s_keep, s_send, ys, keys, x_full = call(
        keys_kernel,
        (
            pair_shape,
            pair_shape,
            shaped((heads, toks, DK + DV), BF16),
            shaped((key_heads, toks, DK), BF16),
            shaped((HALO + toks, width), BF16),
        ),
        [x_own, *pieces[1:], halo, halo_core, w_kv, conv_weight, cols, rows, decays],
        [
            pltpu.VMEM((key_heads * (1 + ratio), HALO + toks, 128), F32),
            pltpu.VMEM((heads, DK, DK + DV), BF16),
        ],
        flops=2 * toks * width * group,
        n_head=n_head,
        key_heads=key_heads,
        ratio=ratio,
    )
    s_pair = xor_sent(s_send, "ctx", 1)
    w_other = xor_sent(lax.optimization_barrier((out_proj, s_keep))[0], "head", 1)
    o_shape = shaped((heads, toks, DV), F32)
    q, o, gate = call(
        queries_kernel,
        (shaped((heads, toks, DK), BF16), o_shape, o_shape),
        [x_full, w_q, w_z, conv_weight, cols, rows, keys, ys, norm_gain[None, :]],
        [pltpu.VMEM((key_heads, HALO + toks, 128), F32)],
        flops=2 * toks * width * group,
        key_heads=key_heads,
        ratio=ratio,
    )
    total = call(join_kernel, pair_shape, [s_keep, s_pair], flops=heads * 2**22, step=1)
    step, before, before_step = 2, None, 2
    while 2 * step < n_ctx:
        got = xor_sent(total, "ctx", step)
        more = 4 * step < n_ctx
        total = call(join_kernel, pair_shape if more else state_shape, [total, got], flops=heads * 2**22, step=step)
        if before is None:
            before = got
        else:
            if before_step == 2:
                entry = jnp.concatenate([jnp.eye(DK, dtype=BF16), jnp.zeros((DK, DV), BF16)], axis=1)
                before = jnp.where(lax.axis_index("ctx") // 2 % 2 == 1, before, entry)
                before_step = 1
            before = call(prefix_kernel, pair_shape, [before, got], step=step)
        step *= 2
    got = xor_sent(total, "ctx", step)
    own_state, out_state = call(
        states_kernel,
        (state_shape, state_shape),
        [s_keep, s_pair, before, got],
        before_step=before_step,
        step=step,
    )
    got_state = xor_sent(out_state, "ctx", 1)
    rows_shape = shaped((toks // 2, heads * DV), BF16)
    keep, send = call(
        normed_kernel,
        (rows_shape, rows_shape),
        [q, o, own_state, got_state, gate],
        [pltpu.VMEM((toks, heads * DV), BF16)],
        flops=heads * 2**23,
        n_head=n_head,
    )
    other = xor_sent(send, "head", 1)
    out_args = [keep, other, out_proj, w_other]
    out = None
    partial = {}
    for i in reversed(range(n_head // 2)):
        dtype = F32 if i == 0 else BF16
        partial[i] = call(
            out_kernel, shaped((part, width), dtype), out_args, flops=part * width * 2**12, first=i, part=part
        )
        if i:
            partial[i] = xor_sent(partial[i], "head", 2 * i)
    for i in range(n_head // 2):
        out = partial[i].astype(F32) if out is None else out + partial[i].astype(F32)
    return out.astype(BF16)


def solution(mesh):
    in_specs = (
        P(("ctx", "head"), None),
        P(None, "head", None),
        P(None, "head", None),
        P(None, "head", "ctx"),
        P(),
        P("head", None),
    )
    out_specs = P(("ctx", "head"), None)
    return jax.shard_map(local, mesh=mesh, in_specs=in_specs, out_specs=out_specs, check_vma=False)
```

```python
import functools

import jax
import jax.numpy as jnp
from jax import lax
from jax.experimental import pallas as pl
from jax.experimental.pallas import tpu as pltpu
from jax.sharding import PartitionSpec as P

DK = 128
DV = 128
KERNEL = 4
HALO = 16
HALF = 128
EPSILON = 1e-06
F32 = jnp.float32
BF16 = jnp.bfloat16
VMEM_BYTES = 24 * 1024 * 1024


def dot(a, b):
    return jnp.dot(a, b, preferred_element_type=F32)


def dot_t(a, b):
    return lax.dot_general(a, b, (((1,), (1,)), ((), ())), preferred_element_type=F32)


def silu(x):
    return x / (1.0 + jnp.exp(-x))


def l2_normed(x):
    return x * lax.rsqrt(jnp.sum(x * x, axis=-1, keepdims=True) + EPSILON)


def conv_silu(padded, slot, weight, g, lanes, rows):
    acc = padded[slot, HALO - KERNEL + 1 : HALO - KERNEL + 1 + rows, :] * weight[0, g : g + 1, lanes]
    for i in range(1, KERNEL):
        lo = HALO - KERNEL + 1 + i
        acc = acc + padded[slot, lo : lo + rows, :] * weight[i, g : g + 1, lanes]
    return silu(acc)


def block_decay(ccol, crow, a, b):
    gap = ccol[a * HALF : (a + 1) * HALF] - crow[:, b * HALF : (b + 1) * HALF]
    return jnp.exp(jnp.minimum(gap, 0.0))


def gates_kernel(logits_any, x_any, rows, cols, decays, tail, x_own, logits, sems):
    logits_copy = pltpu.make_async_copy(logits_any, logits, sems.at[3])
    logits_copy.start()
    tail_copy = pltpu.make_async_copy(x_any.at[pl.ds(x_any.shape[0] - HALO, HALO), :], tail, sems.at[0])
    own_copy = pltpu.make_async_copy(x_any, x_own, sems.at[1])
    tail_copy.start()
    own_copy.start()
    logits_copy.wait()
    toks = logits.shape[2]
    blocks = toks // HALF
    x = logits[0]
    log_decay = -(jnp.maximum(x, 0.0) + jnp.log1p(jnp.exp(-jnp.abs(x))))
    beta = 1.0 / (1.0 + jnp.exp(-logits[1]))
    heads = x.shape[0]
    ri = lax.broadcasted_iota(jnp.int32, (toks, toks), 0)
    ci = lax.broadcasted_iota(jnp.int32, (toks, toks), 1)
    exact = lax.Precision.HIGHEST
    rows[...] = jnp.dot(log_decay, (ri <= ci).astype(F32), precision=exact, preferred_element_type=F32)
    last_dims = (((1,), (1,)), ((), ()))
    ccols = lax.dot_general((ri >= ci).astype(F32), log_decay, last_dims, precision=exact, preferred_element_type=F32)
    bcols = lax.dot_general((ri == ci).astype(F32), beta, last_dims, precision=exact, preferred_element_type=F32)
    cols[:, 0:heads] = ccols
    cols[:, heads : 2 * heads] = bcols
    below = ri[:HALF, :HALF] > ci[:HALF, :HALF]
    for j in range(heads):
        i = 0
        for a in range(blocks):
            for b in range(a + 1):
                m = block_decay(ccols[:, j : j + 1], rows[j : j + 1, :], a, b)
                m = m * bcols[a * HALF : (a + 1) * HALF, j : j + 1]
                decays[j, i] = jnp.where(below, m, 0.0) if a == b else m
                i += 1
    tail_copy.wait()
    own_copy.wait()


def keys_kernel(*refs, n_head, key_heads, ratio):
    pieces = refs[:n_head]
    halo, halo_core, w, cw, cols, rows, decays, s_keep, s_send, y_out, k_out, x_out, padded, s_all = refs[n_head:]
    me = lax.axis_index("head")
    part = pieces[0].shape[0]
    toks = part * n_head
    blocks = toks // HALF
    heads = key_heads * ratio
    direct = (me % 2 == 1) != (me >= n_head - 2)
    x_out[0:HALO, :] = jnp.where(direct, halo[...], halo_core[...])
    for s in range(n_head):
        at = pl.multiple_of(HALO + (me ^ s) * part, 16)
        x_out[pl.ds(at, part), :] = pieces[s][...]
    width = DK + ratio * DV
    for g in range(key_heads):
        proj = dot(x_out[...], w[:, g * width : (g + 1) * width])
        proj = proj.astype(BF16).astype(F32)
        for t in range(1 + ratio):
            padded[g * (1 + ratio) + t] = proj[:, t * 128 : (t + 1) * 128]
    ri = lax.broadcasted_iota(jnp.int32, (HALF, HALF), 0)
    ci = lax.broadcasted_iota(jnp.int32, (HALF, HALF), 1)
    below = ri > ci
    level = jnp.where(below, ri ^ ci, 0)
    eye = jnp.where(ri == ci, 1.0, 0.0).astype(F32)
    kts, rhs, lowers, offs = [], [], [], []
    for g in range(key_heads):
        base = g * (1 + ratio)
        k = l2_normed(conv_silu(padded, base, cw, g, slice(DK, 2 * DK), toks))
        kb = k.astype(BF16)
        k_out[g] = kb
        kf = kb.astype(F32)
        kts.append(kf.T)
        ks = [kb[b * HALF : (b + 1) * HALF] for b in range(blocks)]
        grams = {(a, b): dot_t(ks[a], ks[b]) for a in range(blocks) for b in range(a + 1)}
        for r in range(ratio):
            j = g * ratio + r
            lanes = slice(2 * DK + r * DV, 2 * DK + (r + 1) * DV)
            v = conv_silu(padded, base + 1 + r, cw, g, lanes, toks)
            ccol = cols[:, j : j + 1]
            bcol = cols[:, heads + j : heads + j + 1]
            rk = (kf * (bcol * jnp.exp(ccol))).astype(BF16)
            rv = (v * bcol).astype(BF16)
            rhs.append(jnp.concatenate([rk, rv], axis=1))
            low, off, i = [], {}, 0
            for a in range(blocks):
                for b in range(a + 1):
                    m = grams[(a, b)] * decays[j, i]
                    i += 1
                    if a == b:
                        low.append(m)
                    else:
                        off[(a, b)] = m.astype(BF16)
            lowers += low
            offs.append(off)
    inv = [eye - jnp.where(level == 1, m, 0.0) for m in lowers]
    size = 2
    while size < HALF:
        here = (level >= size) & (level < 2 * size)
        inv_b = [m.astype(BF16) for m in inv]
        cx = [dot(jnp.where(here, m, 0.0).astype(BF16), x).astype(BF16) for m, x in zip(lowers, inv_b)]
        inv = [x - dot(xb, c) for x, xb, c in zip(inv, inv_b, cx)]
        size *= 2
    inv_b = [m.astype(BF16) for m in inv]
    for j in range(heads):
        ys = []
        for a in range(blocks):
            r = rhs[j][a * HALF : (a + 1) * HALF]
            if a:
                acc = r.astype(F32)
                for b in range(a):
                    acc = acc - dot(offs[j][(a, b)], ys[b])
                r = acc.astype(BF16)
            ys.append(dot(inv_b[j * blocks + a], r).astype(BF16))
        y = jnp.concatenate(ys, axis=0)
        y_out[j] = y
        crow = rows[j : j + 1, :]
        last = crow[:, toks - 1 : toks]
        kd = (kts[j // ratio] * jnp.exp(last - crow)).astype(BF16)
        s = dot(kd, y)
        s_all[j, :, 0:DK] = (eye * jnp.exp(last) - s[:, 0:DK]).astype(BF16)
        s_all[j, :, DK:] = s[:, DK:].astype(BF16)
    odd = lax.axis_index("ctx") % 2
    half = heads // 2
    s_keep[...] = s_all[pl.ds(odd * half, half)]
    s_send[...] = s_all[pl.ds((1 - odd) * half, half)]


def queries_kernel(x, wq, wz, cw, cols, rows, keys, ys, gain, q_out, o_out, g_out, padded, *, key_heads, ratio):
    toks = x.shape[0] - HALO
    blocks = toks // HALF
    ri = lax.broadcasted_iota(jnp.int32, (HALF, HALF), 0)
    ci = lax.broadcasted_iota(jnp.int32, (HALF, HALF), 1)
    upto = ri >= ci
    for g in range(key_heads):
        padded[g] = dot(x[...], wq[:, g * DK : (g + 1) * DK]).astype(BF16).astype(F32)
        proj = dot(x[HALO:, :], wz[:, g * ratio * DV : (g + 1) * ratio * DV]).astype(BF16).astype(F32)
        for r in range(ratio):
            z = proj[:, r * DV : (r + 1) * DV]
            g_out[g * ratio + r] = gain[...] * silu(z)
    for g in range(key_heads):
        q = l2_normed(conv_silu(padded, g, cw, g, slice(0, DK), toks)) * DK ** (-0.5)
        qb = q.astype(BF16)
        kb = keys[g]
        grams = {
            (a, b): dot_t(qb[a * HALF : (a + 1) * HALF], kb[b * HALF : (b + 1) * HALF])
            for a in range(blocks)
            for b in range(a + 1)
        }
        for r in range(ratio):
            j = g * ratio + r
            ccol = cols[:, j : j + 1]
            crow = rows[j : j + 1, :]
            for a in range(blocks):
                at = slice(a * HALF, (a + 1) * HALF)
                acc = None
                for b in range(a + 1):
                    m = grams[(a, b)] * block_decay(ccol, crow, a, b)
                    if a == b:
                        m = jnp.where(upto, m, 0.0)
                    term = dot(m.astype(BF16), ys[j, b * HALF : (b + 1) * HALF, :])
                    acc = term if acc is None else acc + term
                q_out[j, at, :] = (q[at] * jnp.exp(ccol[at]) - acc[:, 0:DK]).astype(BF16)
                o_out[j, at, :] = acc[:, DK:]


def placed(step):
    return lax.axis_index("ctx") // step % 2 == 1


def join_kernel(own, got, out, *, step):
    upper = placed(step)
    for j in range(own.shape[0]):
        mine, other = own[j], got[j]
        later = jnp.where(upper, mine, other)
        earlier = jnp.where(upper, other, mine)
        if out.shape[-1] == DV:
            out[j] = (dot(later[:, 0:DK], earlier[:, DK:]) + later[:, DK:].astype(F32)).astype(BF16)
        else:
            prod = dot(later[:, 0:DK], earlier)
            out[j, :, 0:DK] = prod[:, 0:DK].astype(BF16)
            out[j, :, DK:] = (prod[:, DK:] + later[:, DK:].astype(F32)).astype(BF16)


def prefix_kernel(before, got, out, *, step):
    upper = placed(step)
    for j in range(before.shape[0]):
        prod = dot(before[j, :, 0:DK], got[j])
        prod_t, prod_b = prod[:, 0:DK], prod[:, DK:] + before[j, :, DK:].astype(F32)
        out[j, :, 0:DK] = jnp.where(upper, prod_t.astype(BF16), before[j, :, 0:DK])
        out[j, :, DK:] = jnp.where(upper, prod_b.astype(BF16), before[j, :, DK:])


def states_kernel(own, pair, before, got, keep, send, *, before_step, step):
    odd = placed(1)
    began = placed(before_step)
    upper = placed(step)
    for j in range(own.shape[0]):
        t, b = before[j, :, 0:DK], before[j, :, DK:].astype(F32)
        if before_step == 2:
            last = got[j].astype(F32)
            entered = jnp.where(began, dot(t, got[j]), last)
            b = jnp.where(began, b, 0.0)
        else:
            entered = dot(t, got[j])
        entered = jnp.where(upper, entered, 0.0) + b
        first = jnp.where(odd, pair[j], own[j])
        passed = dot(first[:, 0:DK], entered.astype(BF16)) + first[:, DK:].astype(F32)
        keep[j] = jnp.where(odd, passed, entered).astype(BF16)
        send[j] = jnp.where(odd, entered, passed).astype(BF16)


def normed_kernel(q, o, own, got, gate, keep, send, scratch, *, n_head):
    me = lax.axis_index("head")
    odd = placed(1)
    half = own.shape[0]
    for j in range(q.shape[0]):
        mine, other = own[j % half], got[j % half]
        state = jnp.where(odd, mine, other) if j >= half else jnp.where(odd, other, mine)
        att = o[j] + dot(q[j], state)
        scale = lax.rsqrt(jnp.mean(att * att, axis=-1, keepdims=True) + EPSILON)
        scratch[:, j * DV : (j + 1) * DV] = (att * scale * gate[j]).astype(BF16)
    part = scratch.shape[0] // n_head
    for i in range(n_head // 2):
        at = pl.multiple_of((me ^ (2 * i)) * part, 16)
        keep[i * part : (i + 1) * part, :] = scratch[pl.ds(at, part), :]
        at = pl.multiple_of((me ^ (2 * i + 1)) * part, 16)
        send[i * part : (i + 1) * part, :] = scratch[pl.ds(at, part), :]


def out_kernel(own, got, w_own, w_got, out, *, first, part):
    rows = slice(first * part, (first + 1) * part)
    a, b = own[rows, :], got[rows, :]
    out[...] = (dot(a, w_own[...]) + dot(b, w_got[...])).astype(out.dtype)


def call(body, out_shape, args, us, scratch=(), any_space=(), **static):
    nbytes = sum(a.size * a.dtype.itemsize for a in args)
    vmem = pl.BlockSpec(memory_space=pltpu.VMEM)
    args = [pltpu.with_memory_space_constraint(a, pltpu.HBM) if i in any_space else a for i, a in enumerate(args)]
    return pl.pallas_call(
        functools.partial(body, **static),
        out_shape=out_shape,
        in_specs=[pl.BlockSpec(memory_space=pltpu.HBM) if i in any_space else vmem for i in range(len(args))],
        out_specs=jax.tree.map(lambda _: vmem, out_shape),
        scratch_shapes=list(scratch),
        compiler_params=pltpu.CompilerParams(vmem_limit_bytes=VMEM_BYTES),
        cost_estimate=pl.CostEstimate(flops=int(us * 1.15e9), bytes_accessed=nbytes, transcendentals=0),
    )(*args)


def shaped(shape, dtype):
    return jax.ShapeDtypeStruct(shape, dtype)


def xor_sent(value, axis, step):
    count = lax.axis_size(axis)
    return lax.ppermute(value, axis, [(i, i ^ step) for i in range(count)])


def passed_along(value, axis, steps):
    count = lax.axis_size(axis)
    return lax.ppermute(value, axis, [(i, i + steps) for i in range(count - steps)])


def local(layer_in, in_proj, conv_weight, gate_logits, norm_gain, out_proj):
    n_head, n_ctx = lax.axis_size("head"), lax.axis_size("ctx")
    width, key_heads, group = in_proj.shape
    heads = gate_logits.shape[1]
    ratio = heads // key_heads
    part = layer_in.shape[0]
    toks = part * n_head
    ctx_head = ("ctx", "head")

    pieces = [layer_in] + [None] * (n_head - 1)
    step = n_head // 2
    while step:
        for s in range(0, n_head, 2 * step):
            pieces[s + step] = xor_sent(pieces[s], "head", step)
        step //= 2
    blocks = toks // HALF
    rows, cols, decays, tail, x_own = call(
        gates_kernel,
        (
            shaped((heads, toks), F32),
            shaped((toks, 2 * heads), F32),
            shaped((heads, blocks * (blocks + 1) // 2, HALF, HALF), F32),
            shaped((HALO, width), BF16),
            shaped((part, width), BF16),
        ),
        [gate_logits, layer_in],
        1.1,
        [pltpu.VMEM(gate_logits.shape, F32), pltpu.SemaphoreType.DMA((4,))],
        any_space=(0, 1),
    )
    me = lax.axis_index("head")
    halo = jnp.zeros_like(tail)
    for h in range(n_head - 1, 0, -2):
        target = h if h < n_head - 1 else h - 1
        perm = []
        for c in range(1, n_ctx):
            source, sink = (c - 1) * n_head + n_head - 1, c * n_head + target
            perm += [(source, sink), (sink, source)]
        halo = jnp.where(me == target, lax.ppermute(tail, ctx_head, perm), halo)
    v_end = 2 * DK + ratio * DV
    w_kv = in_proj[:, :, DK:v_end].reshape(width, key_heads * (v_end - DK))
    halo, w_kv = lax.optimization_barrier((halo, w_kv))
    halo_core = xor_sent(halo, "head", 1)
    w_q = in_proj[:, :, 0:DK].reshape(width, key_heads * DK)
    w_z = in_proj[:, :, v_end:].reshape(width, heads * DV)

    half = heads // 2
    pair_shape = shaped((half, DK, DK + DV), BF16)
    state_shape = shaped((half, DK, DV), BF16)
    s_keep, s_send, ys, keys, x_full = call(
        keys_kernel,
        (
            pair_shape,
            pair_shape,
            shaped((heads, toks, DK + DV), BF16),
            shaped((key_heads, toks, DK), BF16),
            shaped((HALO + toks, width), BF16),
        ),
        [x_own, *pieces[1:], halo, halo_core, w_kv, conv_weight, cols, rows, decays],
        5.0,
        [
            pltpu.VMEM((key_heads * (1 + ratio), HALO + toks, 128), F32),
            pltpu.VMEM((heads, DK, DK + DV), BF16),
        ],
        n_head=n_head,
        key_heads=key_heads,
        ratio=ratio,
    )
    s_pair = xor_sent(s_send, "ctx", 1)
    w_other = xor_sent(lax.optimization_barrier((out_proj, s_keep))[0], "head", 1)
    o_shape = shaped((heads, toks, DV), F32)
    q, o, gate = call(
        queries_kernel,
        (shaped((heads, toks, DK), BF16), o_shape, o_shape),
        [x_full, w_q, w_z, conv_weight, cols, rows, keys, ys, norm_gain[None, :]],
        1.9,
        [pltpu.VMEM((key_heads, HALO + toks, 128), F32)],
        key_heads=key_heads,
        ratio=ratio,
    )
    total = call(join_kernel, pair_shape, [s_keep, s_pair], 0.2, step=1)
    step, before, before_step = 2, None, 2
    while 2 * step < n_ctx:
        got = xor_sent(total, "ctx", step)
        more = 4 * step < n_ctx
        total = call(join_kernel, pair_shape if more else state_shape, [total, got], 0.2, step=step)
        if before is None:
            before = got
        else:
            if before_step == 2:
                entry = jnp.concatenate([jnp.eye(DK, dtype=BF16), jnp.zeros((DK, DV), BF16)], axis=1)
                before = jnp.where(lax.axis_index("ctx") // 2 % 2 == 1, before, entry)
                before_step = 1
            before = call(prefix_kernel, pair_shape, [before, got], 0.2, step=step)
        step *= 2
    got = xor_sent(total, "ctx", step)
    own_state, out_state = call(
        states_kernel,
        (state_shape, state_shape),
        [s_keep, s_pair, before, got],
        0.3,
        before_step=before_step,
        step=step,
    )
    got_state = xor_sent(out_state, "ctx", 1)
    rows_shape = shaped((toks // 2, heads * DV), BF16)
    keep, send = call(
        normed_kernel,
        (rows_shape, rows_shape),
        [q, o, own_state, got_state, gate],
        0.4,
        [pltpu.VMEM((toks, heads * DV), BF16)],
        n_head=n_head,
    )
    other = xor_sent(send, "head", 1)
    out_args = [keep, other, out_proj, w_other]
    out = None
    partial = {}
    for i in reversed(range(n_head // 2)):
        dtype = F32 if i == 0 else BF16
        partial[i] = call(
            out_kernel, shaped((part, width), dtype), out_args, 0.8, first=i, part=part
        )
        if i:
            partial[i] = xor_sent(partial[i], "head", 2 * i)
    for i in range(n_head // 2):
        out = partial[i].astype(F32) if out is None else out + partial[i].astype(F32)
    return out.astype(BF16)


def solution(mesh):
    in_specs = (
        P(("ctx", "head"), None),
        P(None, "head", None),
        P(None, "head", None),
        P(None, "head", "ctx"),
        P(),
        P("head", None),
    )
    out_specs = P(("ctx", "head"), None)
    return jax.shard_map(local, mesh=mesh, in_specs=in_specs, out_specs=out_specs, check_vma=False)
```

```python
import functools

import jax
import jax.numpy as jnp
from jax import lax
from jax.experimental import pallas as pl
from jax.experimental.pallas import tpu as pltpu
from jax.sharding import PartitionSpec as P

DK = 128
DV = 128
KERNEL = 4
HALO = 16
HALF = 128
EPSILON = 1e-06
F32 = jnp.float32
BF16 = jnp.bfloat16
VMEM_BYTES = 24 * 1024 * 1024


def dot(a, b):
    return jnp.dot(a, b, preferred_element_type=F32)


def dot_t(a, b):
    return lax.dot_general(a, b, (((1,), (1,)), ((), ())), preferred_element_type=F32)


def silu(x):
    return x / (1.0 + jnp.exp(-x))


def l2_normed(x):
    return x * lax.rsqrt(jnp.sum(x * x, axis=-1, keepdims=True) + EPSILON)


def conv_silu(padded, slot, weights, rows):
    acc = padded[slot, HALO - KERNEL + 1 : HALO - KERNEL + 1 + rows, :] * weights[0]
    for i in range(1, KERNEL):
        lo = HALO - KERNEL + 1 + i
        acc = acc + padded[slot, lo : lo + rows, :] * weights[i]
    return silu(acc)


def block_decay(ccol, crow, a, b):
    gap = ccol[a * HALF : (a + 1) * HALF] - crow[:, b * HALF : (b + 1) * HALF]
    return jnp.exp(jnp.minimum(gap, 0.0))


def placed(step):
    return lax.axis_index("ctx") // step % 2 == 1


def true_index(local, count):
    half = count // 2
    odd = lax.axis_index("ctx") % 2
    return (1 - odd if local < half else odd) * half + local % half


def fetch_kernel(x_any, logits_any, tail, x_own, logits, sems):
    logits_copy = pltpu.make_async_copy(logits_any, logits, sems.at[2])
    tail_copy = pltpu.make_async_copy(x_any.at[pl.ds(x_any.shape[0] - HALO, HALO), :], tail, sems.at[0])
    own_copy = pltpu.make_async_copy(x_any, x_own, sems.at[1])
    tail_copy.start()
    own_copy.start()
    logits_copy.start()
    tail_copy.wait()
    own_copy.wait()
    logits_copy.wait()


def gates_kernel(logits, rows, cols, decays):
    toks = logits.shape[2]
    blocks = toks // HALF
    half = logits.shape[1] // 2
    given = [logits[i] for i in range(2)]
    given = [jnp.where(placed(1), a, jnp.concatenate([a[half:], a[:half]], axis=0)) for a in given]
    x = given[0]
    log_decay = -(jnp.maximum(x, 0.0) + jnp.log1p(jnp.exp(-jnp.abs(x))))
    beta = 1.0 / (1.0 + jnp.exp(-given[1]))
    heads = x.shape[0]
    ri = lax.broadcasted_iota(jnp.int32, (toks, toks), 0)
    ci = lax.broadcasted_iota(jnp.int32, (toks, toks), 1)
    exact = lax.Precision.HIGHEST
    rows[...] = jnp.dot(log_decay, (ri <= ci).astype(F32), precision=exact, preferred_element_type=F32)
    last_dims = (((1,), (1,)), ((), ()))
    ccols = lax.dot_general((ri >= ci).astype(F32), log_decay, last_dims, precision=exact, preferred_element_type=F32)
    bcols = lax.dot_general((ri == ci).astype(F32), beta, last_dims, precision=exact, preferred_element_type=F32)
    cols[:, 0:heads] = ccols
    cols[:, heads : 2 * heads] = bcols
    below = ri[:HALF, :HALF] > ci[:HALF, :HALF]
    for j in range(heads):
        i = 0
        for a in range(blocks):
            for b in range(a + 1):
                m = block_decay(ccols[:, j : j + 1], rows[j : j + 1, :], a, b)
                m = m * bcols[a * HALF : (a + 1) * HALF, j : j + 1]
                decays[j, i] = jnp.where(below, m, 0.0) if a == b else m
                i += 1


def conv_weights(weight, g, lanes):
    taps = []
    for i in range(KERNEL):
        tap = weight[i, 0:1, lanes]
        for h in range(1, weight.shape[1]):
            tap = jnp.where(g == h, weight[i, h : h + 1, lanes], tap)
        taps.append(tap)
    return taps


def keys_terms(x, w, cw, cols, rows, decays, s_out, y_out, k_out, padded, *, first, key_heads, ratio):
    toks = x.shape[0] - HALO
    blocks = toks // HALF
    count = key_heads // 2
    heads = key_heads * ratio
    width = DK + ratio * DV
    ri = lax.broadcasted_iota(jnp.int32, (HALF, HALF), 0)
    ci = lax.broadcasted_iota(jnp.int32, (HALF, HALF), 1)
    level = jnp.where(ri > ci, ri ^ ci, 0)
    eye = jnp.where(ri == ci, 1.0, 0.0).astype(F32)
    for g in range(count):
        at = pl.multiple_of(true_index(first + g, key_heads) * width, 128)
        proj = dot(x[...], w[:, pl.ds(at, width)]).astype(BF16).astype(F32)
        for t in range(1 + ratio):
            padded[g * (1 + ratio) + t] = proj[:, t * 128 : (t + 1) * 128]
    kts, rhs, lowers, offs = [], [], [], []
    for g in range(count):
        base = g * (1 + ratio)
        group = true_index(first + g, key_heads)
        k = l2_normed(conv_silu(padded, base, conv_weights(cw, group, slice(DK, 2 * DK)), toks))
        kb = k.astype(BF16)
        k_out[g] = kb
        kf = kb.astype(F32)
        kts.append(kf.T)
        ks = [kb[b * HALF : (b + 1) * HALF] for b in range(blocks)]
        grams = {(a, b): dot_t(ks[a], ks[b]) for a in range(blocks) for b in range(a + 1)}
        for r in range(ratio):
            j = (first + g) * ratio + r
            lanes = slice(2 * DK + r * DV, 2 * DK + (r + 1) * DV)
            v = conv_silu(padded, base + 1 + r, conv_weights(cw, group, lanes), toks)
            ccol = cols[:, j : j + 1]
            bcol = cols[:, heads + j : heads + j + 1]
            rk = (kf * (bcol * jnp.exp(ccol))).astype(BF16)
            rv = (v * bcol).astype(BF16)
            rhs.append(jnp.concatenate([rk, rv], axis=1))
            off, i = {}, 0
            for a in range(blocks):
                for b in range(a + 1):
                    m = grams[(a, b)] * decays[j, i]
                    i += 1
                    if a == b:
                        lowers.append(m)
                    else:
                        off[(a, b)] = m.astype(BF16)
            offs.append(off)
    inv = [eye - jnp.where(level == 1, m, 0.0) for m in lowers]
    size = 2
    while size < HALF:
        here = (level >= size) & (level < 2 * size)
        inv_b = [m.astype(BF16) for m in inv]
        cx = [dot(jnp.where(here, m, 0.0).astype(BF16), x).astype(BF16) for m, x in zip(lowers, inv_b)]
        inv = [x - dot(xb, c) for x, xb, c in zip(inv, inv_b, cx)]
        size *= 2
    inv_b = [m.astype(BF16) for m in inv]
    solved = [[] for _ in rhs]
    for a in range(blocks):
        for j, given in enumerate(rhs):
            r = given[a * HALF : (a + 1) * HALF]
            if a:
                acc = r.astype(F32)
                for b in range(a):
                    acc = acc - dot(offs[j][(a, b)], solved[j][b])
                r = acc.astype(BF16)
            solved[j].append(dot(inv_b[j * blocks + a], r).astype(BF16))
    for j in range(len(rhs)):
        y = jnp.concatenate(solved[j], axis=0)
        y_out[j] = y
        at = first * ratio + j
        crow = rows[at : at + 1, :]
        last = crow[:, toks - 1 : toks]
        kd = (kts[j // ratio] * jnp.exp(last - crow)).astype(BF16)
        s = dot(kd, y)
        s_out[j, :, 0:DK] = (eye * jnp.exp(last) - s[:, 0:DK]).astype(BF16)
        s_out[j, :, DK:] = s[:, DK:].astype(BF16)


def keys_first_kernel(*refs, n_head, key_heads, ratio):
    pieces = refs[:n_head]
    halo, halo_core, w, cw, cols, rows, decays, s_out, y_out, k_out, x_out, padded = refs[n_head:]
    me = lax.axis_index("head")
    part = pieces[0].shape[0]
    direct = (me % 2 == 1) != (me >= n_head - 2)
    x_out[0:HALO, :] = jnp.where(direct, halo[...], halo_core[...])
    for s in range(n_head):
        at = pl.multiple_of(HALO + (me ^ s) * part, 16)
        x_out[pl.ds(at, part), :] = pieces[s][...]
    keys_terms(
        x_out, w, cw, cols, rows, decays, s_out, y_out, k_out, padded, first=0, key_heads=key_heads, ratio=ratio
    )


def keys_second_kernel(x, w, cw, cols, rows, decays, s_out, y_out, k_out, padded, *, key_heads, ratio):
    keys_terms(
        x, w, cw, cols, rows, decays, s_out, y_out, k_out, padded,
        first=key_heads // 2, key_heads=key_heads, ratio=ratio,
    )


def queries_kernel(
    x, wq, wz, cw, cols, rows, keys_a, keys_b, ys_a, ys_b, gain, q_out, o_out, g_out, padded, *, key_heads, ratio
):
    toks = x.shape[0] - HALO
    blocks = toks // HALF
    ri = lax.broadcasted_iota(jnp.int32, (HALF, HALF), 0)
    ci = lax.broadcasted_iota(jnp.int32, (HALF, HALF), 1)
    upto = ri >= ci
    for g in range(key_heads):
        group = true_index(g, key_heads)
        at = pl.multiple_of(group * DK, 128)
        padded[g] = dot(x[...], wq[:, pl.ds(at, DK)]).astype(BF16).astype(F32)
        at = pl.multiple_of(group * ratio * DV, 128)
        proj = dot(x[HALO:, :], wz[:, pl.ds(at, ratio * DV)]).astype(BF16).astype(F32)
        for r in range(ratio):
            z = proj[:, r * DV : (r + 1) * DV]
            g_out[g * ratio + r] = gain[...] * silu(z)
    for g in range(key_heads):
        weights = conv_weights(cw, true_index(g, key_heads), slice(0, DK))
        q = l2_normed(conv_silu(padded, g, weights, toks)) * DK ** (-0.5)
        qb = q.astype(BF16)
        count = key_heads // 2
        kb = keys_b[g - count] if g >= count else keys_a[g]
        grams = {
            (a, b): dot_t(qb[a * HALF : (a + 1) * HALF], kb[b * HALF : (b + 1) * HALF])
            for a in range(blocks)
            for b in range(a + 1)
        }
        for r in range(ratio):
            j = g * ratio + r
            ccol = cols[:, j : j + 1]
            crow = rows[j : j + 1, :]
            ys, i = (ys_b, j - count * ratio) if g >= count else (ys_a, j)
            for a in range(blocks):
                at = slice(a * HALF, (a + 1) * HALF)
                acc = None
                for b in range(a + 1):
                    m = grams[(a, b)] * block_decay(ccol, crow, a, b)
                    if a == b:
                        m = jnp.where(upto, m, 0.0)
                    term = dot(m.astype(BF16), ys[i, b * HALF : (b + 1) * HALF, :])
                    acc = term if acc is None else acc + term
                q_out[j, at, :] = (q[at] * jnp.exp(ccol[at]) - acc[:, 0:DK]).astype(BF16)
                o_out[j, at, :] = acc[:, DK:]


def join_kernel(own, got, out, *, step):
    upper = placed(step)
    for j in range(own.shape[0]):
        mine, other = own[j], got[j]
        later = jnp.where(upper, mine, other)
        earlier = jnp.where(upper, other, mine)
        if out.shape[-1] == DV:
            out[j] = (dot(later[:, 0:DK], earlier[:, DK:]) + later[:, DK:].astype(F32)).astype(BF16)
        else:
            prod = dot(later[:, 0:DK], earlier)
            out[j, :, 0:DK] = prod[:, 0:DK].astype(BF16)
            out[j, :, DK:] = (prod[:, DK:] + later[:, DK:].astype(F32)).astype(BF16)


def prefix_kernel(before, got, out, *, step):
    upper = placed(step)
    for j in range(before.shape[0]):
        prod = dot(before[j, :, 0:DK], got[j])
        prod_t, prod_b = prod[:, 0:DK], prod[:, DK:] + before[j, :, DK:].astype(F32)
        out[j, :, 0:DK] = jnp.where(upper, prod_t.astype(BF16), before[j, :, 0:DK])
        out[j, :, DK:] = jnp.where(upper, prod_b.astype(BF16), before[j, :, DK:])


def states_kernel(own, pair, before, got, keep, send, *, before_step, step):
    odd = placed(1)
    began = placed(before_step)
    upper = placed(step)
    for j in range(own.shape[0]):
        t, b = before[j, :, 0:DK], before[j, :, DK:].astype(F32)
        if before_step == 2:
            last = got[j].astype(F32)
            entered = jnp.where(began, dot(t, got[j]), last)
            b = jnp.where(began, b, 0.0)
        else:
            entered = dot(t, got[j])
        entered = jnp.where(upper, entered, 0.0) + b
        first = jnp.where(odd, pair[j], own[j])
        passed = dot(first[:, 0:DK], entered.astype(BF16)) + first[:, DK:].astype(F32)
        keep[j] = jnp.where(odd, passed, entered).astype(BF16)
        send[j] = jnp.where(odd, entered, passed).astype(BF16)


def normed_kernel(q, o, own, got, gate, keep, send, scratch, *, n_head):
    me = lax.axis_index("head")
    heads = q.shape[0]
    half = heads // 2
    for j in range(heads):
        att = o[j] + dot(q[j], own[j - half] if j >= half else got[j])
        scale = lax.rsqrt(jnp.mean(att * att, axis=-1, keepdims=True) + EPSILON)
        at = pl.multiple_of(true_index(j, heads) * DV, 128)
        scratch[:, pl.ds(at, DV)] = (att * scale * gate[j]).astype(BF16)
    part = scratch.shape[0] // n_head
    for i in range(n_head // 2):
        at = pl.multiple_of((me ^ (2 * i)) * part, 16)
        keep[i * part : (i + 1) * part, :] = scratch[pl.ds(at, part), :]
        at = pl.multiple_of((me ^ (2 * i + 1)) * part, 16)
        send[i * part : (i + 1) * part, :] = scratch[pl.ds(at, part), :]


def out_own_kernel(own, w, *outs):
    part = outs[0].shape[0]
    for i, out in enumerate(outs):
        out[...] = dot(own[i * part : (i + 1) * part, :], w[...])


def out_kernel(got, w, before, out, *, first):
    part = out.shape[0]
    rows = slice(first * part, (first + 1) * part)
    out[...] = (before[...] + dot(got[rows, :], w[...])).astype(out.dtype)


def call(body, out_shape, args, us, scratch=(), any_space=(), **static):
    nbytes = sum(a.size * a.dtype.itemsize for a in args)
    vmem = pl.BlockSpec(memory_space=pltpu.VMEM)
    args = [pltpu.with_memory_space_constraint(a, pltpu.HBM) if i in any_space else a for i, a in enumerate(args)]
    return pl.pallas_call(
        functools.partial(body, **static),
        out_shape=out_shape,
        in_specs=[pl.BlockSpec(memory_space=pltpu.HBM) if i in any_space else vmem for i in range(len(args))],
        out_specs=jax.tree.map(lambda _: vmem, out_shape),
        scratch_shapes=list(scratch),
        compiler_params=pltpu.CompilerParams(vmem_limit_bytes=VMEM_BYTES),
        cost_estimate=pl.CostEstimate(flops=int(us * 1.15e9), bytes_accessed=nbytes, transcendentals=0),
    )(*args)


def shaped(shape, dtype):
    return jax.ShapeDtypeStruct(shape, dtype)


def xor_sent(value, axis, step):
    count = lax.axis_size(axis)
    return lax.ppermute(value, axis, [(i, i ^ step) for i in range(count)])


def passed_along(value, axis, steps):
    count = lax.axis_size(axis)
    return lax.ppermute(value, axis, [(i, i + steps) for i in range(count - steps)])


def local(layer_in, in_proj, conv_weight, gate_logits, norm_gain, out_proj):
    n_head, n_ctx = lax.axis_size("head"), lax.axis_size("ctx")
    width, key_heads, group = in_proj.shape
    heads = gate_logits.shape[1]
    ratio = heads // key_heads
    part = layer_in.shape[0]
    toks = part * n_head
    ctx_head = ("ctx", "head")

    pieces = [layer_in] + [None] * (n_head - 1)
    step = n_head // 2
    while step:
        for s in range(0, n_head, 2 * step):
            pieces[s + step] = xor_sent(pieces[s], "head", step)
        step //= 2
    blocks = toks // HALF
    tail, x_own, logits = call(
        fetch_kernel,
        (shaped((HALO, width), BF16), shaped((part, width), BF16), shaped(gate_logits.shape, F32)),
        [layer_in, gate_logits],
        6.0,
        [pltpu.SemaphoreType.DMA((3,))],
        any_space=(0, 1),
    )
    rows, cols, decays = call(
        gates_kernel,
        (
            shaped((heads, toks), F32),
            shaped((toks, 2 * heads), F32),
            shaped((heads, blocks * (blocks + 1) // 2, HALF, HALF), F32),
        ),
        [logits],
        1.0,
    )
    me = lax.axis_index("head")
    halo = jnp.zeros_like(tail)
    for h in range(n_head - 1, 0, -2):
        target = h if h < n_head - 1 else h - 1
        perm = []
        for c in range(1, n_ctx):
            source, sink = (c - 1) * n_head + n_head - 1, c * n_head + target
            perm += [(source, sink), (sink, source)]
        halo = jnp.where(me == target, lax.ppermute(tail, ctx_head, perm), halo)
    v_end = 2 * DK + ratio * DV
    w_kv = in_proj[:, :, DK:v_end].reshape(width, key_heads * (v_end - DK))
    halo_core = xor_sent(halo, "head", 1)
    w_q = in_proj[:, :, 0:DK].reshape(width, key_heads * DK)
    w_z = in_proj[:, :, v_end:].reshape(width, heads * DV)

    half = heads // 2
    pair_shape = shaped((half, DK, DK + DV), BF16)
    state_shape = shaped((half, DK, DV), BF16)
    key_count = key_heads // 2
    ys_shape = shaped((half, toks, DK + DV), BF16)
    keys_shape = shaped((key_count, toks, DK), BF16)
    padded = pltpu.VMEM((key_count * (1 + ratio), HALO + toks, 128), F32)
    s_send, ys_a, keys_a, x_full = call(
        keys_first_kernel,
        (pair_shape, ys_shape, keys_shape, shaped((HALO + toks, width), BF16)),
        [x_own, *pieces[1:], halo, halo_core, w_kv, conv_weight, cols, rows, decays],
        3.0,
        [padded],
        n_head=n_head,
        key_heads=key_heads,
        ratio=ratio,
    )
    s_pair = xor_sent(s_send, "ctx", 1)
    s_keep, ys_b, keys_b = call(
        keys_second_kernel,
        (pair_shape, ys_shape, keys_shape),
        [x_full, w_kv, conv_weight, cols, rows, decays],
        3.0,
        [padded],
        key_heads=key_heads,
        ratio=ratio,
    )
    w_other = xor_sent(lax.optimization_barrier((out_proj, s_send))[0], "head", 1)
    o_shape = shaped((heads, toks, DV), F32)
    q, o, gate = call(
        queries_kernel,
        (shaped((heads, toks, DK), BF16), o_shape, o_shape),
        [x_full, w_q, w_z, conv_weight, cols, rows, keys_a, keys_b, ys_a, ys_b, norm_gain[None, :]],
        1.9,
        [pltpu.VMEM((key_heads, HALO + toks, 128), F32)],
        key_heads=key_heads,
        ratio=ratio,
    )
    total = call(join_kernel, pair_shape, [s_keep, s_pair], 0.2, step=1)
    step, before, before_step = 2, None, 2
    while 2 * step < n_ctx:
        got = xor_sent(total, "ctx", step)
        more = 4 * step < n_ctx
        total = call(join_kernel, pair_shape if more else state_shape, [total, got], 0.2, step=step)
        if before is None:
            before = got
        else:
            if before_step == 2:
                entry = jnp.concatenate([jnp.eye(DK, dtype=BF16), jnp.zeros((DK, DV), BF16)], axis=1)
                before = jnp.where(lax.axis_index("ctx") // 2 % 2 == 1, before, entry)
                before_step = 1
            before = call(prefix_kernel, pair_shape, [before, got], 0.2, step=step)
        step *= 2
    got = xor_sent(total, "ctx", step)
    own_state, out_state = call(
        states_kernel,
        (state_shape, state_shape),
        [s_keep, s_pair, before, got],
        0.3,
        before_step=before_step,
        step=step,
    )
    got_state = xor_sent(out_state, "ctx", 1)
    rows_shape = shaped((toks // 2, heads * DV), BF16)
    keep, send = call(
        normed_kernel,
        (rows_shape, rows_shape),
        [q, o, own_state, got_state, gate],
        0.4,
        [pltpu.VMEM((toks, heads * DV), BF16)],
        n_head=n_head,
    )
    other = xor_sent(send, "head", 1)
    out_shape = shaped((part, width), F32)
    sums = call(out_own_kernel, (out_shape,) * (n_head // 2), [keep, out_proj], 0.8)
    out = None
    partial = {}
    for i in reversed(range(n_head // 2)):
        shape = out_shape if i == 0 else shaped((part, width), BF16)
        partial[i] = call(out_kernel, shape, [other, w_other, sums[i]], 0.5, first=i)
        if i:
            partial[i] = xor_sent(partial[i], "head", 2 * i)
    for i in range(n_head // 2):
        out = partial[i].astype(F32) if out is None else out + partial[i].astype(F32)
    return out.astype(BF16)


def solution(mesh):
    in_specs = (
        P(("ctx", "head"), None),
        P(None, "head", None),
        P(None, "head", None),
        P(None, "head", "ctx"),
        P(),
        P("head", None),
    )
    out_specs = P(("ctx", "head"), None)
    return jax.shard_map(local, mesh=mesh, in_specs=in_specs, out_specs=out_specs, check_vma=False)
```

```python
import functools

import jax
import jax.numpy as jnp
from jax import lax
from jax.experimental import pallas as pl
from jax.experimental.pallas import tpu as pltpu
from jax.sharding import PartitionSpec as P

DK = 128
DV = 128
KERNEL = 4
HALO = 16
HALF = 128
EPSILON = 1e-06
F32 = jnp.float32
BF16 = jnp.bfloat16
VMEM_BYTES = 24 * 1024 * 1024


def dot(a, b):
    return jnp.dot(a, b, preferred_element_type=F32)


def dot_t(a, b):
    return lax.dot_general(a, b, (((1,), (1,)), ((), ())), preferred_element_type=F32)


def silu(x):
    return x / (1.0 + jnp.exp(-x))


def l2_normed(x):
    return x * lax.rsqrt(jnp.sum(x * x, axis=-1, keepdims=True) + EPSILON)


def conv_silu(padded, slot, weights, rows):
    acc = padded[slot, HALO - KERNEL + 1 : HALO - KERNEL + 1 + rows, :] * weights[0]
    for i in range(1, KERNEL):
        lo = HALO - KERNEL + 1 + i
        acc = acc + padded[slot, lo : lo + rows, :] * weights[i]
    return silu(acc)


def block_decay(ccol, crow, a, b):
    gap = ccol[a * HALF : (a + 1) * HALF] - crow[:, b * HALF : (b + 1) * HALF]
    return jnp.exp(jnp.minimum(gap, 0.0))


def placed(step):
    return lax.axis_index("ctx") // step % 2 == 1


def true_index(local, count):
    half = count // 2
    odd = lax.axis_index("ctx") % 2
    return (1 - odd if local < half else odd) * half + local % half


def fetch_kernel(x_any, logits_any, tail, x_own, logits, sems):
    logits_copy = pltpu.make_async_copy(logits_any, logits, sems.at[2])
    tail_copy = pltpu.make_async_copy(x_any.at[pl.ds(x_any.shape[0] - HALO, HALO), :], tail, sems.at[0])
    own_copy = pltpu.make_async_copy(x_any, x_own, sems.at[1])
    tail_copy.start()
    own_copy.start()
    logits_copy.start()
    tail_copy.wait()
    own_copy.wait()
    logits_copy.wait()


def gates_kernel(logits, rows, cols, decays):
    toks = logits.shape[2]
    blocks = toks // HALF
    half = logits.shape[1] // 2
    given = [logits[i] for i in range(2)]
    given = [jnp.where(placed(1), a, jnp.concatenate([a[half:], a[:half]], axis=0)) for a in given]
    x = given[0]
    log_decay = -(jnp.maximum(x, 0.0) + jnp.log1p(jnp.exp(-jnp.abs(x))))
    beta = 1.0 / (1.0 + jnp.exp(-given[1]))
    heads = x.shape[0]
    ri = lax.broadcasted_iota(jnp.int32, (toks, toks), 0)
    ci = lax.broadcasted_iota(jnp.int32, (toks, toks), 1)
    exact = lax.Precision.HIGHEST
    rows[...] = jnp.dot(log_decay, (ri <= ci).astype(F32), precision=exact, preferred_element_type=F32)
    last_dims = (((1,), (1,)), ((), ()))
    ccols = lax.dot_general((ri >= ci).astype(F32), log_decay, last_dims, precision=exact, preferred_element_type=F32)
    bcols = lax.dot_general((ri == ci).astype(F32), beta, last_dims, precision=exact, preferred_element_type=F32)
    cols[:, 0:heads] = ccols
    cols[:, heads : 2 * heads] = bcols
    below = ri[:HALF, :HALF] > ci[:HALF, :HALF]
    for j in range(heads):
        i = 0
        for a in range(blocks):
            for b in range(a + 1):
                m = block_decay(ccols[:, j : j + 1], rows[j : j + 1, :], a, b)
                m = m * bcols[a * HALF : (a + 1) * HALF, j : j + 1]
                decays[j, i] = jnp.where(below, m, 0.0) if a == b else m
                i += 1


def conv_weights(weight, g, lanes):
    taps = []
    for i in range(KERNEL):
        tap = weight[i, 0:1, lanes]
        for h in range(1, weight.shape[1]):
            tap = jnp.where(g == h, weight[i, h : h + 1, lanes], tap)
        taps.append(tap)
    return taps


def keys_terms(x, w, cw, cols, rows, decays, s_out, y_out, k_out, padded, *, first, key_heads, ratio):
    toks = x.shape[0] - HALO
    blocks = toks // HALF
    count = key_heads // 2
    heads = key_heads * ratio
    width = DK + ratio * DV
    ri = lax.broadcasted_iota(jnp.int32, (HALF, HALF), 0)
    ci = lax.broadcasted_iota(jnp.int32, (HALF, HALF), 1)
    level = jnp.where(ri > ci, ri ^ ci, 0)
    eye = jnp.where(ri == ci, 1.0, 0.0).astype(F32)
    for g in range(count):
        at = pl.multiple_of(true_index(first + g, key_heads) * width, 128)
        proj = dot(x[...], w[:, pl.ds(at, width)]).astype(BF16).astype(F32)
        for t in range(1 + ratio):
            padded[g * (1 + ratio) + t] = proj[:, t * 128 : (t + 1) * 128]
    kts, rhs, lowers, offs = [], [], [], []
    for g in range(count):
        base = g * (1 + ratio)
        group = true_index(first + g, key_heads)
        k = l2_normed(conv_silu(padded, base, conv_weights(cw, group, slice(DK, 2 * DK)), toks))
        kb = k.astype(BF16)
        k_out[g] = kb
        kf = kb.astype(F32)
        kts.append(kf.T)
        ks = [kb[b * HALF : (b + 1) * HALF] for b in range(blocks)]
        grams = {(a, b): dot_t(ks[a], ks[b]) for a in range(blocks) for b in range(a + 1)}
        for r in range(ratio):
            j = (first + g) * ratio + r
            lanes = slice(2 * DK + r * DV, 2 * DK + (r + 1) * DV)
            v = conv_silu(padded, base + 1 + r, conv_weights(cw, group, lanes), toks)
            ccol = cols[:, j : j + 1]
            bcol = cols[:, heads + j : heads + j + 1]
            rk = (kf * (bcol * jnp.exp(ccol))).astype(BF16)
            rv = (v * bcol).astype(BF16)
            rhs.append(jnp.concatenate([rk, rv], axis=1))
            off, i = {}, 0
            for a in range(blocks):
                for b in range(a + 1):
                    m = grams[(a, b)] * decays[j, i]
                    i += 1
                    if a == b:
                        lowers.append(m)
                    else:
                        off[(a, b)] = m.astype(BF16)
            offs.append(off)
    inv = [eye - jnp.where(level == 1, m, 0.0) for m in lowers]
    size = 2
    while size < HALF:
        here = (level >= size) & (level < 2 * size)
        inv_b = [m.astype(BF16) for m in inv]
        cx = [dot(jnp.where(here, m, 0.0).astype(BF16), x).astype(BF16) for m, x in zip(lowers, inv_b)]
        inv = [x - dot(xb, c) for x, xb, c in zip(inv, inv_b, cx)]
        size *= 2
    inv_b = [m.astype(BF16) for m in inv]
    solved = [[] for _ in rhs]
    for a in range(blocks):
        for j, given in enumerate(rhs):
            r = given[a * HALF : (a + 1) * HALF]
            if a:
                acc = r.astype(F32)
                for b in range(a):
                    acc = acc - dot(offs[j][(a, b)], solved[j][b])
                r = acc.astype(BF16)
            solved[j].append(dot(inv_b[j * blocks + a], r).astype(BF16))
    for j in range(len(rhs)):
        y = jnp.concatenate(solved[j], axis=0)
        y_out[j] = y
        at = first * ratio + j
        crow = rows[at : at + 1, :]
        last = crow[:, toks - 1 : toks]
        kd = (kts[j // ratio] * jnp.exp(last - crow)).astype(BF16)
        s = dot(kd, y)
        s_out[j, :, 0:DK] = (eye * jnp.exp(last) - s[:, 0:DK]).astype(BF16)
        s_out[j, :, DK:] = s[:, DK:].astype(BF16)


def keys_first_kernel(*refs, n_head, key_heads, ratio):
    pieces = refs[:n_head]
    halo, halo_core, w, cw, cols, rows, decays, s_out, y_out, k_out, x_out, padded = refs[n_head:]
    me = lax.axis_index("head")
    part = pieces[0].shape[0]
    direct = (me % 2 == 1) != (me >= n_head - 2)
    x_out[0:HALO, :] = jnp.where(direct, halo[...], halo_core[...])
    for s in range(n_head):
        at = pl.multiple_of(HALO + (me ^ s) * part, 16)
        x_out[pl.ds(at, part), :] = pieces[s][...]
    keys_terms(
        x_out, w, cw, cols, rows, decays, s_out, y_out, k_out, padded, first=0, key_heads=key_heads, ratio=ratio
    )


def keys_second_kernel(x, w, cw, cols, rows, decays, s_out, y_out, k_out, padded, *, key_heads, ratio):
    keys_terms(
        x, w, cw, cols, rows, decays, s_out, y_out, k_out, padded,
        first=key_heads // 2, key_heads=key_heads, ratio=ratio,
    )


def queries_kernel(
    x, wq, wz, cw, cols, rows, keys_a, keys_b, ys_a, ys_b, gain, q_out, o_out, g_out, padded, *, key_heads, ratio
):
    toks = x.shape[0] - HALO
    blocks = toks // HALF
    ri = lax.broadcasted_iota(jnp.int32, (HALF, HALF), 0)
    ci = lax.broadcasted_iota(jnp.int32, (HALF, HALF), 1)
    upto = ri >= ci
    for g in range(key_heads):
        group = true_index(g, key_heads)
        at = pl.multiple_of(group * DK, 128)
        padded[g] = dot(x[...], wq[:, pl.ds(at, DK)]).astype(BF16).astype(F32)
        at = pl.multiple_of(group * ratio * DV, 128)
        proj = dot(x[HALO:, :], wz[:, pl.ds(at, ratio * DV)]).astype(BF16).astype(F32)
        for r in range(ratio):
            z = proj[:, r * DV : (r + 1) * DV]
            g_out[g * ratio + r] = gain[...] * silu(z)
    for g in range(key_heads):
        weights = conv_weights(cw, true_index(g, key_heads), slice(0, DK))
        q = l2_normed(conv_silu(padded, g, weights, toks)) * DK ** (-0.5)
        qb = q.astype(BF16)
        count = key_heads // 2
        kb = keys_b[g - count] if g >= count else keys_a[g]
        grams = {
            (a, b): dot_t(qb[a * HALF : (a + 1) * HALF], kb[b * HALF : (b + 1) * HALF])
            for a in range(blocks)
            for b in range(a + 1)
        }
        for r in range(ratio):
            j = g * ratio + r
            ccol = cols[:, j : j + 1]
            crow = rows[j : j + 1, :]
            ys, i = (ys_b, j - count * ratio) if g >= count else (ys_a, j)
            for a in range(blocks):
                at = slice(a * HALF, (a + 1) * HALF)
                acc = None
                for b in range(a + 1):
                    m = grams[(a, b)] * block_decay(ccol, crow, a, b)
                    if a == b:
                        m = jnp.where(upto, m, 0.0)
                    term = dot(m.astype(BF16), ys[i, b * HALF : (b + 1) * HALF, :])
                    acc = term if acc is None else acc + term
                q_out[j, at, :] = (q[at] * jnp.exp(ccol[at]) - acc[:, 0:DK]).astype(BF16)
                o_out[j, at, :] = acc[:, DK:]


def join_kernel(own, got, out, *, step):
    upper = placed(step)
    for j in range(own.shape[0]):
        mine, other = own[j], got[j]
        later = jnp.where(upper, mine, other)
        earlier = jnp.where(upper, other, mine)
        if out.shape[-1] == DV:
            out[j] = (dot(later[:, 0:DK], earlier[:, DK:]) + later[:, DK:].astype(F32)).astype(BF16)
        else:
            prod = dot(later[:, 0:DK], earlier)
            out[j, :, 0:DK] = prod[:, 0:DK].astype(BF16)
            out[j, :, DK:] = (prod[:, DK:] + later[:, DK:].astype(F32)).astype(BF16)


def prefix_kernel(before, got, out, *, step):
    upper = placed(step)
    for j in range(before.shape[0]):
        prod = dot(before[j, :, 0:DK], got[j])
        prod_t, prod_b = prod[:, 0:DK], prod[:, DK:] + before[j, :, DK:].astype(F32)
        out[j, :, 0:DK] = jnp.where(upper, prod_t.astype(BF16), before[j, :, 0:DK])
        out[j, :, DK:] = jnp.where(upper, prod_b.astype(BF16), before[j, :, DK:])


def states_kernel(own, pair, before, got, keep, send, *, before_step, step):
    odd = placed(1)
    began = placed(before_step)
    upper = placed(step)
    for j in range(own.shape[0]):
        t, b = before[j, :, 0:DK], before[j, :, DK:].astype(F32)
        if before_step == 2:
            last = got[j].astype(F32)
            entered = jnp.where(began, dot(t, got[j]), last)
            b = jnp.where(began, b, 0.0)
        else:
            entered = dot(t, got[j])
        entered = jnp.where(upper, entered, 0.0) + b
        first = jnp.where(odd, pair[j], own[j])
        passed = dot(first[:, 0:DK], entered.astype(BF16)) + first[:, DK:].astype(F32)
        keep[j] = jnp.where(odd, passed, entered).astype(BF16)
        send[j] = jnp.where(odd, entered, passed).astype(BF16)


def normed_kernel(q, o, own, got, gate, keep, send, scratch, *, n_head):
    me = lax.axis_index("head")
    heads = q.shape[0]
    half = heads // 2
    for j in range(heads):
        att = o[j] + dot(q[j], own[j - half] if j >= half else got[j])
        scale = lax.rsqrt(jnp.mean(att * att, axis=-1, keepdims=True) + EPSILON)
        at = pl.multiple_of(true_index(j, heads) * DV, 128)
        scratch[:, pl.ds(at, DV)] = (att * scale * gate[j]).astype(BF16)
    part = scratch.shape[0] // n_head
    for i in range(n_head // 2):
        at = pl.multiple_of((me ^ (2 * i)) * part, 16)
        keep[i * part : (i + 1) * part, :] = scratch[pl.ds(at, part), :]
        at = pl.multiple_of((me ^ (2 * i + 1)) * part, 16)
        send[i * part : (i + 1) * part, :] = scratch[pl.ds(at, part), :]


def early_kernel(keep, send, w, out):
    even = lax.axis_index("head") % 2 == 0
    part = keep.shape[0] - out.shape[0]
    out[...] = dot(jnp.where(even, keep[part:, :], send[part:, :]), w[...]).astype(BF16)


def out_own_kernel(own, w, *outs):
    part = outs[0].shape[0]
    for i, out in enumerate(outs):
        out[...] = dot(own[i * part : (i + 1) * part, :], w[...])


def out_kernel(got, w, before, out, *, first):
    part = out.shape[0]
    rows = slice(first * part, (first + 1) * part)
    out[...] = (before[...] + dot(got[rows, :], w[...])).astype(out.dtype)


def total_kernel(*refs):
    even = lax.axis_index("head") % 2 == 0
    count = (len(refs) - 2) // 3
    acc = refs[0][...]
    for i in range(count):
        mine, passed, late = (refs[1 + i + t * count][...].astype(F32) for t in range(3))
        acc = acc + jnp.where(even, mine + passed, late)
    refs[-1][...] = acc.astype(BF16)


def call(body, out_shape, args, us, scratch=(), any_space=(), **static):
    nbytes = sum(a.size * a.dtype.itemsize for a in args)
    vmem = pl.BlockSpec(memory_space=pltpu.VMEM)
    args = [pltpu.with_memory_space_constraint(a, pltpu.HBM) if i in any_space else a for i, a in enumerate(args)]
    return pl.pallas_call(
        functools.partial(body, **static),
        out_shape=out_shape,
        in_specs=[pl.BlockSpec(memory_space=pltpu.HBM) if i in any_space else vmem for i in range(len(args))],
        out_specs=jax.tree.map(lambda _: vmem, out_shape),
        scratch_shapes=list(scratch),
        compiler_params=pltpu.CompilerParams(vmem_limit_bytes=VMEM_BYTES),
        cost_estimate=pl.CostEstimate(flops=int(us * 1.15e9), bytes_accessed=nbytes, transcendentals=0),
    )(*args)


def shaped(shape, dtype):
    return jax.ShapeDtypeStruct(shape, dtype)


def xor_sent(value, axis, step):
    count = lax.axis_size(axis)
    return lax.ppermute(value, axis, [(i, i ^ step) for i in range(count)])


def halo_pairs(n_ctx, n_head, target):
    source = n_head - 1
    pairs = [((c - 1, source), (c, target)) for c in range(1, n_ctx)]
    spare = [h for h in range(n_head) if h not in (source, target)]
    if n_ctx % 4 == 0 and len(spare) == 2:
        a, b = spare
        pairs += [((0, target), (0, a)), ((n_ctx - 1, source), (n_ctx - 1, b)), ((1, a), (1, b)), ((0, b), (2, b))]
        pairs += [((c, a), (c + 1, a)) for c in range(2, n_ctx, 2)]
        pairs += [((c + i, b), (c + i + 2, b)) for c in range(3, n_ctx - 1, 4) for i in range(2)]
    flat = [(c * n_head + h, d * n_head + k) for (c, h), (d, k) in pairs]
    return sorted(flat + [(d, c) for c, d in flat])


def local(layer_in, in_proj, conv_weight, gate_logits, norm_gain, out_proj):
    n_head, n_ctx = lax.axis_size("head"), lax.axis_size("ctx")
    width, key_heads, group = in_proj.shape
    heads = gate_logits.shape[1]
    ratio = heads // key_heads
    part = layer_in.shape[0]
    toks = part * n_head
    ctx_head = ("ctx", "head")

    pieces = [layer_in] + [None] * (n_head - 1)
    step = n_head // 2
    while step:
        for s in range(0, n_head, 2 * step):
            pieces[s + step] = xor_sent(pieces[s], "head", step)
        step //= 2
    blocks = toks // HALF
    tail, x_own, logits = call(
        fetch_kernel,
        (shaped((HALO, width), BF16), shaped((part, width), BF16), shaped(gate_logits.shape, F32)),
        [layer_in, gate_logits],
        6.0,
        [pltpu.SemaphoreType.DMA((3,))],
        any_space=(0, 1),
    )
    rows, cols, decays = call(
        gates_kernel,
        (
            shaped((heads, toks), F32),
            shaped((toks, 2 * heads), F32),
            shaped((heads, blocks * (blocks + 1) // 2, HALF, HALF), F32),
        ),
        [logits],
        1.0,
    )
    me = lax.axis_index("head")
    halo = jnp.zeros_like(tail)
    for h in range(n_head - 1, 0, -2):
        target = h if h < n_head - 1 else h - 1
        wanted = (me == target) & (lax.axis_index("ctx") > 0)
        halo = jnp.where(wanted, lax.ppermute(tail, ctx_head, halo_pairs(n_ctx, n_head, target)), halo)
    v_end = 2 * DK + ratio * DV
    w_kv = in_proj[:, :, DK:v_end].reshape(width, key_heads * (v_end - DK))
    halo_core = xor_sent(halo, "head", 1)
    w_q = in_proj[:, :, 0:DK].reshape(width, key_heads * DK)
    w_z = in_proj[:, :, v_end:].reshape(width, heads * DV)

    half = heads // 2
    pair_shape = shaped((half, DK, DK + DV), BF16)
    state_shape = shaped((half, DK, DV), BF16)
    key_count = key_heads // 2
    ys_shape = shaped((half, toks, DK + DV), BF16)
    keys_shape = shaped((key_count, toks, DK), BF16)
    padded = pltpu.VMEM((key_count * (1 + ratio), HALO + toks, 128), F32)
    s_send, ys_a, keys_a, x_full = call(
        keys_first_kernel,
        (pair_shape, ys_shape, keys_shape, shaped((HALO + toks, width), BF16)),
        [x_own, *pieces[1:], halo, halo_core, w_kv, conv_weight, cols, rows, decays],
        3.0,
        [padded],
        n_head=n_head,
        key_heads=key_heads,
        ratio=ratio,
    )
    s_pair = xor_sent(s_send, "ctx", 1)
    s_keep, ys_b, keys_b = call(
        keys_second_kernel,
        (pair_shape, ys_shape, keys_shape),
        [x_full, w_kv, conv_weight, cols, rows, decays],
        3.0,
        [padded],
        key_heads=key_heads,
        ratio=ratio,
    )
    w_other = xor_sent(lax.optimization_barrier((out_proj, s_send))[0], "head", 1)
    o_shape = shaped((heads, toks, DV), F32)
    q, o, gate = call(
        queries_kernel,
        (shaped((heads, toks, DK), BF16), o_shape, o_shape),
        [x_full, w_q, w_z, conv_weight, cols, rows, keys_a, keys_b, ys_a, ys_b, norm_gain[None, :]],
        1.9,
        [pltpu.VMEM((key_heads, HALO + toks, 128), F32)],
        key_heads=key_heads,
        ratio=ratio,
    )
    total = call(join_kernel, pair_shape, [s_keep, s_pair], 0.2, step=1)
    step, before, before_step = 2, None, 2
    while 2 * step < n_ctx:
        got = xor_sent(total, "ctx", step)
        more = 4 * step < n_ctx
        total = call(join_kernel, pair_shape if more else state_shape, [total, got], 0.2, step=step)
        if before is None:
            before = got
        else:
            if before_step == 2:
                entry = jnp.concatenate([jnp.eye(DK, dtype=BF16), jnp.zeros((DK, DV), BF16)], axis=1)
                before = jnp.where(lax.axis_index("ctx") // 2 % 2 == 1, before, entry)
                before_step = 1
            before = call(prefix_kernel, pair_shape, [before, got], 0.2, step=step)
        step *= 2
    got = xor_sent(total, "ctx", step)
    own_state, out_state = call(
        states_kernel,
        (state_shape, state_shape),
        [s_keep, s_pair, before, got],
        0.3,
        before_step=before_step,
        step=step,
    )
    got_state = xor_sent(out_state, "ctx", 1)
    rows_shape = shaped((toks // 2, heads * DV), BF16)
    keep, send = call(
        normed_kernel,
        (rows_shape, rows_shape),
        [q, o, own_state, got_state, gate],
        0.4,
        [pltpu.VMEM((toks, heads * DV), BF16)],
        n_head=n_head,
    )
    other = xor_sent(send, "head", 1)
    early = call(early_kernel, shaped((toks // 2 - part, width), BF16), [keep, send, out_proj], 0.4)
    early_got = [
        xor_sent(early[(i - 1) * part : i * part], "head", 2 * i) for i in range(1, n_head // 2)
    ]
    out_shape = shaped((part, width), F32)
    sums = call(out_own_kernel, (out_shape,) * (n_head // 2), [keep, out_proj], 0.8)
    late_got = []
    for i in range(1, n_head // 2):
        late = call(out_kernel, shaped((part, width), BF16), [other, w_other, sums[i]], 0.5, first=i)
        late_perm = [
            (c * n_head + h, c * n_head + (h ^ (2 * i)) if h % 2 else (c ^ 1) * n_head + h)
            for c in range(n_ctx)
            for h in range(n_head)
        ]
        late_got.append(lax.ppermute(late, ctx_head, late_perm))
    out = call(out_kernel, out_shape, [other, w_other, sums[0]], 0.5, first=0)
    out, *early_got = lax.optimization_barrier((out, *early_got))
    passed = [xor_sent(mine, "head", 1) for mine in early_got]
    return call(total_kernel, shaped((part, width), BF16), [out, *early_got, *passed, *late_got], 0.5)


def solution(mesh):
    in_specs = (
        P(("ctx", "head"), None),
        P(None, "head", None),
        P(None, "head", None),
        P(None, "head", "ctx"),
        P(),
        P("head", None),
    )
    out_specs = P(("ctx", "head"), None)
    return jax.shard_map(local, mesh=mesh, in_specs=in_specs, out_specs=out_specs, check_vma=False)
```

```python
import functools

import jax
import jax.numpy as jnp
from jax import lax
from jax.experimental import pallas as pl
from jax.experimental.pallas import tpu as pltpu
from jax.sharding import PartitionSpec as P

DK = 128
DV = 128
KERNEL = 4
HALO = 16
HALF = 128
EPSILON = 1e-06
F32 = jnp.float32
BF16 = jnp.bfloat16
VMEM_BYTES = 24 * 1024 * 1024


def dot(a, b):
    return jnp.dot(a, b, preferred_element_type=F32)


def dot_t(a, b):
    return lax.dot_general(a, b, (((1,), (1,)), ((), ())), preferred_element_type=F32)


def silu(x):
    return x / (1.0 + jnp.exp(-x))


def l2_normed(x):
    return x * lax.rsqrt(jnp.sum(x * x, axis=-1, keepdims=True) + EPSILON)


def conv_silu(padded, slot, weights, rows):
    acc = padded[slot, HALO - KERNEL + 1 : HALO - KERNEL + 1 + rows, :] * weights[0]
    for i in range(1, KERNEL):
        lo = HALO - KERNEL + 1 + i
        acc = acc + padded[slot, lo : lo + rows, :] * weights[i]
    return silu(acc)


def block_decay(ccol, crow, a, b):
    gap = ccol[a * HALF : (a + 1) * HALF] - crow[:, b * HALF : (b + 1) * HALF]
    return jnp.exp(jnp.minimum(gap, 0.0))


def placed(step):
    return lax.axis_index("ctx") // step % 2 == 1


def true_index(local, count):
    half = count // 2
    odd = lax.axis_index("ctx") % 2
    return (1 - odd if local < half else odd) * half + local % half


def fetch_kernel(x_any, logits_any, packed, x_own, logits, tail, rows, sems):
    logits_copy = pltpu.make_async_copy(logits_any, logits, sems.at[2])
    tail_copy = pltpu.make_async_copy(x_any.at[pl.ds(x_any.shape[0] - HALO, HALO), :], tail, sems.at[0])
    own_copy = pltpu.make_async_copy(x_any, x_own, sems.at[1])
    tail_copy.start()
    own_copy.start()
    logits_copy.start()
    tail_copy.wait()
    width = tail.shape[1]
    last = tail[...].astype(F32)
    taps = KERNEL - 1
    for r in range(taps):
        for t in range(width // 128):
            at = r * (width // 128) + t
            rows[at : at + 1, :] = last[HALO - taps + r : HALO - taps + r + 1, t * 128 : (t + 1) * 128]
    packed[...] = rows[...].astype(BF16)
    own_copy.wait()
    logits_copy.wait()


def gates_kernel(logits, rows, cols, decays):
    toks = logits.shape[2]
    blocks = toks // HALF
    half = logits.shape[1] // 2
    given = [logits[i] for i in range(2)]
    given = [jnp.where(placed(1), a, jnp.concatenate([a[half:], a[:half]], axis=0)) for a in given]
    x = given[0]
    log_decay = -(jnp.maximum(x, 0.0) + jnp.log1p(jnp.exp(-jnp.abs(x))))
    beta = 1.0 / (1.0 + jnp.exp(-given[1]))
    heads = x.shape[0]
    ri = lax.broadcasted_iota(jnp.int32, (toks, toks), 0)
    ci = lax.broadcasted_iota(jnp.int32, (toks, toks), 1)
    exact = lax.Precision.HIGHEST
    rows[...] = jnp.dot(log_decay, (ri <= ci).astype(F32), precision=exact, preferred_element_type=F32)
    last_dims = (((1,), (1,)), ((), ()))
    ccols = lax.dot_general((ri >= ci).astype(F32), log_decay, last_dims, precision=exact, preferred_element_type=F32)
    bcols = lax.dot_general((ri == ci).astype(F32), beta, last_dims, precision=exact, preferred_element_type=F32)
    cols[:, 0:heads] = ccols
    cols[:, heads : 2 * heads] = bcols
    below = ri[:HALF, :HALF] > ci[:HALF, :HALF]
    for j in range(heads):
        i = 0
        for a in range(blocks):
            for b in range(a + 1):
                m = block_decay(ccols[:, j : j + 1], rows[j : j + 1, :], a, b)
                m = m * bcols[a * HALF : (a + 1) * HALF, j : j + 1]
                decays[j, i] = jnp.where(below, m, 0.0) if a == b else m
                i += 1


def conv_weights(weight, g, lanes):
    taps = []
    for i in range(KERNEL):
        tap = weight[i, 0:1, lanes]
        for h in range(1, weight.shape[1]):
            tap = jnp.where(g == h, weight[i, h : h + 1, lanes], tap)
        taps.append(tap)
    return taps


def keys_terms(x, w, cw, cols, rows, decays, s_out, y_out, k_out, padded, *, first, key_heads, ratio):
    toks = x.shape[0] - HALO
    blocks = toks // HALF
    count = key_heads // 2
    heads = key_heads * ratio
    width = DK + ratio * DV
    ri = lax.broadcasted_iota(jnp.int32, (HALF, HALF), 0)
    ci = lax.broadcasted_iota(jnp.int32, (HALF, HALF), 1)
    level = jnp.where(ri > ci, ri ^ ci, 0)
    eye = jnp.where(ri == ci, 1.0, 0.0).astype(F32)
    for g in range(count):
        at = pl.multiple_of(true_index(first + g, key_heads) * width, 128)
        proj = dot(x[...], w[:, pl.ds(at, width)]).astype(BF16).astype(F32)
        for t in range(1 + ratio):
            padded[g * (1 + ratio) + t] = proj[:, t * 128 : (t + 1) * 128]
    kts, rhs, lowers, offs = [], [], [], []
    for g in range(count):
        base = g * (1 + ratio)
        group = true_index(first + g, key_heads)
        k = l2_normed(conv_silu(padded, base, conv_weights(cw, group, slice(DK, 2 * DK)), toks))
        kb = k.astype(BF16)
        k_out[g] = kb
        kf = kb.astype(F32)
        kts.append(kf.T)
        ks = [kb[b * HALF : (b + 1) * HALF] for b in range(blocks)]
        grams = {(a, b): dot_t(ks[a], ks[b]) for a in range(blocks) for b in range(a + 1)}
        for r in range(ratio):
            j = (first + g) * ratio + r
            lanes = slice(2 * DK + r * DV, 2 * DK + (r + 1) * DV)
            v = conv_silu(padded, base + 1 + r, conv_weights(cw, group, lanes), toks)
            ccol = cols[:, j : j + 1]
            bcol = cols[:, heads + j : heads + j + 1]
            rk = (kf * (bcol * jnp.exp(ccol))).astype(BF16)
            rv = (v * bcol).astype(BF16)
            rhs.append(jnp.concatenate([rk, rv], axis=1))
            off, i = {}, 0
            for a in range(blocks):
                for b in range(a + 1):
                    m = grams[(a, b)] * decays[j, i]
                    i += 1
                    if a == b:
                        lowers.append(m)
                    else:
                        off[(a, b)] = m.astype(BF16)
            offs.append(off)
    inv = [eye - jnp.where(level == 1, m, 0.0) for m in lowers]
    size = 2
    while size < HALF:
        here = (level >= size) & (level < 2 * size)
        inv_b = [m.astype(BF16) for m in inv]
        cx = [dot(jnp.where(here, m, 0.0).astype(BF16), x).astype(BF16) for m, x in zip(lowers, inv_b)]
        inv = [x - dot(xb, c) for x, xb, c in zip(inv, inv_b, cx)]
        size *= 2
    inv_b = [m.astype(BF16) for m in inv]
    solved = [[] for _ in rhs]
    for a in range(blocks):
        for j, given in enumerate(rhs):
            r = given[a * HALF : (a + 1) * HALF]
            if a:
                acc = r.astype(F32)
                for b in range(a):
                    acc = acc - dot(offs[j][(a, b)], solved[j][b])
                r = acc.astype(BF16)
            solved[j].append(dot(inv_b[j * blocks + a], r).astype(BF16))
    for j in range(len(rhs)):
        y = jnp.concatenate(solved[j], axis=0)
        y_out[j] = y
        at = first * ratio + j
        crow = rows[at : at + 1, :]
        last = crow[:, toks - 1 : toks]
        kd = (kts[j // ratio] * jnp.exp(last - crow)).astype(BF16)
        s = dot(kd, y)
        s_out[j, :, 0:DK] = (eye * jnp.exp(last) - s[:, 0:DK]).astype(BF16)
        s_out[j, :, DK:] = s[:, DK:].astype(BF16)


def keys_first_kernel(*refs, n_head, key_heads, ratio):
    pieces = refs[:n_head]
    halo, halo_core, w, cw, cols, rows, decays, s_out, y_out, k_out, x_out, padded, halo_rows = refs[n_head:]
    me = lax.axis_index("head")
    part = pieces[0].shape[0]
    direct = (me % 2 == 1) != (me >= n_head - 2)
    given = jnp.where(direct, halo[...].astype(F32), halo_core[...].astype(F32))
    taps, tiles = KERNEL - 1, x_out.shape[1] // 128
    halo_rows[...] = jnp.zeros_like(halo_rows)
    for r in range(taps):
        for t in range(tiles):
            at = HALO - taps + r
            halo_rows[at : at + 1, t * 128 : (t + 1) * 128] = given[r * tiles + t : r * tiles + t + 1, :]
    x_out[0:HALO, :] = halo_rows[...].astype(BF16)
    for s in range(n_head):
        at = pl.multiple_of(HALO + (me ^ s) * part, 16)
        x_out[pl.ds(at, part), :] = pieces[s][...]
    keys_terms(
        x_out, w, cw, cols, rows, decays, s_out, y_out, k_out, padded, first=0, key_heads=key_heads, ratio=ratio
    )


def keys_second_kernel(x, w, cw, cols, rows, decays, s_out, y_out, k_out, padded, *, key_heads, ratio):
    keys_terms(
        x, w, cw, cols, rows, decays, s_out, y_out, k_out, padded,
        first=key_heads // 2, key_heads=key_heads, ratio=ratio,
    )


def queries_kernel(
    x, wq, wz, cw, cols, rows, keys_a, keys_b, ys_a, ys_b, gain, q_out, o_out, g_out, padded, *, key_heads, ratio
):
    toks = x.shape[0] - HALO
    blocks = toks // HALF
    ri = lax.broadcasted_iota(jnp.int32, (HALF, HALF), 0)
    ci = lax.broadcasted_iota(jnp.int32, (HALF, HALF), 1)
    upto = ri >= ci
    for g in range(key_heads):
        group = true_index(g, key_heads)
        at = pl.multiple_of(group * DK, 128)
        padded[g] = dot(x[...], wq[:, pl.ds(at, DK)]).astype(BF16).astype(F32)
        at = pl.multiple_of(group * ratio * DV, 128)
        proj = dot(x[HALO:, :], wz[:, pl.ds(at, ratio * DV)]).astype(BF16).astype(F32)
        for r in range(ratio):
            z = proj[:, r * DV : (r + 1) * DV]
            g_out[g * ratio + r] = gain[...] * silu(z)
    for g in range(key_heads):
        weights = conv_weights(cw, true_index(g, key_heads), slice(0, DK))
        q = l2_normed(conv_silu(padded, g, weights, toks)) * DK ** (-0.5)
        qb = q.astype(BF16)
        count = key_heads // 2
        kb = keys_b[g - count] if g >= count else keys_a[g]
        grams = {
            (a, b): dot_t(qb[a * HALF : (a + 1) * HALF], kb[b * HALF : (b + 1) * HALF])
            for a in range(blocks)
            for b in range(a + 1)
        }
        for r in range(ratio):
            j = g * ratio + r
            ccol = cols[:, j : j + 1]
            crow = rows[j : j + 1, :]
            ys, i = (ys_b, j - count * ratio) if g >= count else (ys_a, j)
            for a in range(blocks):
                at = slice(a * HALF, (a + 1) * HALF)
                acc = None
                for b in range(a + 1):
                    m = grams[(a, b)] * block_decay(ccol, crow, a, b)
                    if a == b:
                        m = jnp.where(upto, m, 0.0)
                    term = dot(m.astype(BF16), ys[i, b * HALF : (b + 1) * HALF, :])
                    acc = term if acc is None else acc + term
                q_out[j, at, :] = (q[at] * jnp.exp(ccol[at]) - acc[:, 0:DK]).astype(BF16)
                o_out[j, at, :] = acc[:, DK:]


def join_kernel(own, got, out, *, step):
    upper = placed(step)
    for j in range(own.shape[0]):
        mine, other = own[j], got[j]
        later = jnp.where(upper, mine, other)
        earlier = jnp.where(upper, other, mine)
        if out.shape[-1] == DV:
            out[j] = (dot(later[:, 0:DK], earlier[:, DK:]) + later[:, DK:].astype(F32)).astype(BF16)
        else:
            prod = dot(later[:, 0:DK], earlier)
            out[j, :, 0:DK] = prod[:, 0:DK].astype(BF16)
            out[j, :, DK:] = (prod[:, DK:] + later[:, DK:].astype(F32)).astype(BF16)


def prefix_kernel(before, got, out, *, step):
    upper = placed(step)
    for j in range(before.shape[0]):
        prod = dot(before[j, :, 0:DK], got[j])
        prod_t, prod_b = prod[:, 0:DK], prod[:, DK:] + before[j, :, DK:].astype(F32)
        out[j, :, 0:DK] = jnp.where(upper, prod_t.astype(BF16), before[j, :, 0:DK])
        out[j, :, DK:] = jnp.where(upper, prod_b.astype(BF16), before[j, :, DK:])


def states_kernel(own, pair, before, got, keep, send, *, before_step, step):
    odd = placed(1)
    began = placed(before_step)
    upper = placed(step)
    for j in range(own.shape[0]):
        t, b = before[j, :, 0:DK], before[j, :, DK:].astype(F32)
        if before_step == 2:
            last = got[j].astype(F32)
            entered = jnp.where(began, dot(t, got[j]), last)
            b = jnp.where(began, b, 0.0)
        else:
            entered = dot(t, got[j])
        entered = jnp.where(upper, entered, 0.0) + b
        first = jnp.where(odd, pair[j], own[j])
        passed = dot(first[:, 0:DK], entered.astype(BF16)) + first[:, DK:].astype(F32)
        keep[j] = jnp.where(odd, passed, entered).astype(BF16)
        send[j] = jnp.where(odd, entered, passed).astype(BF16)


def normed_kernel(q, o, own, got, gate, keep, send, scratch, *, n_head):
    me = lax.axis_index("head")
    heads = q.shape[0]
    half = heads // 2
    for j in range(heads):
        att = o[j] + dot(q[j], own[j - half] if j >= half else got[j])
        scale = lax.rsqrt(jnp.mean(att * att, axis=-1, keepdims=True) + EPSILON)
        at = pl.multiple_of(true_index(j, heads) * DV, 128)
        scratch[:, pl.ds(at, DV)] = (att * scale * gate[j]).astype(BF16)
    part = scratch.shape[0] // n_head
    for i in range(n_head // 2):
        at = pl.multiple_of((me ^ (2 * i)) * part, 16)
        keep[i * part : (i + 1) * part, :] = scratch[pl.ds(at, part), :]
        at = pl.multiple_of((me ^ (2 * i + 1)) * part, 16)
        send[i * part : (i + 1) * part, :] = scratch[pl.ds(at, part), :]


def early_kernel(keep, send, w, out):
    even = lax.axis_index("head") % 2 == 0
    part = keep.shape[0] - out.shape[0]
    out[...] = dot(jnp.where(even, keep[part:, :], send[part:, :]), w[...]).astype(BF16)


def out_own_kernel(own, w, *outs):
    part = outs[0].shape[0]
    for i, out in enumerate(outs):
        out[...] = dot(own[i * part : (i + 1) * part, :], w[...])


def out_kernel(got, w, before, out, *, first):
    part = out.shape[0]
    rows = slice(first * part, (first + 1) * part)
    out[...] = (before[...] + dot(got[rows, :], w[...])).astype(out.dtype)


def total_kernel(*refs):
    even = lax.axis_index("head") % 2 == 0
    count = (len(refs) - 2) // 3
    acc = refs[0][...]
    for i in range(count):
        mine, passed, late = (refs[1 + i + t * count][...].astype(F32) for t in range(3))
        acc = acc + jnp.where(even, mine + passed, late)
    refs[-1][...] = acc.astype(BF16)


def call(body, out_shape, args, us, scratch=(), any_space=(), **static):
    nbytes = sum(a.size * a.dtype.itemsize for a in args)
    vmem = pl.BlockSpec(memory_space=pltpu.VMEM)
    args = [pltpu.with_memory_space_constraint(a, pltpu.HBM) if i in any_space else a for i, a in enumerate(args)]
    return pl.pallas_call(
        functools.partial(body, **static),
        out_shape=out_shape,
        in_specs=[pl.BlockSpec(memory_space=pltpu.HBM) if i in any_space else vmem for i in range(len(args))],
        out_specs=jax.tree.map(lambda _: vmem, out_shape),
        scratch_shapes=list(scratch),
        compiler_params=pltpu.CompilerParams(vmem_limit_bytes=VMEM_BYTES),
        cost_estimate=pl.CostEstimate(flops=int(us * 1.15e9), bytes_accessed=nbytes, transcendentals=0),
    )(*args)


def shaped(shape, dtype):
    return jax.ShapeDtypeStruct(shape, dtype)


def xor_sent(value, axis, step):
    count = lax.axis_size(axis)
    return lax.ppermute(value, axis, [(i, i ^ step) for i in range(count)])


def halo_pairs(n_ctx, n_head, target):
    source = n_head - 1
    pairs = [((c - 1, source), (c, target)) for c in range(1, n_ctx)]
    spare = [h for h in range(n_head) if h not in (source, target)]
    if n_ctx % 4 == 0 and len(spare) == 2:
        a, b = spare
        pairs += [((0, target), (0, a)), ((n_ctx - 1, source), (n_ctx - 1, b)), ((1, a), (1, b)), ((0, b), (2, b))]
        pairs += [((c, a), (c + 1, a)) for c in range(2, n_ctx, 2)]
        pairs += [((c + i, b), (c + i + 2, b)) for c in range(3, n_ctx - 1, 4) for i in range(2)]
    flat = [(c * n_head + h, d * n_head + k) for (c, h), (d, k) in pairs]
    return sorted(flat + [(d, c) for c, d in flat])


def local(layer_in, in_proj, conv_weight, gate_logits, norm_gain, out_proj):
    n_head, n_ctx = lax.axis_size("head"), lax.axis_size("ctx")
    width, key_heads, group = in_proj.shape
    heads = gate_logits.shape[1]
    ratio = heads // key_heads
    part = layer_in.shape[0]
    toks = part * n_head
    ctx_head = ("ctx", "head")

    pieces = [layer_in] + [None] * (n_head - 1)
    step = n_head // 2
    while step:
        for s in range(0, n_head, 2 * step):
            pieces[s + step] = xor_sent(pieces[s], "head", step)
        step //= 2
    blocks = toks // HALF
    packed_shape = shaped(((KERNEL - 1) * (width // 128), 128), BF16)
    tail, x_own, logits = call(
        fetch_kernel,
        (packed_shape, shaped((part, width), BF16), shaped(gate_logits.shape, F32)),
        [layer_in, gate_logits],
        6.0,
        [pltpu.VMEM((HALO, width), BF16), pltpu.VMEM(packed_shape.shape, F32), pltpu.SemaphoreType.DMA((3,))],
        any_space=(0, 1),
    )
    rows, cols, decays = call(
        gates_kernel,
        (
            shaped((heads, toks), F32),
            shaped((toks, 2 * heads), F32),
            shaped((heads, blocks * (blocks + 1) // 2, HALF, HALF), F32),
        ),
        [logits],
        1.0,
    )
    me = lax.axis_index("head")
    halo = jnp.zeros_like(tail)
    for h in range(n_head - 1, 0, -2):
        target = h if h < n_head - 1 else h - 1
        wanted = (me == target) & (lax.axis_index("ctx") > 0)
        halo = jnp.where(wanted, lax.ppermute(tail, ctx_head, halo_pairs(n_ctx, n_head, target)), halo)
    v_end = 2 * DK + ratio * DV
    w_kv = in_proj[:, :, DK:v_end].reshape(width, key_heads * (v_end - DK))
    halo, w_kv = lax.optimization_barrier((halo, w_kv))
    halo_core = xor_sent(halo, "head", 1)
    w_q = in_proj[:, :, 0:DK].reshape(width, key_heads * DK)
    w_z = in_proj[:, :, v_end:].reshape(width, heads * DV)

    half = heads // 2
    pair_shape = shaped((half, DK, DK + DV), BF16)
    state_shape = shaped((half, DK, DV), BF16)
    key_count = key_heads // 2
    ys_shape = shaped((half, toks, DK + DV), BF16)
    keys_shape = shaped((key_count, toks, DK), BF16)
    padded = pltpu.VMEM((key_count * (1 + ratio), HALO + toks, 128), F32)
    s_send, ys_a, keys_a, x_full = call(
        keys_first_kernel,
        (pair_shape, ys_shape, keys_shape, shaped((HALO + toks, width), BF16)),
        [x_own, *pieces[1:], halo, halo_core, w_kv, conv_weight, cols, rows, decays],
        3.0,
        [padded, pltpu.VMEM((HALO, width), F32)],
        n_head=n_head,
        key_heads=key_heads,
        ratio=ratio,
    )
    s_pair = xor_sent(s_send, "ctx", 1)
    s_keep, ys_b, keys_b = call(
        keys_second_kernel,
        (pair_shape, ys_shape, keys_shape),
        [x_full, w_kv, conv_weight, cols, rows, decays],
        3.0,
        [padded],
        key_heads=key_heads,
        ratio=ratio,
    )
    w_other = xor_sent(lax.optimization_barrier((out_proj, s_send))[0], "head", 1)
    total = call(join_kernel, pair_shape, [s_keep, s_pair], 0.2, step=1)
    step, before, before_step = 2, None, 2
    while 2 * step < n_ctx:
        got = xor_sent(total, "ctx", step)
        if step == 2:
            got, w_q, w_z = lax.optimization_barrier((got, w_q, w_z))
        more = 4 * step < n_ctx
        total = call(join_kernel, pair_shape if more else state_shape, [total, got], 0.2, step=step)
        if before is None:
            before = got
        else:
            if before_step == 2:
                entry = jnp.concatenate([jnp.eye(DK, dtype=BF16), jnp.zeros((DK, DV), BF16)], axis=1)
                before = jnp.where(lax.axis_index("ctx") // 2 % 2 == 1, before, entry)
                before_step = 1
            before = call(prefix_kernel, pair_shape, [before, got], 0.2, step=step)
        step *= 2
    got = xor_sent(total, "ctx", step)
    own_state, out_state = call(
        states_kernel,
        (state_shape, state_shape),
        [s_keep, s_pair, before, got],
        0.3,
        before_step=before_step,
        step=step,
    )
    got_state = xor_sent(out_state, "ctx", 1)
    o_shape = shaped((heads, toks, DV), F32)
    q, o, gate = call(
        queries_kernel,
        (shaped((heads, toks, DK), BF16), o_shape, o_shape),
        [x_full, w_q, w_z, conv_weight, cols, rows, keys_a, keys_b, ys_a, ys_b, norm_gain[None, :]],
        1.9,
        [pltpu.VMEM((key_heads, HALO + toks, 128), F32)],
        key_heads=key_heads,
        ratio=ratio,
    )
    rows_shape = shaped((toks // 2, heads * DV), BF16)
    keep, send = call(
        normed_kernel,
        (rows_shape, rows_shape),
        [q, o, own_state, got_state, gate],
        0.4,
        [pltpu.VMEM((toks, heads * DV), BF16)],
        n_head=n_head,
    )
    other = xor_sent(send, "head", 1)
    early = call(early_kernel, shaped((toks // 2 - part, width), BF16), [keep, send, out_proj], 0.4)
    early_got = [
        xor_sent(early[(i - 1) * part : i * part], "head", 2 * i) for i in range(1, n_head // 2)
    ]
    out_shape = shaped((part, width), F32)
    sums = call(out_own_kernel, (out_shape,) * (n_head // 2), [keep, out_proj], 0.8)
    late_got = []
    for i in range(1, n_head // 2):
        late = call(out_kernel, shaped((part, width), BF16), [other, w_other, sums[i]], 0.5, first=i)
        late_perm = [
            (c * n_head + h, c * n_head + (h ^ (2 * i)) if h % 2 else (c ^ 1) * n_head + h)
            for c in range(n_ctx)
            for h in range(n_head)
        ]
        late_got.append(lax.ppermute(late, ctx_head, late_perm))
    out = call(out_kernel, out_shape, [other, w_other, sums[0]], 0.5, first=0)
    out, *early_got = lax.optimization_barrier((out, *early_got))
    passed = [xor_sent(mine, "head", 1) for mine in early_got]
    return call(total_kernel, shaped((part, width), BF16), [out, *early_got, *passed, *late_got], 0.5)


def solution(mesh):
    in_specs = (
        P(("ctx", "head"), None),
        P(None, "head", None),
        P(None, "head", None),
        P(None, "head", "ctx"),
        P(),
        P("head", None),
    )
    out_specs = P(("ctx", "head"), None)
    return jax.shard_map(local, mesh=mesh, in_specs=in_specs, out_specs=out_specs, check_vma=False)
```

```python
import functools

import jax
import jax.numpy as jnp
from jax import lax
from jax.experimental import pallas as pl
from jax.experimental.pallas import tpu as pltpu
from jax.sharding import PartitionSpec as P

DK = 128
DV = 128
KERNEL = 4
HALO = 16
HALF = 128
EPSILON = 1e-06
F32 = jnp.float32
BF16 = jnp.bfloat16
VMEM_BYTES = 24 * 1024 * 1024


def dot(a, b):
    return jnp.dot(a, b, preferred_element_type=F32)


def dot_t(a, b):
    return lax.dot_general(a, b, (((1,), (1,)), ((), ())), preferred_element_type=F32)


def silu(x):
    return x / (1.0 + jnp.exp(-x))


def l2_normed(x):
    return x * lax.rsqrt(jnp.sum(x * x, axis=-1, keepdims=True) + EPSILON)


def conv_silu(padded, slot, weights, rows):
    acc = padded[slot, HALO - KERNEL + 1 : HALO - KERNEL + 1 + rows, :] * weights[0]
    for i in range(1, KERNEL):
        lo = HALO - KERNEL + 1 + i
        acc = acc + padded[slot, lo : lo + rows, :] * weights[i]
    return silu(acc)


def block_decay(ccol, crow, a, b):
    gap = ccol[a * HALF : (a + 1) * HALF] - crow[:, b * HALF : (b + 1) * HALF]
    return jnp.exp(jnp.minimum(gap, 0.0))


def placed(step):
    return lax.axis_index("ctx") // step % 2 == 1


def true_index(local, count):
    half = count // 2
    odd = lax.axis_index("ctx") % 2
    return (1 - odd if local < half else odd) * half + local % half


def fetch_kernel(x_any, logits_any, packed, x_own, logits, tail, rows, sems):
    logits_copy = pltpu.make_async_copy(logits_any, logits, sems.at[2])
    tail_copy = pltpu.make_async_copy(x_any.at[pl.ds(x_any.shape[0] - HALO, HALO), :], tail, sems.at[0])
    own_copy = pltpu.make_async_copy(x_any, x_own, sems.at[1])
    tail_copy.start()
    own_copy.start()
    logits_copy.start()
    tail_copy.wait()
    width = tail.shape[1]
    last = tail[...].astype(F32)
    taps = KERNEL - 1
    for r in range(taps):
        for t in range(width // 128):
            at = r * (width // 128) + t
            rows[at : at + 1, :] = last[HALO - taps + r : HALO - taps + r + 1, t * 128 : (t + 1) * 128]
    packed[...] = rows[...].astype(BF16)
    own_copy.wait()
    logits_copy.wait()


def gates_kernel(logits, rows, cols, decays):
    toks = logits.shape[2]
    blocks = toks // HALF
    half = logits.shape[1] // 2
    given = [logits[i] for i in range(2)]
    given = [jnp.where(placed(1), a, jnp.concatenate([a[half:], a[:half]], axis=0)) for a in given]
    x = given[0]
    log_decay = -(jnp.maximum(x, 0.0) + jnp.log1p(jnp.exp(-jnp.abs(x))))
    beta = 1.0 / (1.0 + jnp.exp(-given[1]))
    heads = x.shape[0]
    ri = lax.broadcasted_iota(jnp.int32, (toks, toks), 0)
    ci = lax.broadcasted_iota(jnp.int32, (toks, toks), 1)
    exact = lax.Precision.HIGHEST
    rows[...] = jnp.dot(log_decay, (ri <= ci).astype(F32), precision=exact, preferred_element_type=F32)
    last_dims = (((1,), (1,)), ((), ()))
    ccols = lax.dot_general((ri >= ci).astype(F32), log_decay, last_dims, precision=exact, preferred_element_type=F32)
    bcols = lax.dot_general((ri == ci).astype(F32), beta, last_dims, precision=exact, preferred_element_type=F32)
    cols[:, 0:heads] = ccols
    cols[:, heads : 2 * heads] = bcols
    below = ri[:HALF, :HALF] > ci[:HALF, :HALF]
    for j in range(heads):
        i = 0
        for a in range(blocks):
            for b in range(a + 1):
                m = block_decay(ccols[:, j : j + 1], rows[j : j + 1, :], a, b)
                m = m * bcols[a * HALF : (a + 1) * HALF, j : j + 1]
                decays[j, i] = jnp.where(below, m, 0.0) if a == b else m
                i += 1


def conv_weights(weight, g, lanes):
    taps = []
    for i in range(KERNEL):
        tap = weight[i, 0:1, lanes]
        for h in range(1, weight.shape[1]):
            tap = jnp.where(g == h, weight[i, h : h + 1, lanes], tap)
        taps.append(tap)
    return taps


def keys_terms(x, w, cw, cols, rows, decays, s_out, y_out, k_out, padded, *, first, key_heads, ratio):
    toks = x.shape[0] - HALO
    blocks = toks // HALF
    count = key_heads // 2
    heads = key_heads * ratio
    width = DK + ratio * DV
    ri = lax.broadcasted_iota(jnp.int32, (HALF, HALF), 0)
    ci = lax.broadcasted_iota(jnp.int32, (HALF, HALF), 1)
    level = jnp.where(ri > ci, ri ^ ci, 0)
    eye = jnp.where(ri == ci, 1.0, 0.0).astype(F32)
    for g in range(count):
        at = pl.multiple_of(true_index(first + g, key_heads) * width, 128)
        proj = dot(x[...], w[:, pl.ds(at, width)]).astype(BF16).astype(F32)
        for t in range(1 + ratio):
            padded[g * (1 + ratio) + t] = proj[:, t * 128 : (t + 1) * 128]
    kts, rhs, lowers, offs = [], [], [], []
    for g in range(count):
        base = g * (1 + ratio)
        group = true_index(first + g, key_heads)
        k = l2_normed(conv_silu(padded, base, conv_weights(cw, group, slice(DK, 2 * DK)), toks))
        kb = k.astype(BF16)
        k_out[g] = kb
        kf = kb.astype(F32)
        kts.append(kf.T)
        ks = [kb[b * HALF : (b + 1) * HALF] for b in range(blocks)]
        grams = {(a, b): dot_t(ks[a], ks[b]) for a in range(blocks) for b in range(a + 1)}
        for r in range(ratio):
            j = (first + g) * ratio + r
            lanes = slice(2 * DK + r * DV, 2 * DK + (r + 1) * DV)
            v = conv_silu(padded, base + 1 + r, conv_weights(cw, group, lanes), toks)
            ccol = cols[:, j : j + 1]
            bcol = cols[:, heads + j : heads + j + 1]
            rk = (kf * (bcol * jnp.exp(ccol))).astype(BF16)
            rv = (v * bcol).astype(BF16)
            rhs.append(jnp.concatenate([rk, rv], axis=1))
            off, i = {}, 0
            for a in range(blocks):
                for b in range(a + 1):
                    m = grams[(a, b)] * decays[j, i]
                    i += 1
                    if a == b:
                        lowers.append(m)
                    else:
                        off[(a, b)] = m.astype(BF16)
            offs.append(off)
    inv = [eye - jnp.where(level == 1, m, 0.0) for m in lowers]
    inv_b = [m.astype(BF16) for m in inv]
    size = 2
    while size < HALF:
        here = (level >= size) & (level < 4 * size)
        steps = [dot(x, jnp.where(here, m, 0.0).astype(BF16)).astype(BF16) for m, x in zip(lowers, inv_b)]
        squares = [dot(n, n).astype(BF16) for n in steps]
        inv = [x - dot(n, xb) for x, xb, n in zip(inv, inv_b, steps)]
        inv = [x + dot(n, x.astype(BF16)) for x, n in zip(inv, squares)]
        inv_b = [m.astype(BF16) for m in inv]
        size *= 4
    solved = [[] for _ in rhs]
    for a in range(blocks):
        for j, given in enumerate(rhs):
            r = given[a * HALF : (a + 1) * HALF]
            if a:
                acc = r.astype(F32)
                for b in range(a):
                    acc = acc - dot(offs[j][(a, b)], solved[j][b])
                r = acc.astype(BF16)
            solved[j].append(dot(inv_b[j * blocks + a], r).astype(BF16))
    for j in range(len(rhs)):
        y = jnp.concatenate(solved[j], axis=0)
        y_out[j] = y
        at = first * ratio + j
        crow = rows[at : at + 1, :]
        last = crow[:, toks - 1 : toks]
        kd = (kts[j // ratio] * jnp.exp(last - crow)).astype(BF16)
        s = dot(kd, y)
        s_out[j, :, 0:DK] = (eye * jnp.exp(last) - s[:, 0:DK]).astype(BF16)
        s_out[j, :, DK:] = s[:, DK:].astype(BF16)


def keys_first_kernel(*refs, n_head, key_heads, ratio):
    pieces = refs[:n_head]
    halo, halo_core, w, cw, cols, rows, decays, s_out, y_out, k_out, x_out, padded, halo_rows = refs[n_head:]
    me = lax.axis_index("head")
    part = pieces[0].shape[0]
    direct = (me % 2 == 1) != (me >= n_head - 2)
    given = jnp.where(direct, halo[...].astype(F32), halo_core[...].astype(F32))
    taps, tiles = KERNEL - 1, x_out.shape[1] // 128
    halo_rows[...] = jnp.zeros_like(halo_rows)
    for r in range(taps):
        for t in range(tiles):
            at = HALO - taps + r
            halo_rows[at : at + 1, t * 128 : (t + 1) * 128] = given[r * tiles + t : r * tiles + t + 1, :]
    x_out[0:HALO, :] = halo_rows[...].astype(BF16)
    for s in range(n_head):
        at = pl.multiple_of(HALO + (me ^ s) * part, 16)
        x_out[pl.ds(at, part), :] = pieces[s][...]
    keys_terms(
        x_out, w, cw, cols, rows, decays, s_out, y_out, k_out, padded, first=0, key_heads=key_heads, ratio=ratio
    )


def keys_second_kernel(x, w, cw, cols, rows, decays, s_out, y_out, k_out, padded, *, key_heads, ratio):
    keys_terms(
        x, w, cw, cols, rows, decays, s_out, y_out, k_out, padded,
        first=key_heads // 2, key_heads=key_heads, ratio=ratio,
    )


def queries_kernel(
    x, wq, wz, cw, cols, rows, keys_a, keys_b, ys_a, ys_b, gain, q_out, o_out, g_out, padded, *, key_heads, ratio
):
    toks = x.shape[0] - HALO
    blocks = toks // HALF
    ri = lax.broadcasted_iota(jnp.int32, (HALF, HALF), 0)
    ci = lax.broadcasted_iota(jnp.int32, (HALF, HALF), 1)
    upto = ri >= ci
    for g in range(key_heads):
        group = true_index(g, key_heads)
        at = pl.multiple_of(group * DK, 128)
        padded[g] = dot(x[...], wq[:, pl.ds(at, DK)]).astype(BF16).astype(F32)
        at = pl.multiple_of(group * ratio * DV, 128)
        proj = dot(x[HALO:, :], wz[:, pl.ds(at, ratio * DV)]).astype(BF16).astype(F32)
        for r in range(ratio):
            z = proj[:, r * DV : (r + 1) * DV]
            g_out[g * ratio + r] = gain[...] * silu(z)
    for g in range(key_heads):
        weights = conv_weights(cw, true_index(g, key_heads), slice(0, DK))
        q = l2_normed(conv_silu(padded, g, weights, toks)) * DK ** (-0.5)
        qb = q.astype(BF16)
        count = key_heads // 2
        kb = keys_b[g - count] if g >= count else keys_a[g]
        grams = {
            (a, b): dot_t(qb[a * HALF : (a + 1) * HALF], kb[b * HALF : (b + 1) * HALF])
            for a in range(blocks)
            for b in range(a + 1)
        }
        for r in range(ratio):
            j = g * ratio + r
            ccol = cols[:, j : j + 1]
            crow = rows[j : j + 1, :]
            ys, i = (ys_b, j - count * ratio) if g >= count else (ys_a, j)
            for a in range(blocks):
                at = slice(a * HALF, (a + 1) * HALF)
                acc = None
                for b in range(a + 1):
                    m = grams[(a, b)] * block_decay(ccol, crow, a, b)
                    if a == b:
                        m = jnp.where(upto, m, 0.0)
                    term = dot(m.astype(BF16), ys[i, b * HALF : (b + 1) * HALF, :])
                    acc = term if acc is None else acc + term
                q_out[j, at, :] = (q[at] * jnp.exp(ccol[at]) - acc[:, 0:DK]).astype(BF16)
                o_out[j, at, :] = acc[:, DK:]


def join_kernel(own, got, out, *, step):
    upper = placed(step)
    for j in range(own.shape[0]):
        mine, other = own[j], got[j]
        later = jnp.where(upper, mine, other)
        earlier = jnp.where(upper, other, mine)
        if out.shape[-1] == DV:
            out[j] = (dot(later[:, 0:DK], earlier[:, DK:]) + later[:, DK:].astype(F32)).astype(BF16)
        else:
            prod = dot(later[:, 0:DK], earlier)
            out[j, :, 0:DK] = prod[:, 0:DK].astype(BF16)
            out[j, :, DK:] = (prod[:, DK:] + later[:, DK:].astype(F32)).astype(BF16)


def prefix_kernel(before, got, out, *, step):
    upper = placed(step)
    for j in range(before.shape[0]):
        prod = dot(before[j, :, 0:DK], got[j])
        prod_t, prod_b = prod[:, 0:DK], prod[:, DK:] + before[j, :, DK:].astype(F32)
        out[j, :, 0:DK] = jnp.where(upper, prod_t.astype(BF16), before[j, :, 0:DK])
        out[j, :, DK:] = jnp.where(upper, prod_b.astype(BF16), before[j, :, DK:])


def states_kernel(own, pair, before, got, keep, send, *, before_step, step):
    odd = placed(1)
    began = placed(before_step)
    upper = placed(step)
    for j in range(own.shape[0]):
        t, b = before[j, :, 0:DK], before[j, :, DK:].astype(F32)
        if before_step == 2:
            last = got[j].astype(F32)
            entered = jnp.where(began, dot(t, got[j]), last)
            b = jnp.where(began, b, 0.0)
        else:
            entered = dot(t, got[j])
        entered = jnp.where(upper, entered, 0.0) + b
        first = jnp.where(odd, pair[j], own[j])
        passed = dot(first[:, 0:DK], entered.astype(BF16)) + first[:, DK:].astype(F32)
        keep[j] = jnp.where(odd, passed, entered).astype(BF16)
        send[j] = jnp.where(odd, entered, passed).astype(BF16)


def normed_kernel(q, o, own, got, gate, keep, send, scratch, *, n_head):
    me = lax.axis_index("head")
    heads = q.shape[0]
    half = heads // 2
    for j in range(heads):
        att = o[j] + dot(q[j], own[j - half] if j >= half else got[j])
        scale = lax.rsqrt(jnp.mean(att * att, axis=-1, keepdims=True) + EPSILON)
        at = pl.multiple_of(true_index(j, heads) * DV, 128)
        scratch[:, pl.ds(at, DV)] = (att * scale * gate[j]).astype(BF16)
    part = scratch.shape[0] // n_head
    for i in range(n_head // 2):
        at = pl.multiple_of((me ^ (2 * i)) * part, 16)
        keep[i * part : (i + 1) * part, :] = scratch[pl.ds(at, part), :]
        at = pl.multiple_of((me ^ (2 * i + 1)) * part, 16)
        send[i * part : (i + 1) * part, :] = scratch[pl.ds(at, part), :]


def early_kernel(keep, send, w, out):
    even = lax.axis_index("head") % 2 == 0
    part = keep.shape[0] - out.shape[0]
    out[...] = dot(jnp.where(even, keep[part:, :], send[part:, :]), w[...]).astype(BF16)


def out_own_kernel(own, w, *outs):
    part = outs[0].shape[0]
    for i, out in enumerate(outs):
        out[...] = dot(own[i * part : (i + 1) * part, :], w[...])


def out_kernel(got, w, before, out, *, first):
    part = out.shape[0]
    rows = slice(first * part, (first + 1) * part)
    out[...] = (before[...] + dot(got[rows, :], w[...])).astype(out.dtype)


def total_kernel(*refs):
    even = lax.axis_index("head") % 2 == 0
    count = (len(refs) - 2) // 3
    acc = refs[0][...]
    for i in range(count):
        mine, passed, late = (refs[1 + i + t * count][...].astype(F32) for t in range(3))
        acc = acc + jnp.where(even, mine + passed, late)
    refs[-1][...] = acc.astype(BF16)


def call(body, out_shape, args, us, scratch=(), any_space=(), **static):
    nbytes = sum(a.size * a.dtype.itemsize for a in args)
    vmem = pl.BlockSpec(memory_space=pltpu.VMEM)
    args = [pltpu.with_memory_space_constraint(a, pltpu.HBM) if i in any_space else a for i, a in enumerate(args)]
    return pl.pallas_call(
        functools.partial(body, **static),
        out_shape=out_shape,
        in_specs=[pl.BlockSpec(memory_space=pltpu.HBM) if i in any_space else vmem for i in range(len(args))],
        out_specs=jax.tree.map(lambda _: vmem, out_shape),
        scratch_shapes=list(scratch),
        compiler_params=pltpu.CompilerParams(vmem_limit_bytes=VMEM_BYTES),
        cost_estimate=pl.CostEstimate(flops=int(us * 1.15e9), bytes_accessed=nbytes, transcendentals=0),
    )(*args)


def shaped(shape, dtype):
    return jax.ShapeDtypeStruct(shape, dtype)


def xor_sent(value, axis, step):
    count = lax.axis_size(axis)
    return lax.ppermute(value, axis, [(i, i ^ step) for i in range(count)])


def halo_pairs(n_ctx, n_head, target):
    source = n_head - 1
    pairs = [((c - 1, source), (c, target)) for c in range(1, n_ctx)]
    spare = [h for h in range(n_head) if h not in (source, target)]
    if n_ctx % 4 == 0 and len(spare) == 2:
        a, b = spare
        pairs += [((0, target), (0, a)), ((n_ctx - 1, source), (n_ctx - 1, b)), ((1, a), (1, b)), ((0, b), (2, b))]
        pairs += [((c, a), (c + 1, a)) for c in range(2, n_ctx, 2)]
        pairs += [((c + i, b), (c + i + 2, b)) for c in range(3, n_ctx - 1, 4) for i in range(2)]
    flat = [(c * n_head + h, d * n_head + k) for (c, h), (d, k) in pairs]
    return sorted(flat + [(d, c) for c, d in flat])


def local(layer_in, in_proj, conv_weight, gate_logits, norm_gain, out_proj):
    n_head, n_ctx = lax.axis_size("head"), lax.axis_size("ctx")
    width, key_heads, group = in_proj.shape
    heads = gate_logits.shape[1]
    ratio = heads // key_heads
    part = layer_in.shape[0]
    toks = part * n_head
    ctx_head = ("ctx", "head")

    pieces = [layer_in] + [None] * (n_head - 1)
    step = n_head // 2
    while step:
        for s in range(0, n_head, 2 * step):
            pieces[s + step] = xor_sent(pieces[s], "head", step)
        step //= 2
    blocks = toks // HALF
    packed_shape = shaped(((KERNEL - 1) * (width // 128), 128), BF16)
    tail, x_own, logits = call(
        fetch_kernel,
        (packed_shape, shaped((part, width), BF16), shaped(gate_logits.shape, F32)),
        [layer_in, gate_logits],
        6.0,
        [pltpu.VMEM((HALO, width), BF16), pltpu.VMEM(packed_shape.shape, F32), pltpu.SemaphoreType.DMA((3,))],
        any_space=(0, 1),
    )
    rows, cols, decays = call(
        gates_kernel,
        (
            shaped((heads, toks), F32),
            shaped((toks, 2 * heads), F32),
            shaped((heads, blocks * (blocks + 1) // 2, HALF, HALF), F32),
        ),
        [logits],
        1.0,
    )
    me = lax.axis_index("head")
    halo = jnp.zeros_like(tail)
    for h in range(n_head - 1, 0, -2):
        target = h if h < n_head - 1 else h - 1
        wanted = (me == target) & (lax.axis_index("ctx") > 0)
        halo = jnp.where(wanted, lax.ppermute(tail, ctx_head, halo_pairs(n_ctx, n_head, target)), halo)
    v_end = 2 * DK + ratio * DV
    w_kv = in_proj[:, :, DK:v_end].reshape(width, key_heads * (v_end - DK))
    halo, w_kv = lax.optimization_barrier((halo, w_kv))
    halo_core = xor_sent(halo, "head", 1)
    w_q = in_proj[:, :, 0:DK].reshape(width, key_heads * DK)
    w_z = in_proj[:, :, v_end:].reshape(width, heads * DV)

    half = heads // 2
    pair_shape = shaped((half, DK, DK + DV), BF16)
    state_shape = shaped((half, DK, DV), BF16)
    key_count = key_heads // 2
    ys_shape = shaped((half, toks, DK + DV), BF16)
    keys_shape = shaped((key_count, toks, DK), BF16)
    padded = pltpu.VMEM((key_count * (1 + ratio), HALO + toks, 128), F32)
    s_send, ys_a, keys_a, x_full = call(
        keys_first_kernel,
        (pair_shape, ys_shape, keys_shape, shaped((HALO + toks, width), BF16)),
        [x_own, *pieces[1:], halo, halo_core, w_kv, conv_weight, cols, rows, decays],
        3.0,
        [padded, pltpu.VMEM((HALO, width), F32)],
        n_head=n_head,
        key_heads=key_heads,
        ratio=ratio,
    )
    s_pair = xor_sent(s_send, "ctx", 1)
    s_keep, ys_b, keys_b = call(
        keys_second_kernel,
        (pair_shape, ys_shape, keys_shape),
        [x_full, w_kv, conv_weight, cols, rows, decays],
        3.0,
        [padded],
        key_heads=key_heads,
        ratio=ratio,
    )
    w_other = xor_sent(lax.optimization_barrier((out_proj, s_send))[0], "head", 1)
    total = call(join_kernel, pair_shape, [s_keep, s_pair], 0.2, step=1)
    step, before, before_step = 2, None, 2
    while 2 * step < n_ctx:
        got = xor_sent(total, "ctx", step)
        if step == 2:
            got, w_q, w_z = lax.optimization_barrier((got, w_q, w_z))
        more = 4 * step < n_ctx
        total = call(join_kernel, pair_shape if more else state_shape, [total, got], 0.2, step=step)
        if before is None:
            before = got
        else:
            if before_step == 2:
                entry = jnp.concatenate([jnp.eye(DK, dtype=BF16), jnp.zeros((DK, DV), BF16)], axis=1)
                before = jnp.where(lax.axis_index("ctx") // 2 % 2 == 1, before, entry)
                before_step = 1
            before = call(prefix_kernel, pair_shape, [before, got], 0.2, step=step)
        step *= 2
    got = xor_sent(total, "ctx", step)
    own_state, out_state = call(
        states_kernel,
        (state_shape, state_shape),
        [s_keep, s_pair, before, got],
        0.3,
        before_step=before_step,
        step=step,
    )
    got_state = xor_sent(out_state, "ctx", 1)
    o_shape = shaped((heads, toks, DV), F32)
    q, o, gate = call(
        queries_kernel,
        (shaped((heads, toks, DK), BF16), o_shape, o_shape),
        [x_full, w_q, w_z, conv_weight, cols, rows, keys_a, keys_b, ys_a, ys_b, norm_gain[None, :]],
        1.9,
        [pltpu.VMEM((key_heads, HALO + toks, 128), F32)],
        key_heads=key_heads,
        ratio=ratio,
    )
    rows_shape = shaped((toks // 2, heads * DV), BF16)
    keep, send = call(
        normed_kernel,
        (rows_shape, rows_shape),
        [q, o, own_state, got_state, gate],
        0.4,
        [pltpu.VMEM((toks, heads * DV), BF16)],
        n_head=n_head,
    )
    other = xor_sent(send, "head", 1)
    early = call(early_kernel, shaped((toks // 2 - part, width), BF16), [keep, send, out_proj], 0.4)
    early_got = [
        xor_sent(early[(i - 1) * part : i * part], "head", 2 * i) for i in range(1, n_head // 2)
    ]
    out_shape = shaped((part, width), F32)
    sums = call(out_own_kernel, (out_shape,) * (n_head // 2), [keep, out_proj], 0.8)
    late_got = []
    for i in range(1, n_head // 2):
        late = call(out_kernel, shaped((part, width), BF16), [other, w_other, sums[i]], 0.5, first=i)
        late_perm = [
            (c * n_head + h, c * n_head + (h ^ (2 * i)) if h % 2 else (c ^ 1) * n_head + h)
            for c in range(n_ctx)
            for h in range(n_head)
        ]
        late_got.append(lax.ppermute(late, ctx_head, late_perm))
    out = call(out_kernel, out_shape, [other, w_other, sums[0]], 0.5, first=0)
    out, *early_got = lax.optimization_barrier((out, *early_got))
    passed = [xor_sent(mine, "head", 1) for mine in early_got]
    return call(total_kernel, shaped((part, width), BF16), [out, *early_got, *passed, *late_got], 0.5)


def solution(mesh):
    in_specs = (
        P(("ctx", "head"), None),
        P(None, "head", None),
        P(None, "head", None),
        P(None, "head", "ctx"),
        P(),
        P("head", None),
    )
    out_specs = P(("ctx", "head"), None)
    return jax.shard_map(local, mesh=mesh, in_specs=in_specs, out_specs=out_specs, check_vma=False)
```

```python
import functools

import jax
import jax.numpy as jnp
from jax import lax
from jax.experimental import pallas as pl
from jax.experimental.pallas import tpu as pltpu
from jax.sharding import PartitionSpec as P

DK = 128
DV = 128
KERNEL = 4
HALO = 16
HALF = 128
EPSILON = 1e-06
F32 = jnp.float32
BF16 = jnp.bfloat16
VMEM_BYTES = 24 * 1024 * 1024


def dot(a, b):
    return jnp.dot(a, b, preferred_element_type=F32)


def dot_t(a, b):
    return lax.dot_general(a, b, (((1,), (1,)), ((), ())), preferred_element_type=F32)


def silu(x):
    return x / (1.0 + jnp.exp(-x))


def l2_normed(x):
    return x * lax.rsqrt(jnp.sum(x * x, axis=-1, keepdims=True) + EPSILON)


def conv_silu(padded, slot, weights, rows):
    acc = padded[slot, HALO - KERNEL + 1 : HALO - KERNEL + 1 + rows, :] * weights[0]
    for i in range(1, KERNEL):
        lo = HALO - KERNEL + 1 + i
        acc = acc + padded[slot, lo : lo + rows, :] * weights[i]
    return silu(acc)


def block_decay(ccol, crow, a, b):
    gap = ccol[a * HALF : (a + 1) * HALF] - crow[:, b * HALF : (b + 1) * HALF]
    return jnp.exp(jnp.minimum(gap, 0.0))


def placed(step):
    return lax.axis_index("ctx") // step % 2 == 1


def true_index(local, count):
    half = count // 2
    odd = lax.axis_index("ctx") % 2
    return (1 - odd if local < half else odd) * half + local % half


def fetch_kernel(x_any, logits_any, packed, x_own, logits, tail, rows, sems):
    logits_copy = pltpu.make_async_copy(logits_any, logits, sems.at[2])
    tail_copy = pltpu.make_async_copy(x_any.at[pl.ds(x_any.shape[0] - HALO, HALO), :], tail, sems.at[0])
    own_copy = pltpu.make_async_copy(x_any, x_own, sems.at[1])
    tail_copy.start()
    own_copy.start()
    logits_copy.start()
    tail_copy.wait()
    width = tail.shape[1]
    last = tail[...].astype(F32)
    taps = KERNEL - 1
    for r in range(taps):
        for t in range(width // 128):
            at = r * (width // 128) + t
            rows[at : at + 1, :] = last[HALO - taps + r : HALO - taps + r + 1, t * 128 : (t + 1) * 128]
    packed[...] = rows[...].astype(BF16)
    own_copy.wait()
    logits_copy.wait()


def gates_kernel(logits, rows, cols, decays):
    toks = logits.shape[2]
    blocks = toks // HALF
    half = logits.shape[1] // 2
    given = [logits[i] for i in range(2)]
    given = [jnp.where(placed(1), a, jnp.concatenate([a[half:], a[:half]], axis=0)) for a in given]
    x = given[0]
    log_decay = -(jnp.maximum(x, 0.0) + jnp.log1p(jnp.exp(-jnp.abs(x))))
    beta = 1.0 / (1.0 + jnp.exp(-given[1]))
    heads = x.shape[0]
    ri = lax.broadcasted_iota(jnp.int32, (toks, toks), 0)
    ci = lax.broadcasted_iota(jnp.int32, (toks, toks), 1)
    exact = lax.Precision.HIGHEST
    cum = jnp.dot(log_decay, (ri <= ci).astype(F32), precision=exact, preferred_element_type=F32)
    rows[...] = cum
    both = jnp.concatenate([cum, beta], axis=0).T
    cols[...] = both
    ccols, bcols = both[:, 0:heads], both[:, heads:]
    below = ri[:HALF, :HALF] > ci[:HALF, :HALF]
    for j in range(heads):
        i = 0
        for a in range(blocks):
            for b in range(a + 1):
                m = block_decay(ccols[:, j : j + 1], rows[j : j + 1, :], a, b)
                m = m * bcols[a * HALF : (a + 1) * HALF, j : j + 1]
                decays[j, i] = jnp.where(below, m, 0.0) if a == b else m
                i += 1


def conv_weights(weight, g, lanes):
    taps = []
    for i in range(KERNEL):
        tap = weight[i, 0:1, lanes]
        for h in range(1, weight.shape[1]):
            tap = jnp.where(g == h, weight[i, h : h + 1, lanes], tap)
        taps.append(tap)
    return taps


def keys_terms(x, w, cw, cols, rows, decays, s_out, y_out, k_out, padded, *, first, key_heads, ratio):
    toks = x.shape[0] - HALO
    blocks = toks // HALF
    count = key_heads // 2
    heads = key_heads * ratio
    width = DK + ratio * DV
    ri = lax.broadcasted_iota(jnp.int32, (HALF, HALF), 0)
    ci = lax.broadcasted_iota(jnp.int32, (HALF, HALF), 1)
    level = jnp.where(ri > ci, ri ^ ci, 0)
    eye = jnp.where(ri == ci, 1.0, 0.0).astype(F32)
    for g in range(count):
        at = pl.multiple_of(true_index(first + g, key_heads) * width, 128)
        proj = dot(x[...], w[:, pl.ds(at, width)]).astype(BF16).astype(F32)
        for t in range(1 + ratio):
            padded[g * (1 + ratio) + t] = proj[:, t * 128 : (t + 1) * 128]
    kts, rhs, lowers, offs = [], [], [], []
    for g in range(count):
        base = g * (1 + ratio)
        group = true_index(first + g, key_heads)
        k = l2_normed(conv_silu(padded, base, conv_weights(cw, group, slice(DK, 2 * DK)), toks))
        kb = k.astype(BF16)
        k_out[g] = kb
        kf = kb.astype(F32)
        kts.append(kf.T)
        ks = [kb[b * HALF : (b + 1) * HALF] for b in range(blocks)]
        grams = {(a, b): dot_t(ks[a], ks[b]) for a in range(blocks) for b in range(a + 1)}
        for r in range(ratio):
            j = (first + g) * ratio + r
            lanes = slice(2 * DK + r * DV, 2 * DK + (r + 1) * DV)
            v = conv_silu(padded, base + 1 + r, conv_weights(cw, group, lanes), toks)
            ccol = cols[:, j : j + 1]
            bcol = cols[:, heads + j : heads + j + 1]
            rk = (kf * (bcol * jnp.exp(ccol))).astype(BF16)
            rv = (v * bcol).astype(BF16)
            rhs.append(jnp.concatenate([rk, rv], axis=1))
            off, i = {}, 0
            for a in range(blocks):
                for b in range(a + 1):
                    m = grams[(a, b)] * decays[j, i]
                    i += 1
                    if a == b:
                        lowers.append(m)
                    else:
                        off[(a, b)] = m.astype(BF16)
            offs.append(off)
    inv = [eye - jnp.where(level == 1, m, 0.0) for m in lowers]
    inv_b = [m.astype(BF16) for m in inv]
    size = 2
    while size < HALF:
        here = (level >= size) & (level < 4 * size)
        steps = [dot(x, jnp.where(here, m, 0.0).astype(BF16)).astype(BF16) for m, x in zip(lowers, inv_b)]
        squares = [dot(n, n).astype(BF16) for n in steps]
        inv = [x - dot(n, xb) for x, xb, n in zip(inv, inv_b, steps)]
        inv = [x + dot(n, x.astype(BF16)) for x, n in zip(inv, squares)]
        inv_b = [m.astype(BF16) for m in inv]
        size *= 4
    solved = [[] for _ in rhs]
    for a in range(blocks):
        for j, given in enumerate(rhs):
            r = given[a * HALF : (a + 1) * HALF]
            if a:
                acc = r.astype(F32)
                for b in range(a):
                    acc = acc - dot(offs[j][(a, b)], solved[j][b])
                r = acc.astype(BF16)
            solved[j].append(dot(inv_b[j * blocks + a], r).astype(BF16))
    for j in range(len(rhs)):
        y = jnp.concatenate(solved[j], axis=0)
        y_out[j] = y
        at = first * ratio + j
        crow = rows[at : at + 1, :]
        last = crow[:, toks - 1 : toks]
        kd = (kts[j // ratio] * jnp.exp(last - crow)).astype(BF16)
        s = dot(kd, y)
        s_out[j, :, 0:DK] = (eye * jnp.exp(last) - s[:, 0:DK]).astype(BF16)
        s_out[j, :, DK:] = s[:, DK:].astype(BF16)


def keys_first_kernel(*refs, n_head, key_heads, ratio):
    pieces = refs[:n_head]
    halo, halo_core, w, cw, cols, rows, decays, s_out, y_out, k_out, x_out, padded, halo_rows = refs[n_head:]
    me = lax.axis_index("head")
    part = pieces[0].shape[0]
    direct = (me % 2 == 1) != (me >= n_head - 2)
    given = jnp.where(direct, halo[...].astype(F32), halo_core[...].astype(F32))
    taps, tiles = KERNEL - 1, x_out.shape[1] // 128
    halo_rows[...] = jnp.zeros_like(halo_rows)
    for r in range(taps):
        for t in range(tiles):
            at = HALO - taps + r
            halo_rows[at : at + 1, t * 128 : (t + 1) * 128] = given[r * tiles + t : r * tiles + t + 1, :]
    x_out[0:HALO, :] = halo_rows[...].astype(BF16)
    for s in range(n_head):
        at = pl.multiple_of(HALO + (me ^ s) * part, 16)
        x_out[pl.ds(at, part), :] = pieces[s][...]
    keys_terms(
        x_out, w, cw, cols, rows, decays, s_out, y_out, k_out, padded, first=0, key_heads=key_heads, ratio=ratio
    )


def keys_second_kernel(x, w, cw, cols, rows, decays, s_out, y_out, k_out, padded, *, key_heads, ratio):
    keys_terms(
        x, w, cw, cols, rows, decays, s_out, y_out, k_out, padded,
        first=key_heads // 2, key_heads=key_heads, ratio=ratio,
    )


def queries_kernel(
    x, wq, wz, cw, cols, rows, keys_a, keys_b, ys_a, ys_b, gain, q_out, o_out, g_out, padded, *, key_heads, ratio
):
    toks = x.shape[0] - HALO
    blocks = toks // HALF
    ri = lax.broadcasted_iota(jnp.int32, (HALF, HALF), 0)
    ci = lax.broadcasted_iota(jnp.int32, (HALF, HALF), 1)
    upto = ri >= ci
    for g in range(key_heads):
        group = true_index(g, key_heads)
        at = pl.multiple_of(group * DK, 128)
        padded[g] = dot(x[...], wq[:, pl.ds(at, DK)]).astype(BF16).astype(F32)
        at = pl.multiple_of(group * ratio * DV, 128)
        proj = dot(x[HALO:, :], wz[:, pl.ds(at, ratio * DV)]).astype(BF16).astype(F32)
        for r in range(ratio):
            z = proj[:, r * DV : (r + 1) * DV]
            g_out[g * ratio + r] = gain[...] * silu(z)
    for g in range(key_heads):
        weights = conv_weights(cw, true_index(g, key_heads), slice(0, DK))
        q = l2_normed(conv_silu(padded, g, weights, toks)) * DK ** (-0.5)
        qb = q.astype(BF16)
        count = key_heads // 2
        kb = keys_b[g - count] if g >= count else keys_a[g]
        grams = {
            (a, b): dot_t(qb[a * HALF : (a + 1) * HALF], kb[b * HALF : (b + 1) * HALF])
            for a in range(blocks)
            for b in range(a + 1)
        }
        for r in range(ratio):
            j = g * ratio + r
            ccol = cols[:, j : j + 1]
            crow = rows[j : j + 1, :]
            ys, i = (ys_b, j - count * ratio) if g >= count else (ys_a, j)
            for a in range(blocks):
                at = slice(a * HALF, (a + 1) * HALF)
                acc = None
                for b in range(a + 1):
                    m = grams[(a, b)] * block_decay(ccol, crow, a, b)
                    if a == b:
                        m = jnp.where(upto, m, 0.0)
                    term = dot(m.astype(BF16), ys[i, b * HALF : (b + 1) * HALF, :])
                    acc = term if acc is None else acc + term
                q_out[j, at, :] = (q[at] * jnp.exp(ccol[at]) - acc[:, 0:DK]).astype(BF16)
                o_out[j, at, :] = acc[:, DK:]


def join_kernel(own, got, out, *, step):
    upper = placed(step)
    for j in range(own.shape[0]):
        mine, other = own[j], got[j]
        later = jnp.where(upper, mine, other)
        earlier = jnp.where(upper, other, mine)
        if out.shape[-1] == DV:
            out[j] = (dot(later[:, 0:DK], earlier[:, DK:]) + later[:, DK:].astype(F32)).astype(BF16)
        else:
            prod = dot(later[:, 0:DK], earlier)
            out[j, :, 0:DK] = prod[:, 0:DK].astype(BF16)
            out[j, :, DK:] = (prod[:, DK:] + later[:, DK:].astype(F32)).astype(BF16)


def prefix_kernel(before, got, out, *, step):
    upper = placed(step)
    for j in range(before.shape[0]):
        prod = dot(before[j, :, 0:DK], got[j])
        prod_t, prod_b = prod[:, 0:DK], prod[:, DK:] + before[j, :, DK:].astype(F32)
        out[j, :, 0:DK] = jnp.where(upper, prod_t.astype(BF16), before[j, :, 0:DK])
        out[j, :, DK:] = jnp.where(upper, prod_b.astype(BF16), before[j, :, DK:])


def states_kernel(own, pair, before, got, keep, send, *, before_step, step):
    odd = placed(1)
    began = placed(before_step)
    upper = placed(step)
    for j in range(own.shape[0]):
        t, b = before[j, :, 0:DK], before[j, :, DK:].astype(F32)
        if before_step == 2:
            last = got[j].astype(F32)
            entered = jnp.where(began, dot(t, got[j]), last)
            b = jnp.where(began, b, 0.0)
        else:
            entered = dot(t, got[j])
        entered = jnp.where(upper, entered, 0.0) + b
        first = jnp.where(odd, pair[j], own[j])
        passed = dot(first[:, 0:DK], entered.astype(BF16)) + first[:, DK:].astype(F32)
        keep[j] = jnp.where(odd, passed, entered).astype(BF16)
        send[j] = jnp.where(odd, entered, passed).astype(BF16)


def gated_norm(q, o, state, gate):
    att = o + dot(q, state)
    scale = lax.rsqrt(jnp.mean(att * att, axis=-1, keepdims=True) + EPSILON)
    return (att * scale * gate).astype(BF16)


def own_normed_kernel(q, o, own, gate, out):
    half = own.shape[0]
    for j in range(half):
        i = half + j
        out[:, j * DV : (j + 1) * DV] = gated_norm(q[i], o[i], own[j], gate[i])


def normed_kernel(q, o, got, gate, own, keep, send, scratch, *, n_head):
    me = lax.axis_index("head")
    heads = q.shape[0]
    half = heads // 2
    for j in range(heads):
        at = pl.multiple_of(true_index(j, heads) * DV, 128)
        if j < half:
            scratch[:, pl.ds(at, DV)] = gated_norm(q[j], o[j], got[j], gate[j])
        else:
            scratch[:, pl.ds(at, DV)] = own[:, (j - half) * DV : (j - half + 1) * DV]
    part = scratch.shape[0] // n_head
    for i in range(n_head // 2):
        at = pl.multiple_of((me ^ (2 * i)) * part, 16)
        keep[i * part : (i + 1) * part, :] = scratch[pl.ds(at, part), :]
        at = pl.multiple_of((me ^ (2 * i + 1)) * part, 16)
        send[i * part : (i + 1) * part, :] = scratch[pl.ds(at, part), :]


def early_kernel(keep, send, w, out):
    even = lax.axis_index("head") % 2 == 0
    part = keep.shape[0] - out.shape[0]
    out[...] = dot(jnp.where(even, keep[part:, :], send[part:, :]), w[...]).astype(BF16)


def out_own_kernel(own, w, *outs):
    part = outs[0].shape[0]
    for i, out in enumerate(outs):
        out[...] = dot(own[i * part : (i + 1) * part, :], w[...])


def out_kernel(got, w, before, out, *, first):
    part = out.shape[0]
    rows = slice(first * part, (first + 1) * part)
    out[...] = (before[...] + dot(got[rows, :], w[...])).astype(out.dtype)


def total_kernel(*refs):
    even = lax.axis_index("head") % 2 == 0
    count = (len(refs) - 2) // 3
    acc = refs[0][...]
    for i in range(count):
        mine, passed, late = (refs[1 + i + t * count][...].astype(F32) for t in range(3))
        acc = acc + jnp.where(even, mine + passed, late)
    refs[-1][...] = acc.astype(BF16)


def call(body, out_shape, args, us, scratch=(), any_space=(), **static):
    nbytes = sum(a.size * a.dtype.itemsize for a in args)
    vmem = pl.BlockSpec(memory_space=pltpu.VMEM)
    args = [pltpu.with_memory_space_constraint(a, pltpu.HBM) if i in any_space else a for i, a in enumerate(args)]
    return pl.pallas_call(
        functools.partial(body, **static),
        out_shape=out_shape,
        in_specs=[pl.BlockSpec(memory_space=pltpu.HBM) if i in any_space else vmem for i in range(len(args))],
        out_specs=jax.tree.map(lambda _: vmem, out_shape),
        scratch_shapes=list(scratch),
        compiler_params=pltpu.CompilerParams(vmem_limit_bytes=VMEM_BYTES),
        cost_estimate=pl.CostEstimate(flops=int(us * 1.15e9), bytes_accessed=nbytes, transcendentals=0),
    )(*args)


def shaped(shape, dtype):
    return jax.ShapeDtypeStruct(shape, dtype)


def xor_sent(value, axis, step):
    count = lax.axis_size(axis)
    return lax.ppermute(value, axis, [(i, i ^ step) for i in range(count)])


def halo_pairs(n_ctx, n_head, target):
    source = n_head - 1
    pairs = [((c - 1, source), (c, target)) for c in range(1, n_ctx)]
    spare = [h for h in range(n_head) if h not in (source, target)]
    if n_ctx % 4 == 0 and len(spare) == 2:
        a, b = spare
        pairs += [((0, target), (0, a)), ((n_ctx - 1, source), (n_ctx - 1, b)), ((1, a), (1, b)), ((0, b), (2, b))]
        pairs += [((c, a), (c + 1, a)) for c in range(2, n_ctx, 2)]
        pairs += [((c + i, b), (c + i + 2, b)) for c in range(3, n_ctx - 1, 4) for i in range(2)]
    flat = [(c * n_head + h, d * n_head + k) for (c, h), (d, k) in pairs]
    return sorted(flat + [(d, c) for c, d in flat])


def local(layer_in, in_proj, conv_weight, gate_logits, norm_gain, out_proj):
    n_head, n_ctx = lax.axis_size("head"), lax.axis_size("ctx")
    width, key_heads, group = in_proj.shape
    heads = gate_logits.shape[1]
    ratio = heads // key_heads
    part = layer_in.shape[0]
    toks = part * n_head
    ctx_head = ("ctx", "head")

    pieces = [layer_in] + [None] * (n_head - 1)
    step = n_head // 2
    while step:
        for s in range(0, n_head, 2 * step):
            pieces[s + step] = xor_sent(pieces[s], "head", step)
        step //= 2
    blocks = toks // HALF
    packed_shape = shaped(((KERNEL - 1) * (width // 128), 128), BF16)
    tail, x_own, logits = call(
        fetch_kernel,
        (packed_shape, shaped((part, width), BF16), shaped(gate_logits.shape, F32)),
        [layer_in, gate_logits],
        6.0,
        [pltpu.VMEM((HALO, width), BF16), pltpu.VMEM(packed_shape.shape, F32), pltpu.SemaphoreType.DMA((3,))],
        any_space=(0, 1),
    )
    rows, cols, decays = call(
        gates_kernel,
        (
            shaped((heads, toks), F32),
            shaped((toks, 2 * heads), F32),
            shaped((heads, blocks * (blocks + 1) // 2, HALF, HALF), F32),
        ),
        [logits],
        1.0,
    )
    me = lax.axis_index("head")
    halo = jnp.zeros_like(tail)
    for h in range(n_head - 1, 0, -2):
        target = h if h < n_head - 1 else h - 1
        wanted = (me == target) & (lax.axis_index("ctx") > 0)
        halo = jnp.where(wanted, lax.ppermute(tail, ctx_head, halo_pairs(n_ctx, n_head, target)), halo)
    v_end = 2 * DK + ratio * DV
    w_kv = in_proj[:, :, DK:v_end].reshape(width, key_heads * (v_end - DK))
    halo, w_kv = lax.optimization_barrier((halo, w_kv))
    halo_core = xor_sent(halo, "head", 1)
    w_q = in_proj[:, :, 0:DK].reshape(width, key_heads * DK)
    w_z = in_proj[:, :, v_end:].reshape(width, heads * DV)

    half = heads // 2
    pair_shape = shaped((half, DK, DK + DV), BF16)
    state_shape = shaped((half, DK, DV), BF16)
    key_count = key_heads // 2
    ys_shape = shaped((half, toks, DK + DV), BF16)
    keys_shape = shaped((key_count, toks, DK), BF16)
    padded = pltpu.VMEM((key_count * (1 + ratio), HALO + toks, 128), F32)
    s_send, ys_a, keys_a, x_full = call(
        keys_first_kernel,
        (pair_shape, ys_shape, keys_shape, shaped((HALO + toks, width), BF16)),
        [x_own, *pieces[1:], halo, halo_core, w_kv, conv_weight, cols, rows, decays],
        3.0,
        [padded, pltpu.VMEM((HALO, width), F32)],
        n_head=n_head,
        key_heads=key_heads,
        ratio=ratio,
    )
    s_pair = xor_sent(s_send, "ctx", 1)
    s_keep, ys_b, keys_b = call(
        keys_second_kernel,
        (pair_shape, ys_shape, keys_shape),
        [x_full, w_kv, conv_weight, cols, rows, decays],
        3.0,
        [padded],
        key_heads=key_heads,
        ratio=ratio,
    )
    w_other = xor_sent(lax.optimization_barrier((out_proj, s_send))[0], "head", 1)
    total = call(join_kernel, pair_shape, [s_keep, s_pair], 0.2, step=1)
    step, before, before_step = 2, None, 2
    while 2 * step < n_ctx:
        got = xor_sent(total, "ctx", step)
        if step == 2:
            got, w_q, w_z = lax.optimization_barrier((got, w_q, w_z))
        more = 4 * step < n_ctx
        total = call(join_kernel, pair_shape if more else state_shape, [total, got], 0.2, step=step)
        if before is None:
            before = got
        else:
            if before_step == 2:
                entry = jnp.concatenate([jnp.eye(DK, dtype=BF16), jnp.zeros((DK, DV), BF16)], axis=1)
                before = jnp.where(lax.axis_index("ctx") // 2 % 2 == 1, before, entry)
                before_step = 1
            before = call(prefix_kernel, pair_shape, [before, got], 0.2, step=step)
        step *= 2
    got = xor_sent(total, "ctx", step)
    own_state, out_state = call(
        states_kernel,
        (state_shape, state_shape),
        [s_keep, s_pair, before, got],
        0.3,
        before_step=before_step,
        step=step,
    )
    got_state = xor_sent(out_state, "ctx", 1)
    o_shape = shaped((heads, toks, DV), F32)
    q, o, gate = call(
        queries_kernel,
        (shaped((heads, toks, DK), BF16), o_shape, o_shape),
        [x_full, w_q, w_z, conv_weight, cols, rows, keys_a, keys_b, ys_a, ys_b, norm_gain[None, :]],
        1.9,
        [pltpu.VMEM((key_heads, HALO + toks, 128), F32)],
        key_heads=key_heads,
        ratio=ratio,
    )
    rows_shape = shaped((toks // 2, heads * DV), BF16)
    own_normed = call(own_normed_kernel, shaped((toks, half * DV), BF16), [q, o, own_state, gate], 0.2)
    keep, send = call(
        normed_kernel,
        (rows_shape, rows_shape),
        [q, o, got_state, gate, own_normed],
        0.4,
        [pltpu.VMEM((toks, heads * DV), BF16)],
        n_head=n_head,
    )
    other = xor_sent(send, "head", 1)
    early = call(early_kernel, shaped((toks // 2 - part, width), BF16), [keep, send, out_proj], 0.4)
    early_got = [
        xor_sent(early[(i - 1) * part : i * part], "head", 2 * i) for i in range(1, n_head // 2)
    ]
    out_shape = shaped((part, width), F32)
    sums = call(out_own_kernel, (out_shape,) * (n_head // 2), [keep, out_proj], 0.8)
    late_got = []
    for i in range(1, n_head // 2):
        late = call(out_kernel, shaped((part, width), BF16), [other, w_other, sums[i]], 0.5, first=i)
        late_perm = [
            (c * n_head + h, c * n_head + (h ^ (2 * i)) if h % 2 else (c ^ 1) * n_head + h)
            for c in range(n_ctx)
            for h in range(n_head)
        ]
        late_got.append(lax.ppermute(late, ctx_head, late_perm))
    out = call(out_kernel, out_shape, [other, w_other, sums[0]], 0.5, first=0)
    out, *early_got = lax.optimization_barrier((out, *early_got))
    passed = [xor_sent(mine, "head", 1) for mine in early_got]
    return call(total_kernel, shaped((part, width), BF16), [out, *early_got, *passed, *late_got], 0.5)


def solution(mesh):
    in_specs = (
        P(("ctx", "head"), None),
        P(None, "head", None),
        P(None, "head", None),
        P(None, "head", "ctx"),
        P(),
        P("head", None),
    )
    out_specs = P(("ctx", "head"), None)
    return jax.shard_map(local, mesh=mesh, in_specs=in_specs, out_specs=out_specs, check_vma=False)
```

```python
import functools

import jax
import jax.numpy as jnp
from jax import lax
from jax.experimental import pallas as pl
from jax.experimental.pallas import tpu as pltpu
from jax.sharding import PartitionSpec as P

DK = 128
DV = 128
KERNEL = 4
HALO = 16
HALF = 128
EPSILON = 1e-06
F32 = jnp.float32
BF16 = jnp.bfloat16
VMEM_BYTES = 24 * 1024 * 1024


def dot(a, b):
    return jnp.dot(a, b, preferred_element_type=F32)


def dot_t(a, b):
    return lax.dot_general(a, b, (((1,), (1,)), ((), ())), preferred_element_type=F32)


def silu(x):
    return x / (1.0 + jnp.exp(-x))


def l2_normed(x):
    return x * lax.rsqrt(jnp.sum(x * x, axis=-1, keepdims=True) + EPSILON)


def conv_silu(padded, slot, weights, rows):
    acc = padded[slot, HALO - KERNEL + 1 : HALO - KERNEL + 1 + rows, :] * weights[0]
    for i in range(1, KERNEL):
        lo = HALO - KERNEL + 1 + i
        acc = acc + padded[slot, lo : lo + rows, :] * weights[i]
    return silu(acc)


def block_decay(ccol, crow, a, b):
    gap = ccol[a * HALF : (a + 1) * HALF] - crow[:, b * HALF : (b + 1) * HALF]
    return jnp.exp(jnp.minimum(gap, 0.0))


def placed(step):
    return lax.axis_index("ctx") // step % 2 == 1


def true_index(local, count):
    half = count // 2
    odd = lax.axis_index("ctx") % 2
    return (1 - odd if local < half else odd) * half + local % half


def fetch_kernel(x_any, logits_any, packed, x_own, logits, tail, rows, sems):
    logits_copy = pltpu.make_async_copy(logits_any, logits, sems.at[2])
    tail_copy = pltpu.make_async_copy(x_any.at[pl.ds(x_any.shape[0] - HALO, HALO), :], tail, sems.at[0])
    own_copy = pltpu.make_async_copy(x_any, x_own, sems.at[1])
    tail_copy.start()
    own_copy.start()
    logits_copy.start()
    tail_copy.wait()
    width = tail.shape[1]
    last = tail[...].astype(F32)
    taps = KERNEL - 1
    for r in range(taps):
        for t in range(width // 128):
            at = r * (width // 128) + t
            rows[at : at + 1, :] = last[HALO - taps + r : HALO - taps + r + 1, t * 128 : (t + 1) * 128]
    packed[...] = rows[...].astype(BF16)
    own_copy.wait()
    logits_copy.wait()


def gates_kernel(logits, rows, cols, decays):
    toks = logits.shape[2]
    blocks = toks // HALF
    half = logits.shape[1] // 2
    given = [logits[i] for i in range(2)]
    given = [jnp.where(placed(1), a, jnp.concatenate([a[half:], a[:half]], axis=0)) for a in given]
    x = given[0]
    log_decay = -(jnp.maximum(x, 0.0) + jnp.log1p(jnp.exp(-jnp.abs(x))))
    beta = 1.0 / (1.0 + jnp.exp(-given[1]))
    heads = x.shape[0]
    ri = lax.broadcasted_iota(jnp.int32, (toks, toks), 0)
    ci = lax.broadcasted_iota(jnp.int32, (toks, toks), 1)
    exact = lax.Precision.HIGHEST
    cum = jnp.dot(log_decay, (ri <= ci).astype(F32), precision=exact, preferred_element_type=F32)
    rows[...] = cum
    both = jnp.concatenate([cum, beta], axis=0).T
    cols[...] = both
    ccols, bcols = both[:, 0:heads], both[:, heads:]
    below = ri[:HALF, :HALF] > ci[:HALF, :HALF]
    for j in range(heads):
        i = 0
        for a in range(blocks):
            for b in range(a + 1):
                m = block_decay(ccols[:, j : j + 1], rows[j : j + 1, :], a, b)
                m = m * bcols[a * HALF : (a + 1) * HALF, j : j + 1]
                decays[j, i] = jnp.where(below, m, 0.0) if a == b else m
                i += 1


def conv_weights(weight, g, lanes):
    taps = []
    for i in range(KERNEL):
        tap = weight[i, 0:1, lanes]
        for h in range(1, weight.shape[1]):
            tap = jnp.where(g == h, weight[i, h : h + 1, lanes], tap)
        taps.append(tap)
    return taps


def keys_terms(x, w, cw, cols, rows, decays, s_out, y_out, k_out, padded, *, first, key_heads, ratio):
    toks = x.shape[0] - HALO
    blocks = toks // HALF
    count = key_heads // 2
    heads = key_heads * ratio
    width = DK + ratio * DV
    ri = lax.broadcasted_iota(jnp.int32, (HALF, HALF), 0)
    ci = lax.broadcasted_iota(jnp.int32, (HALF, HALF), 1)
    level = jnp.where(ri > ci, ri ^ ci, 0)
    eye = jnp.where(ri == ci, 1.0, 0.0).astype(F32)
    for g in range(count):
        at = pl.multiple_of(true_index(first + g, key_heads) * width, 128)
        proj = dot(x[...], w[:, pl.ds(at, width)]).astype(BF16).astype(F32)
        for t in range(1 + ratio):
            padded[g * (1 + ratio) + t] = proj[:, t * 128 : (t + 1) * 128]
    kts, rhs, lowers, offs = [], [], [], []
    for g in range(count):
        base = g * (1 + ratio)
        group = true_index(first + g, key_heads)
        k = l2_normed(conv_silu(padded, base, conv_weights(cw, group, slice(DK, 2 * DK)), toks))
        kb = k.astype(BF16)
        k_out[g] = kb
        kf = kb.astype(F32)
        kts.append(kf.T)
        ks = [kb[b * HALF : (b + 1) * HALF] for b in range(blocks)]
        grams = {(a, b): dot_t(ks[a], ks[b]) for a in range(blocks) for b in range(a + 1)}
        for r in range(ratio):
            j = (first + g) * ratio + r
            lanes = slice(2 * DK + r * DV, 2 * DK + (r + 1) * DV)
            v = conv_silu(padded, base + 1 + r, conv_weights(cw, group, lanes), toks)
            ccol = cols[:, j : j + 1]
            bcol = cols[:, heads + j : heads + j + 1]
            rk = (kf * (bcol * jnp.exp(ccol))).astype(BF16)
            rv = (v * bcol).astype(BF16)
            rhs.append(jnp.concatenate([rk, rv], axis=1))
            off, i = {}, 0
            for a in range(blocks):
                for b in range(a + 1):
                    m = grams[(a, b)] * decays[j, i]
                    i += 1
                    if a == b:
                        lowers.append(m)
                    else:
                        off[(a, b)] = m.astype(BF16)
            offs.append(off)
    inv = [eye - jnp.where(level == 1, m, 0.0) for m in lowers]
    inv_b = [m.astype(BF16) for m in inv]
    size = 2
    while size < HALF:
        here = (level >= size) & (level < 4 * size)
        steps = [dot(x, jnp.where(here, m, 0.0).astype(BF16)).astype(BF16) for m, x in zip(lowers, inv_b)]
        squares = [dot(n, n).astype(BF16) for n in steps]
        inv = [x - dot(n, xb) for x, xb, n in zip(inv, inv_b, steps)]
        inv = [x + dot(n, x.astype(BF16)) for x, n in zip(inv, squares)]
        inv_b = [m.astype(BF16) for m in inv]
        size *= 4
    solved = [[] for _ in rhs]
    for a in range(blocks):
        for j, given in enumerate(rhs):
            r = given[a * HALF : (a + 1) * HALF]
            if a:
                acc = r.astype(F32)
                for b in range(a):
                    acc = acc - dot(offs[j][(a, b)], solved[j][b])
                r = acc.astype(BF16)
            solved[j].append(dot(inv_b[j * blocks + a], r).astype(BF16))
    for j in range(len(rhs)):
        y = jnp.concatenate(solved[j], axis=0)
        y_out[j] = y
        at = first * ratio + j
        crow = rows[at : at + 1, :]
        last = crow[:, toks - 1 : toks]
        kd = (kts[j // ratio] * jnp.exp(last - crow)).astype(BF16)
        s = dot(kd, y)
        s_out[j, :, 0:DK] = (eye * jnp.exp(last) - s[:, 0:DK]).astype(BF16)
        s_out[j, :, DK:] = s[:, DK:].astype(BF16)


def keys_first_kernel(*refs, n_head, key_heads, ratio):
    pieces = refs[:n_head]
    halo, halo_core, w, cw, cols, rows, decays, s_out, y_out, k_out, x_out, padded, halo_rows = refs[n_head:]
    me = lax.axis_index("head")
    part = pieces[0].shape[0]
    direct = (me % 2 == 1) != (me >= n_head - 2)
    given = jnp.where(direct, halo[...].astype(F32), halo_core[...].astype(F32))
    taps, tiles = KERNEL - 1, x_out.shape[1] // 128
    halo_rows[...] = jnp.zeros_like(halo_rows)
    for r in range(taps):
        for t in range(tiles):
            at = HALO - taps + r
            halo_rows[at : at + 1, t * 128 : (t + 1) * 128] = given[r * tiles + t : r * tiles + t + 1, :]
    x_out[0:HALO, :] = halo_rows[...].astype(BF16)
    for s in range(n_head):
        at = pl.multiple_of(HALO + (me ^ s) * part, 16)
        x_out[pl.ds(at, part), :] = pieces[s][...]
    keys_terms(
        x_out, w, cw, cols, rows, decays, s_out, y_out, k_out, padded, first=0, key_heads=key_heads, ratio=ratio
    )


def keys_second_kernel(x, w, cw, cols, rows, decays, s_out, y_out, k_out, padded, *, key_heads, ratio):
    keys_terms(
        x, w, cw, cols, rows, decays, s_out, y_out, k_out, padded,
        first=key_heads // 2, key_heads=key_heads, ratio=ratio,
    )


def queries_kernel(
    x, wq, wz, cw, cols, rows, keys_a, keys_b, ys_a, ys_b, gain, q_out, o_out, g_out, padded, *, key_heads, ratio
):
    toks = x.shape[0] - HALO
    blocks = toks // HALF
    ri = lax.broadcasted_iota(jnp.int32, (HALF, HALF), 0)
    ci = lax.broadcasted_iota(jnp.int32, (HALF, HALF), 1)
    upto = ri >= ci
    for g in range(key_heads):
        group = true_index(g, key_heads)
        at = pl.multiple_of(group * DK, 128)
        padded[g] = dot(x[...], wq[:, pl.ds(at, DK)]).astype(BF16).astype(F32)
        at = pl.multiple_of(group * ratio * DV, 128)
        proj = dot(x[HALO:, :], wz[:, pl.ds(at, ratio * DV)]).astype(BF16).astype(F32)
        for r in range(ratio):
            z = proj[:, r * DV : (r + 1) * DV]
            g_out[g * ratio + r] = gain[...] * silu(z)
    for g in range(key_heads):
        weights = conv_weights(cw, true_index(g, key_heads), slice(0, DK))
        q = l2_normed(conv_silu(padded, g, weights, toks)) * DK ** (-0.5)
        qb = q.astype(BF16)
        count = key_heads // 2
        kb = keys_b[g - count] if g >= count else keys_a[g]
        grams = {
            (a, b): dot_t(qb[a * HALF : (a + 1) * HALF], kb[b * HALF : (b + 1) * HALF])
            for a in range(blocks)
            for b in range(a + 1)
        }
        for r in range(ratio):
            j = g * ratio + r
            ccol = cols[:, j : j + 1]
            crow = rows[j : j + 1, :]
            ys, i = (ys_b, j - count * ratio) if g >= count else (ys_a, j)
            for a in range(blocks):
                at = slice(a * HALF, (a + 1) * HALF)
                acc = None
                for b in range(a + 1):
                    m = grams[(a, b)] * block_decay(ccol, crow, a, b)
                    if a == b:
                        m = jnp.where(upto, m, 0.0)
                    term = dot(m.astype(BF16), ys[i, b * HALF : (b + 1) * HALF, :])
                    acc = term if acc is None else acc + term
                q_out[j, at, :] = (q[at] * jnp.exp(ccol[at]) - acc[:, 0:DK]).astype(BF16)
                o_out[j, at, :] = acc[:, DK:]


def join_kernel(own, got, out, *, step):
    upper = placed(step)
    for j in range(own.shape[0]):
        mine, other = own[j], got[j]
        later = jnp.where(upper, mine, other)
        earlier = jnp.where(upper, other, mine)
        if out.shape[-1] == DV:
            out[j] = (dot(later[:, 0:DK], earlier[:, DK:]) + later[:, DK:].astype(F32)).astype(BF16)
        else:
            prod = dot(later[:, 0:DK], earlier)
            out[j, :, 0:DK] = prod[:, 0:DK].astype(BF16)
            out[j, :, DK:] = (prod[:, DK:] + later[:, DK:].astype(F32)).astype(BF16)


def prefix_kernel(before, got, out, *, step):
    upper = placed(step)
    for j in range(before.shape[0]):
        prod = dot(before[j, :, 0:DK], got[j])
        prod_t, prod_b = prod[:, 0:DK], prod[:, DK:] + before[j, :, DK:].astype(F32)
        out[j, :, 0:DK] = jnp.where(upper, prod_t.astype(BF16), before[j, :, 0:DK])
        out[j, :, DK:] = jnp.where(upper, prod_b.astype(BF16), before[j, :, DK:])


def states_kernel(own, pair, before, got, keep, send, *, before_step, step):
    odd = placed(1)
    began = placed(before_step)
    upper = placed(step)
    for j in range(own.shape[0]):
        t, b = before[j, :, 0:DK], before[j, :, DK:].astype(F32)
        if before_step == 2:
            last = got[j].astype(F32)
            entered = jnp.where(began, dot(t, got[j]), last)
            b = jnp.where(began, b, 0.0)
        else:
            entered = dot(t, got[j])
        entered = jnp.where(upper, entered, 0.0) + b
        first = jnp.where(odd, pair[j], own[j])
        passed = dot(first[:, 0:DK], entered.astype(BF16)) + first[:, DK:].astype(F32)
        keep[j] = jnp.where(odd, passed, entered).astype(BF16)
        send[j] = jnp.where(odd, entered, passed).astype(BF16)


def gated_norm(q, o, state, gate):
    att = o + dot(q, state)
    scale = lax.rsqrt(jnp.mean(att * att, axis=-1, keepdims=True) + EPSILON)
    return (att * scale * gate).astype(BF16)


def own_normed_kernel(q, o, own, gate, out):
    half = own.shape[0]
    for j in range(half):
        i = half + j
        out[:, j * DV : (j + 1) * DV] = gated_norm(q[i], o[i], own[j], gate[i])


def normed_kernel(q, o, got, gate, own, keep, send, scratch, *, n_head):
    me = lax.axis_index("head")
    heads = q.shape[0]
    half = heads // 2
    for j in range(heads):
        at = pl.multiple_of(true_index(j, heads) * DV, 128)
        if j < half:
            scratch[:, pl.ds(at, DV)] = gated_norm(q[j], o[j], got[j], gate[j])
        else:
            scratch[:, pl.ds(at, DV)] = own[:, (j - half) * DV : (j - half + 1) * DV]
    part = scratch.shape[0] // n_head
    for i in range(n_head // 2):
        at = pl.multiple_of((me ^ (2 * i)) * part, 16)
        keep[i * part : (i + 1) * part, :] = scratch[pl.ds(at, part), :]
        at = pl.multiple_of((me ^ (2 * i + 1)) * part, 16)
        send[i * part : (i + 1) * part, :] = scratch[pl.ds(at, part), :]


def early_kernel(keep, send, w, out):
    even = lax.axis_index("head") % 2 == 0
    part = keep.shape[0] - out.shape[0]
    out[...] = dot(jnp.where(even, keep[part:, :], send[part:, :]), w[...]).astype(BF16)


def out_own_kernel(own, w, *outs):
    part = outs[0].shape[0]
    for i, out in enumerate(outs):
        out[...] = dot(own[i * part : (i + 1) * part, :], w[...])


def out_kernel(got, w, before, out, *, first):
    part = out.shape[0]
    rows = slice(first * part, (first + 1) * part)
    out[...] = (before[...] + dot(got[rows, :], w[...])).astype(out.dtype)


def total_kernel(*refs):
    even = lax.axis_index("head") % 2 == 0
    count = (len(refs) - 2) // 3
    acc = refs[0][...]
    for i in range(count):
        mine, passed, late = (refs[1 + i + t * count][...].astype(F32) for t in range(3))
        acc = acc + jnp.where(even, mine + passed, late)
    refs[-1][...] = acc.astype(BF16)


def call(body, out_shape, args, us, scratch=(), any_space=(), **static):
    nbytes = sum(a.size * a.dtype.itemsize for a in args)
    vmem = pl.BlockSpec(memory_space=pltpu.VMEM)
    args = [pltpu.with_memory_space_constraint(a, pltpu.HBM) if i in any_space else a for i, a in enumerate(args)]
    return pl.pallas_call(
        functools.partial(body, **static),
        out_shape=out_shape,
        in_specs=[pl.BlockSpec(memory_space=pltpu.HBM) if i in any_space else vmem for i in range(len(args))],
        out_specs=jax.tree.map(lambda _: vmem, out_shape),
        scratch_shapes=list(scratch),
        compiler_params=pltpu.CompilerParams(vmem_limit_bytes=VMEM_BYTES),
        cost_estimate=pl.CostEstimate(flops=int(us * 1.15e9), bytes_accessed=nbytes, transcendentals=0),
    )(*args)


def shaped(shape, dtype):
    return jax.ShapeDtypeStruct(shape, dtype)


def xor_sent(value, axis, step):
    count = lax.axis_size(axis)
    return lax.ppermute(value, axis, [(i, i ^ step) for i in range(count)])


def halo_pairs(n_ctx, n_head, target):
    source = n_head - 1
    pairs = [((c - 1, source), (c, target)) for c in range(1, n_ctx)]
    spare = [h for h in range(n_head) if h not in (source, target)]
    if n_ctx % 4 == 0 and len(spare) == 2:
        a, b = spare
        pairs += [((0, target), (0, a)), ((n_ctx - 1, source), (n_ctx - 1, b)), ((1, a), (1, b)), ((0, b), (2, b))]
        pairs += [((c, a), (c + 1, a)) for c in range(2, n_ctx, 2)]
        pairs += [((c + i, b), (c + i + 2, b)) for c in range(3, n_ctx - 1, 4) for i in range(2)]
    flat = [(c * n_head + h, d * n_head + k) for (c, h), (d, k) in pairs]
    return sorted(flat + [(d, c) for c, d in flat])


def local(layer_in, in_proj, conv_weight, gate_logits, norm_gain, out_proj):
    n_head, n_ctx = lax.axis_size("head"), lax.axis_size("ctx")
    width, key_heads, group = in_proj.shape
    heads = gate_logits.shape[1]
    ratio = heads // key_heads
    part = layer_in.shape[0]
    toks = part * n_head
    ctx_head = ("ctx", "head")

    pieces = [layer_in] + [None] * (n_head - 1)
    step = n_head // 2
    while step:
        for s in range(0, n_head, 2 * step):
            pieces[s + step] = xor_sent(pieces[s], "head", step)
        step //= 2
    blocks = toks // HALF
    packed_shape = shaped(((KERNEL - 1) * (width // 128), 128), BF16)
    tail, x_own, logits = call(
        fetch_kernel,
        (packed_shape, shaped((part, width), BF16), shaped(gate_logits.shape, F32)),
        [layer_in, gate_logits],
        6.0,
        [pltpu.VMEM((HALO, width), BF16), pltpu.VMEM(packed_shape.shape, F32), pltpu.SemaphoreType.DMA((3,))],
        any_space=(0, 1),
    )
    rows, cols, decays = call(
        gates_kernel,
        (
            shaped((heads, toks), F32),
            shaped((toks, 2 * heads), F32),
            shaped((heads, blocks * (blocks + 1) // 2, HALF, HALF), F32),
        ),
        [logits],
        1.0,
    )
    me = lax.axis_index("head")
    halo = jnp.zeros_like(tail)
    for h in range(n_head - 1, 0, -2):
        target = h if h < n_head - 1 else h - 1
        wanted = (me == target) & (lax.axis_index("ctx") > 0)
        halo = jnp.where(wanted, lax.ppermute(tail, ctx_head, halo_pairs(n_ctx, n_head, target)), halo)
    v_end = 2 * DK + ratio * DV
    w_kv = in_proj[:, :, DK:v_end].reshape(width, key_heads * (v_end - DK))
    halo, w_kv = lax.optimization_barrier((halo, w_kv))
    halo_core = xor_sent(halo, "head", 1)
    w_q = in_proj[:, :, 0:DK].reshape(width, key_heads * DK)
    w_z = in_proj[:, :, v_end:].reshape(width, heads * DV)

    half = heads // 2
    pair_shape = shaped((half, DK, DK + DV), BF16)
    state_shape = shaped((half, DK, DV), BF16)
    key_count = key_heads // 2
    ys_shape = shaped((half, toks, DK + DV), BF16)
    keys_shape = shaped((key_count, toks, DK), BF16)
    padded = pltpu.VMEM((key_count * (1 + ratio), HALO + toks, 128), F32)
    s_send, ys_a, keys_a, x_full = call(
        keys_first_kernel,
        (pair_shape, ys_shape, keys_shape, shaped((HALO + toks, width), BF16)),
        [x_own, *pieces[1:], halo, halo_core, w_kv, conv_weight, cols, rows, decays],
        3.0,
        [padded, pltpu.VMEM((HALO, width), F32)],
        n_head=n_head,
        key_heads=key_heads,
        ratio=ratio,
    )
    s_pair = xor_sent(s_send, "ctx", 1)
    s_keep, ys_b, keys_b = call(
        keys_second_kernel,
        (pair_shape, ys_shape, keys_shape),
        [x_full, w_kv, conv_weight, cols, rows, decays],
        3.0,
        [padded],
        key_heads=key_heads,
        ratio=ratio,
    )
    w_other = xor_sent(lax.optimization_barrier((out_proj, s_send))[0], "head", 1)
    total = call(join_kernel, pair_shape, [s_keep, s_pair], 0.2, step=1)
    step, before, before_step = 2, None, 2
    while 2 * step < n_ctx:
        got = xor_sent(total, "ctx", step)
        if step == 2:
            got, w_q, w_z = lax.optimization_barrier((got, w_q, w_z))
        more = 4 * step < n_ctx
        total = call(join_kernel, pair_shape if more else state_shape, [total, got], 0.2, step=step)
        if before is None:
            before = got
        else:
            if before_step == 2:
                entry = jnp.concatenate([jnp.eye(DK, dtype=BF16), jnp.zeros((DK, DV), BF16)], axis=1)
                before = jnp.where(lax.axis_index("ctx") // 2 % 2 == 1, before, entry)
                before_step = 1
            before = call(prefix_kernel, pair_shape, [before, got], 0.2, step=step)
        step *= 2
    got = xor_sent(total, "ctx", step)
    o_shape = shaped((heads, toks, DV), F32)
    q, o, gate = call(
        queries_kernel,
        (shaped((heads, toks, DK), BF16), o_shape, o_shape),
        [x_full, w_q, w_z, conv_weight, cols, rows, keys_a, keys_b, ys_a, ys_b, norm_gain[None, :]],
        1.9,
        [pltpu.VMEM((key_heads, HALO + toks, 128), F32)],
        key_heads=key_heads,
        ratio=ratio,
    )
    got, q, o, gate = lax.optimization_barrier((got, q, o, gate))
    own_state, out_state = call(
        states_kernel,
        (state_shape, state_shape),
        [s_keep, s_pair, before, got],
        0.3,
        before_step=before_step,
        step=step,
    )
    got_state = xor_sent(out_state, "ctx", 1)
    rows_shape = shaped((toks // 2, heads * DV), BF16)
    own_normed = call(own_normed_kernel, shaped((toks, half * DV), BF16), [q, o, own_state, gate], 0.2)
    keep, send = call(
        normed_kernel,
        (rows_shape, rows_shape),
        [q, o, got_state, gate, own_normed],
        0.4,
        [pltpu.VMEM((toks, heads * DV), BF16)],
        n_head=n_head,
    )
    other = xor_sent(send, "head", 1)
    early = call(early_kernel, shaped((toks // 2 - part, width), BF16), [keep, send, out_proj], 0.4)
    early_got = [
        xor_sent(early[(i - 1) * part : i * part], "head", 2 * i) for i in range(1, n_head // 2)
    ]
    out_shape = shaped((part, width), F32)
    sums = call(out_own_kernel, (out_shape,) * (n_head // 2), [keep, out_proj], 0.8)
    late_got = []
    for i in range(1, n_head // 2):
        late = call(out_kernel, shaped((part, width), BF16), [other, w_other, sums[i]], 0.5, first=i)
        late_perm = [
            (c * n_head + h, c * n_head + (h ^ (2 * i)) if h % 2 else (c ^ 1) * n_head + h)
            for c in range(n_ctx)
            for h in range(n_head)
        ]
        late_got.append(lax.ppermute(late, ctx_head, late_perm))
    out = call(out_kernel, out_shape, [other, w_other, sums[0]], 0.5, first=0)
    out, *early_got = lax.optimization_barrier((out, *early_got))
    passed = [xor_sent(mine, "head", 1) for mine in early_got]
    return call(total_kernel, shaped((part, width), BF16), [out, *early_got, *passed, *late_got], 0.5)


def solution(mesh):
    in_specs = (
        P(("ctx", "head"), None),
        P(None, "head", None),
        P(None, "head", None),
        P(None, "head", "ctx"),
        P(),
        P("head", None),
    )
    out_specs = P(("ctx", "head"), None)
    return jax.shard_map(local, mesh=mesh, in_specs=in_specs, out_specs=out_specs, check_vma=False)
```

```python
import functools

import jax
import jax.numpy as jnp
from jax import lax
from jax.experimental import pallas as pl
from jax.experimental.pallas import tpu as pltpu
from jax.sharding import PartitionSpec as P

DK = 128
DV = 128
KERNEL = 4
HALO = 16
HALF = 128
EPSILON = 1e-06
F32 = jnp.float32
BF16 = jnp.bfloat16
VMEM_BYTES = 24 * 1024 * 1024


def dot(a, b):
    return jnp.dot(a, b, preferred_element_type=F32)


def dot_t(a, b):
    return lax.dot_general(a, b, (((1,), (1,)), ((), ())), preferred_element_type=F32)


def silu(x):
    return x / (1.0 + jnp.exp(-x))


def l2_normed(x):
    return x * lax.rsqrt(jnp.sum(x * x, axis=-1, keepdims=True) + EPSILON)


def conv_silu(padded, slot, weights, rows):
    acc = padded[slot, HALO - KERNEL + 1 : HALO - KERNEL + 1 + rows, :] * weights[0]
    for i in range(1, KERNEL):
        lo = HALO - KERNEL + 1 + i
        acc = acc + padded[slot, lo : lo + rows, :] * weights[i]
    return silu(acc)


def block_decay(ccol, crow, a, b):
    gap = ccol[a * HALF : (a + 1) * HALF] - crow[:, b * HALF : (b + 1) * HALF]
    return jnp.exp(jnp.minimum(gap, 0.0))


def placed(step):
    return lax.axis_index("ctx") // step % 2 == 1


def true_index(local, count):
    half = count // 2
    odd = lax.axis_index("ctx") % 2
    return (1 - odd if local < half else odd) * half + local % half


def fetch_kernel(x_any, logits_any, packed, x_own, logits, tail, rows, sems):
    logits_copy = pltpu.make_async_copy(logits_any, logits, sems.at[2])
    tail_copy = pltpu.make_async_copy(x_any.at[pl.ds(x_any.shape[0] - HALO, HALO), :], tail, sems.at[0])
    own_copy = pltpu.make_async_copy(x_any, x_own, sems.at[1])
    tail_copy.start()
    own_copy.start()
    logits_copy.start()
    tail_copy.wait()
    width = tail.shape[1]
    last = tail[...].astype(F32)
    taps = KERNEL - 1
    for r in range(taps):
        for t in range(width // 128):
            at = r * (width // 128) + t
            rows[at : at + 1, :] = last[HALO - taps + r : HALO - taps + r + 1, t * 128 : (t + 1) * 128]
    packed[...] = rows[...].astype(BF16)
    own_copy.wait()
    logits_copy.wait()


def gates_kernel(logits, rows, cols, decays):
    toks = logits.shape[2]
    blocks = toks // HALF
    half = logits.shape[1] // 2
    given = [logits[i] for i in range(2)]
    given = [jnp.where(placed(1), a, jnp.concatenate([a[half:], a[:half]], axis=0)) for a in given]
    x = given[0]
    log_decay = -(jnp.maximum(x, 0.0) + jnp.log1p(jnp.exp(-jnp.abs(x))))
    beta = 1.0 / (1.0 + jnp.exp(-given[1]))
    heads = x.shape[0]
    ri = lax.broadcasted_iota(jnp.int32, (toks, toks), 0)
    ci = lax.broadcasted_iota(jnp.int32, (toks, toks), 1)
    exact = lax.Precision.HIGHEST
    cum = jnp.dot(log_decay, (ri <= ci).astype(F32), precision=exact, preferred_element_type=F32)
    rows[...] = cum
    both = jnp.concatenate([cum, beta], axis=0).T
    cols[...] = both
    ccols, bcols = both[:, 0:heads], both[:, heads:]
    below = ri[:HALF, :HALF] > ci[:HALF, :HALF]
    for j in range(heads):
        i = 0
        for a in range(blocks):
            for b in range(a + 1):
                m = block_decay(ccols[:, j : j + 1], rows[j : j + 1, :], a, b)
                m = m * bcols[a * HALF : (a + 1) * HALF, j : j + 1]
                decays[j, i] = jnp.where(below, m, 0.0) if a == b else m
                i += 1


def conv_weights(weight, g, lanes):
    taps = []
    for i in range(KERNEL):
        tap = weight[i, 0:1, lanes]
        for h in range(1, weight.shape[1]):
            tap = jnp.where(g == h, weight[i, h : h + 1, lanes], tap)
        taps.append(tap)
    return taps


def keys_terms(x, w, cw, cols, rows, decays, s_out, y_out, k_out, padded, *, first, key_heads, ratio):
    toks = x.shape[0] - HALO
    blocks = toks // HALF
    count = key_heads // 2
    heads = key_heads * ratio
    width = DK + ratio * DV
    ri = lax.broadcasted_iota(jnp.int32, (HALF, HALF), 0)
    ci = lax.broadcasted_iota(jnp.int32, (HALF, HALF), 1)
    level = jnp.where(ri > ci, ri ^ ci, 0)
    eye = jnp.where(ri == ci, 1.0, 0.0).astype(F32)
    for g in range(count):
        at = pl.multiple_of(true_index(first + g, key_heads) * width, 128)
        proj = dot(x[...], w[:, pl.ds(at, width)]).astype(BF16).astype(F32)
        for t in range(1 + ratio):
            padded[g * (1 + ratio) + t] = proj[:, t * 128 : (t + 1) * 128]
    kts, rhs, lowers, offs = [], [], [], []
    for g in range(count):
        base = g * (1 + ratio)
        group = true_index(first + g, key_heads)
        k = l2_normed(conv_silu(padded, base, conv_weights(cw, group, slice(DK, 2 * DK)), toks))
        kb = k.astype(BF16)
        k_out[g] = kb
        kf = kb.astype(F32)
        kts.append(kf.T)
        ks = [kb[b * HALF : (b + 1) * HALF] for b in range(blocks)]
        grams = {(a, b): dot_t(ks[a], ks[b]) for a in range(blocks) for b in range(a + 1)}
        for r in range(ratio):
            j = (first + g) * ratio + r
            lanes = slice(2 * DK + r * DV, 2 * DK + (r + 1) * DV)
            v = conv_silu(padded, base + 1 + r, conv_weights(cw, group, lanes), toks)
            ccol = cols[:, j : j + 1]
            bcol = cols[:, heads + j : heads + j + 1]
            rk = (kf * (bcol * jnp.exp(ccol))).astype(BF16)
            rv = (v * bcol).astype(BF16)
            rhs.append(jnp.concatenate([rk, rv], axis=1))
            off, i = {}, 0
            for a in range(blocks):
                for b in range(a + 1):
                    m = grams[(a, b)] * decays[j, i]
                    i += 1
                    if a == b:
                        lowers.append(m)
                    else:
                        off[(a, b)] = m.astype(BF16)
            offs.append(off)
    inv = [eye - jnp.where(level == 1, m, 0.0) for m in lowers]
    inv_b = [m.astype(BF16) for m in inv]
    size = 2
    while size < HALF:
        here = (level >= size) & (level < 4 * size)
        steps = [dot(x, jnp.where(here, m, 0.0).astype(BF16)).astype(BF16) for m, x in zip(lowers, inv_b)]
        squares = [dot(n, n).astype(BF16) for n in steps]
        inv = [x - dot(n, xb) for x, xb, n in zip(inv, inv_b, steps)]
        inv = [x + dot(n, x.astype(BF16)) for x, n in zip(inv, squares)]
        inv_b = [m.astype(BF16) for m in inv]
        size *= 4
    solved = [[] for _ in rhs]
    for a in range(blocks):
        for j, given in enumerate(rhs):
            r = given[a * HALF : (a + 1) * HALF]
            if a:
                acc = r.astype(F32)
                for b in range(a):
                    acc = acc - dot(offs[j][(a, b)], solved[j][b])
                r = acc.astype(BF16)
            solved[j].append(dot(inv_b[j * blocks + a], r).astype(BF16))
    for j in range(len(rhs)):
        y = jnp.concatenate(solved[j], axis=0)
        y_out[j] = y
        at = first * ratio + j
        crow = rows[at : at + 1, :]
        last = crow[:, toks - 1 : toks]
        kd = (kts[j // ratio] * jnp.exp(last - crow)).astype(BF16)
        s = dot(kd, y)
        s_out[j, :, 0:DK] = (eye * jnp.exp(last) - s[:, 0:DK]).astype(BF16)
        s_out[j, :, DK:] = s[:, DK:].astype(BF16)


def keys_first_kernel(*refs, n_head, key_heads, ratio):
    pieces = refs[:n_head]
    halo, halo_core, w, cw, cols, rows, decays, s_out, y_out, k_out, x_out, padded, halo_rows = refs[n_head:]
    me = lax.axis_index("head")
    part = pieces[0].shape[0]
    direct = (me % 2 == 1) != (me >= n_head - 2)
    given = jnp.where(direct, halo[...].astype(F32), halo_core[...].astype(F32))
    taps, tiles = KERNEL - 1, x_out.shape[1] // 128
    halo_rows[...] = jnp.zeros_like(halo_rows)
    for r in range(taps):
        for t in range(tiles):
            at = HALO - taps + r
            halo_rows[at : at + 1, t * 128 : (t + 1) * 128] = given[r * tiles + t : r * tiles + t + 1, :]
    x_out[0:HALO, :] = halo_rows[...].astype(BF16)
    for s in range(n_head):
        at = pl.multiple_of(HALO + (me ^ s) * part, 16)
        x_out[pl.ds(at, part), :] = pieces[s][...]
    keys_terms(
        x_out, w, cw, cols, rows, decays, s_out, y_out, k_out, padded, first=0, key_heads=key_heads, ratio=ratio
    )


def keys_second_kernel(x, w, cw, cols, rows, decays, s_out, y_out, k_out, padded, *, key_heads, ratio):
    keys_terms(
        x, w, cw, cols, rows, decays, s_out, y_out, k_out, padded,
        first=key_heads // 2, key_heads=key_heads, ratio=ratio,
    )


def queries_kernel(
    x, wq, wz, cw, cols, rows, keys_a, keys_b, ys_a, ys_b, gain, q_out, o_out, g_out, padded, *, key_heads, ratio
):
    toks = x.shape[0] - HALO
    blocks = toks // HALF
    ri = lax.broadcasted_iota(jnp.int32, (HALF, HALF), 0)
    ci = lax.broadcasted_iota(jnp.int32, (HALF, HALF), 1)
    upto = ri >= ci
    for g in range(key_heads):
        group = true_index(g, key_heads)
        at = pl.multiple_of(group * DK, 128)
        padded[g] = dot(x[...], wq[:, pl.ds(at, DK)]).astype(BF16).astype(F32)
        at = pl.multiple_of(group * ratio * DV, 128)
        proj = dot(x[HALO:, :], wz[:, pl.ds(at, ratio * DV)]).astype(BF16).astype(F32)
        for r in range(ratio):
            z = proj[:, r * DV : (r + 1) * DV]
            g_out[g * ratio + r] = gain[...] * silu(z)
    for g in range(key_heads):
        weights = conv_weights(cw, true_index(g, key_heads), slice(0, DK))
        q = l2_normed(conv_silu(padded, g, weights, toks)) * DK ** (-0.5)
        qb = q.astype(BF16)
        count = key_heads // 2
        kb = keys_b[g - count] if g >= count else keys_a[g]
        grams = {
            (a, b): dot_t(qb[a * HALF : (a + 1) * HALF], kb[b * HALF : (b + 1) * HALF])
            for a in range(blocks)
            for b in range(a + 1)
        }
        for r in range(ratio):
            j = g * ratio + r
            ccol = cols[:, j : j + 1]
            crow = rows[j : j + 1, :]
            ys, i = (ys_b, j - count * ratio) if g >= count else (ys_a, j)
            for a in range(blocks):
                at = slice(a * HALF, (a + 1) * HALF)
                acc = None
                for b in range(a + 1):
                    m = grams[(a, b)] * block_decay(ccol, crow, a, b)
                    if a == b:
                        m = jnp.where(upto, m, 0.0)
                    term = dot(m.astype(BF16), ys[i, b * HALF : (b + 1) * HALF, :])
                    acc = term if acc is None else acc + term
                q_out[j, at, :] = (q[at] * jnp.exp(ccol[at]) - acc[:, 0:DK]).astype(BF16)
                o_out[j, at, :] = acc[:, DK:]


def join_kernel(own, got, out, *, step):
    upper = placed(step)
    for j in range(own.shape[0]):
        mine, other = own[j], got[j]
        later = jnp.where(upper, mine, other)
        earlier = jnp.where(upper, other, mine)
        if out.shape[-1] == DV:
            out[j] = (dot(later[:, 0:DK], earlier[:, DK:]) + later[:, DK:].astype(F32)).astype(BF16)
        else:
            prod = dot(later[:, 0:DK], earlier)
            out[j, :, 0:DK] = prod[:, 0:DK].astype(BF16)
            out[j, :, DK:] = (prod[:, DK:] + later[:, DK:].astype(F32)).astype(BF16)


def prefix_kernel(before, got, out, *, step):
    upper = placed(step)
    for j in range(before.shape[0]):
        prod = dot(before[j, :, 0:DK], got[j])
        prod_t, prod_b = prod[:, 0:DK], prod[:, DK:] + before[j, :, DK:].astype(F32)
        out[j, :, 0:DK] = jnp.where(upper, prod_t.astype(BF16), before[j, :, 0:DK])
        out[j, :, DK:] = jnp.where(upper, prod_b.astype(BF16), before[j, :, DK:])


def states_kernel(own, pair, before, got, keep, send, *, before_step, step):
    odd = placed(1)
    began = placed(before_step)
    upper = placed(step)
    for j in range(own.shape[0]):
        t, b = before[j, :, 0:DK], before[j, :, DK:].astype(F32)
        if before_step == 2:
            last = got[j].astype(F32)
            entered = jnp.where(began, dot(t, got[j]), last)
            b = jnp.where(began, b, 0.0)
        else:
            entered = dot(t, got[j])
        entered = jnp.where(upper, entered, 0.0) + b
        first = jnp.where(odd, pair[j], own[j])
        passed = dot(first[:, 0:DK], entered.astype(BF16)) + first[:, DK:].astype(F32)
        keep[j] = jnp.where(odd, passed, entered).astype(BF16)
        send[j] = jnp.where(odd, entered, passed).astype(BF16)


def gated_norm(q, o, state, gate):
    att = o + dot(q, state)
    scale = lax.rsqrt(jnp.mean(att * att, axis=-1, keepdims=True) + EPSILON)
    return (att * scale * gate).astype(BF16)


def own_normed_kernel(q, o, own, gate, out):
    half = own.shape[0]
    for j in range(half):
        i = half + j
        out[:, j * DV : (j + 1) * DV] = gated_norm(q[i], o[i], own[j], gate[i])


def normed_kernel(q, o, got, gate, own, keep, send, scratch, *, n_head):
    me = lax.axis_index("head")
    heads = q.shape[0]
    half = heads // 2
    for j in range(heads):
        at = pl.multiple_of(true_index(j, heads) * DV, 128)
        if j < half:
            scratch[:, pl.ds(at, DV)] = gated_norm(q[j], o[j], got[j], gate[j])
        else:
            scratch[:, pl.ds(at, DV)] = own[:, (j - half) * DV : (j - half + 1) * DV]
    part = scratch.shape[0] // n_head
    for i in range(n_head // 2):
        at = pl.multiple_of((me ^ (2 * i)) * part, 16)
        keep[i * part : (i + 1) * part, :] = scratch[pl.ds(at, part), :]
        at = pl.multiple_of((me ^ (2 * i + 1)) * part, 16)
        send[i * part : (i + 1) * part, :] = scratch[pl.ds(at, part), :]


def early_kernel(keep, send, w, out):
    even = lax.axis_index("head") % 2 == 0
    part = keep.shape[0] - out.shape[0]
    out[...] = dot(jnp.where(even, keep[part:, :], send[part:, :]), w[...]).astype(BF16)


def out_own_kernel(own, w, *outs):
    part = outs[0].shape[0]
    for i, out in enumerate(outs):
        out[...] = dot(own[i * part : (i + 1) * part, :], w[...])


def out_kernel(got, w, before, out, *, first):
    part = out.shape[0]
    rows = slice(first * part, (first + 1) * part)
    out[...] = (before[...] + dot(got[rows, :], w[...])).astype(out.dtype)


def total_kernel(*refs):
    even = lax.axis_index("head") % 2 == 0
    count = (len(refs) - 2) // 3
    acc = refs[0][...]
    for i in range(count):
        mine, passed, late = (refs[1 + i + t * count][...].astype(F32) for t in range(3))
        acc = acc + jnp.where(even, mine + passed, late)
    refs[-1][...] = acc.astype(BF16)


def call(body, out_shape, args, us, scratch=(), any_space=(), **static):
    nbytes = sum(a.size * a.dtype.itemsize for a in args)
    vmem = pl.BlockSpec(memory_space=pltpu.VMEM)
    args = [pltpu.with_memory_space_constraint(a, pltpu.HBM) if i in any_space else a for i, a in enumerate(args)]
    return pl.pallas_call(
        functools.partial(body, **static),
        out_shape=out_shape,
        in_specs=[pl.BlockSpec(memory_space=pltpu.HBM) if i in any_space else vmem for i in range(len(args))],
        out_specs=jax.tree.map(lambda _: vmem, out_shape),
        scratch_shapes=list(scratch),
        compiler_params=pltpu.CompilerParams(vmem_limit_bytes=VMEM_BYTES),
        cost_estimate=pl.CostEstimate(flops=int(us * 1.15e9), bytes_accessed=nbytes, transcendentals=0),
    )(*args)


def shaped(shape, dtype):
    return jax.ShapeDtypeStruct(shape, dtype)


def xor_sent(value, axis, step):
    count = lax.axis_size(axis)
    return lax.ppermute(value, axis, [(i, i ^ step) for i in range(count)])


def halo_pairs(n_ctx, n_head, target):
    source = n_head - 1
    pairs = [((c - 1, source), (c, target)) for c in range(1, n_ctx)]
    spare = [h for h in range(n_head) if h not in (source, target)]
    if n_ctx % 4 == 0 and len(spare) == 2:
        a, b = spare
        pairs += [((0, target), (0, a)), ((n_ctx - 1, source), (n_ctx - 1, b)), ((1, a), (1, b)), ((0, b), (2, b))]
        pairs += [((c, a), (c + 1, a)) for c in range(2, n_ctx, 2)]
        pairs += [((c + i, b), (c + i + 2, b)) for c in range(3, n_ctx - 1, 4) for i in range(2)]
    flat = [(c * n_head + h, d * n_head + k) for (c, h), (d, k) in pairs]
    return sorted(flat + [(d, c) for c, d in flat])


def local(layer_in, in_proj, conv_weight, gate_logits, norm_gain, out_proj):
    n_head, n_ctx = lax.axis_size("head"), lax.axis_size("ctx")
    width, key_heads, group = in_proj.shape
    heads = gate_logits.shape[1]
    ratio = heads // key_heads
    part = layer_in.shape[0]
    toks = part * n_head
    ctx_head = ("ctx", "head")

    pieces = [layer_in] + [None] * (n_head - 1)
    step = n_head // 2
    while step:
        for s in range(0, n_head, 2 * step):
            pieces[s + step] = xor_sent(pieces[s], "head", step)
        step //= 2
    blocks = toks // HALF
    packed_shape = shaped(((KERNEL - 1) * (width // 128), 128), BF16)
    tail, x_own, logits = call(
        fetch_kernel,
        (packed_shape, shaped((part, width), BF16), shaped(gate_logits.shape, F32)),
        [layer_in, gate_logits],
        6.0,
        [pltpu.VMEM((HALO, width), BF16), pltpu.VMEM(packed_shape.shape, F32), pltpu.SemaphoreType.DMA((3,))],
        any_space=(0, 1),
    )
    rows, cols, decays = call(
        gates_kernel,
        (
            shaped((heads, toks), F32),
            shaped((toks, 2 * heads), F32),
            shaped((heads, blocks * (blocks + 1) // 2, HALF, HALF), F32),
        ),
        [logits],
        1.0,
    )
    me = lax.axis_index("head")
    halo = jnp.zeros_like(tail)
    for h in range(n_head - 1, 0, -2):
        target = h if h < n_head - 1 else h - 1
        wanted = (me == target) & (lax.axis_index("ctx") > 0)
        halo = jnp.where(wanted, lax.ppermute(tail, ctx_head, halo_pairs(n_ctx, n_head, target)), halo)
    v_end = 2 * DK + ratio * DV
    w_kv = in_proj[:, :, DK:v_end].reshape(width, key_heads * (v_end - DK))
    halo, w_kv = lax.optimization_barrier((halo, w_kv))
    halo_core = xor_sent(halo, "head", 1)
    w_q = in_proj[:, :, 0:DK].reshape(width, key_heads * DK)
    w_z = in_proj[:, :, v_end:].reshape(width, heads * DV)

    half = heads // 2
    pair_shape = shaped((half, DK, DK + DV), BF16)
    state_shape = shaped((half, DK, DV), BF16)
    key_count = key_heads // 2
    ys_shape = shaped((half, toks, DK + DV), BF16)
    keys_shape = shaped((key_count, toks, DK), BF16)
    padded = pltpu.VMEM((key_count * (1 + ratio), HALO + toks, 128), F32)
    s_send, ys_a, keys_a, x_full = call(
        keys_first_kernel,
        (pair_shape, ys_shape, keys_shape, shaped((HALO + toks, width), BF16)),
        [x_own, *pieces[1:], halo, halo_core, w_kv, conv_weight, cols, rows, decays],
        3.0,
        [padded, pltpu.VMEM((HALO, width), F32)],
        n_head=n_head,
        key_heads=key_heads,
        ratio=ratio,
    )
    s_pair = xor_sent(s_send, "ctx", 1)
    s_keep, ys_b, keys_b = call(
        keys_second_kernel,
        (pair_shape, ys_shape, keys_shape),
        [x_full, w_kv, conv_weight, cols, rows, decays],
        3.0,
        [padded],
        key_heads=key_heads,
        ratio=ratio,
    )
    w_other = xor_sent(lax.optimization_barrier((out_proj, s_send))[0], "head", 1)
    total = call(join_kernel, pair_shape, [s_keep, s_pair], 0.2, step=1)
    step, before, before_step = 2, None, 2
    while 2 * step < n_ctx:
        got = xor_sent(total, "ctx", step)
        if step == 2:
            got, w_q, w_z = lax.optimization_barrier((got, w_q, w_z))
        more = 4 * step < n_ctx
        total = call(join_kernel, pair_shape if more else state_shape, [total, got], 0.2, step=step)
        if before is None:
            before = got
        else:
            if before_step == 2:
                entry = jnp.concatenate([jnp.eye(DK, dtype=BF16), jnp.zeros((DK, DV), BF16)], axis=1)
                before = jnp.where(lax.axis_index("ctx") // 2 % 2 == 1, before, entry)
                before_step = 1
            before = call(prefix_kernel, pair_shape, [before, got], 0.2, step=step)
        step *= 2
    got = xor_sent(total, "ctx", step)
    o_shape = shaped((heads, toks, DV), F32)
    q, o, gate = call(
        queries_kernel,
        (shaped((heads, toks, DK), BF16), o_shape, o_shape),
        [x_full, w_q, w_z, conv_weight, cols, rows, keys_a, keys_b, ys_a, ys_b, norm_gain[None, :]],
        1.9,
        [pltpu.VMEM((key_heads, HALO + toks, 128), F32)],
        key_heads=key_heads,
        ratio=ratio,
    )
    got, q, o, gate = lax.optimization_barrier((got, q, o, gate))
    own_state, out_state = call(
        states_kernel,
        (state_shape, state_shape),
        [s_keep, s_pair, before, got],
        0.3,
        before_step=before_step,
        step=step,
    )
    got_state = xor_sent(out_state, "ctx", 1)
    rows_shape = shaped((toks // 2, heads * DV), BF16)
    own_normed = call(own_normed_kernel, shaped((toks, half * DV), BF16), [q, o, own_state, gate], 0.2)
    keep, send = call(
        normed_kernel,
        (rows_shape, rows_shape),
        [q, o, got_state, gate, own_normed],
        0.4,
        [pltpu.VMEM((toks, heads * DV), BF16)],
        n_head=n_head,
    )
    other = xor_sent(send, "head", 1)
    early = call(early_kernel, shaped((toks // 2 - part, width), BF16), [keep, send, out_proj], 0.4)
    early_got = [
        xor_sent(early[(i - 1) * part : i * part], "head", 2 * i) for i in range(1, n_head // 2)
    ]
    out_shape = shaped((part, width), F32)
    sums = call(out_own_kernel, (out_shape,) * (n_head // 2), [keep, out_proj], 0.8)
    late_got = []
    for i in range(1, n_head // 2):
        late = call(out_kernel, shaped((part, width), BF16), [other, w_other, sums[i]], 0.5, first=i)
        late_perm = [
            (c * n_head + h, c * n_head + (h ^ (2 * i)) if h % 2 else (c ^ 2) * n_head + h)
            for c in range(n_ctx)
            for h in range(n_head)
        ]
        late_got.append(lax.ppermute(late, ctx_head, late_perm))
    out = call(out_kernel, out_shape, [other, w_other, sums[0]], 0.5, first=0)
    out, *early_got = lax.optimization_barrier((out, *early_got))
    passed = [xor_sent(mine, "head", 1) for mine in early_got]
    return call(total_kernel, shaped((part, width), BF16), [out, *early_got, *passed, *late_got], 0.5)


def solution(mesh):
    in_specs = (
        P(("ctx", "head"), None),
        P(None, "head", None),
        P(None, "head", None),
        P(None, "head", "ctx"),
        P(),
        P("head", None),
    )
    out_specs = P(("ctx", "head"), None)
    return jax.shard_map(local, mesh=mesh, in_specs=in_specs, out_specs=out_specs, check_vma=False)
```
